256 devices in a mesh: shard: 16 (over z_hi, x), dp: 16 (over y, z_lo, core).
Axes of the slice: x: 4, y: 4, z: 8 (z_hi: 4, z_lo: 2; z = z_hi * 2 + z_lo), core: 2. Of those that a mesh axis runs over, the one named last changes fastest.
Arguments:
- tokens: bfloat16 [4096, 2304], P('dp'), may hold values from -6 to 6
- target: bfloat16 [4096, 2304], P('dp'), may hold values from -6 to 6
- segments: int32 [4096], P('dp'), may hold values from 0 to 1023, never falling along the last dimension, each value on 1 to 8 neighbouring positions
- gate_weight: bfloat16 [2304, 18432], P('dp', 'shard'), may hold values from -0.125 to 0.125
- up_weight: bfloat16 [2304, 18432], P('dp', 'shard'), may hold values from -0.125 to 0.125
- down_weight: bfloat16 [2304, 18432], P('dp', 'shard'), may hold values from -0.046875 to 0.046875
- vector: bfloat16 [2304, 18432], P('dp', 'shard'), may hold values from -6 to 6
- gradient: bfloat16 [2304, 18432], P('dp', 'shard'), may hold values from -6 to 6
Outputs:
- new_vector: bfloat16 [2304, 18432], P('dp', 'shard')
The draws below stay inside these ranges and needn't reach their ends.
Inputs may be any that keep to these rules, and one draw needn't show every extreme that they name: `segments`: segment numbers never fall along the whole batch; each segment holds 1 to 8 tokens and one holds exactly 8.
All inputs are finite; a program needn't handle non-finite values.
Results may differ from the reference program's by a relative error of at most 0.03.
Values may be sent and summed in bfloat16 or wider, within the bound.
A program may use at most 64 MiB of HBM per device.

```python
import math
import jax
import jax.numpy as jnp
import numpy as np
from jax import lax

D = 2304
FF = 18432
TOK_DEV = 256
SEG_MOST = 8
TOKENS = 4096
SEGMENTS = 1024
N_DP = 16


def raised(values, key, source, target, shards_of, factor):
    def block_of(dim):
        return (jnp.arange(values.shape[dim]) // (values.shape[dim] // shards_of)).reshape((-1,) + (1,) * (values.ndim - 1 - dim))

    near = jax.random.permutation(key, shards_of)[block_of(target)]
    second = (block_of(target) + shards_of // 2) % shards_of
    return jnp.where((block_of(source) == near) | (block_of(source) == second), factor * values, values)


def block_scale(rng, dims, split, least, high):
    def one(dim, shards_of):
        steps = jax.random.uniform(jax.random.fold_in(jax.random.fold_in(rng, 6), dim), (shards_of,), jnp.float32, least / len(split), high / len(split))
        return jnp.repeat(jnp.exp(steps), dims[dim] // shards_of).reshape((-1,) + (1,) * (len(dims) - dim - 1))

    gain = one(*split[0])
    for cut in split[1:]:
        gain = gain * one(*cut)
    return gain


def profile(number_of, total, reach, skew):
    weights = [(1 << 20) // math.isqrt(grade ** skew) + 1 for grade in range(2, number_of + 1)]
    surplus, given = total - reach - (number_of - 1), [1] * (number_of - 1)
    while surplus > 0:
        movable = [i for i in range(number_of - 1) if given[i] < reach]
        pool, remaining = sum([weights[i] for i in movable]), surplus
        for i in movable:
            extra = min(reach - given[i], max(1, remaining * weights[i] // pool), surplus)
            given[i] = given[i] + extra
            surplus = surplus - extra
    return np.array([reach] + given)


def uneven(key, count, total, reach, slope):
    if count == 2:
        one = jax.random.randint(key, (), max(1, total - reach), min(reach, total - 1) + 1)
        return jnp.stack([one, total - one])
    tallies = jnp.asarray(profile(count, total, reach, slope), jnp.int32)
    couples = (count - 1) // 2
    source_of, sink = tallies[1:1 + 2 * couples:2], tallies[2:2 + 2 * couples:2]
    slack = jnp.minimum(source_of - 1, reach - sink)
    passed = jax.random.randint(jax.random.fold_in(key, 1), (couples,), 0, 1 << 20) % (slack + 1)
    tallies = tallies.at[1:1 + 2 * couples:2].set(source_of - passed).at[2:2 + 2 * couples:2].set(sink + passed)
    return tallies[jax.random.permutation(jax.random.fold_in(key, 2), count)]


def bell_draw(key, dims, width, most, shards=(), held_as=jnp.bfloat16):
    loudness = block_scale(key, dims, shards, -0.22, 0.18) if shards else 1.0
    entries = jax.random.normal(key, dims, jnp.float32) * width * loudness
    return jnp.minimum(jnp.maximum(entries, -most), most).astype(held_as)


def gaussian_with(own_key, extent, deviation, bound, cuts, heavy, kind=jnp.bfloat16):
    array = deviation * jax.random.normal(own_key, extent, jnp.float32)
    if cuts:
        array = array * block_scale(own_key, extent, cuts, -0.22, 0.18)
    return jnp.clip(raised(array, jax.random.fold_in(own_key, 3), *heavy), -bound, bound).astype(kind)


def setup_inputs(seed: int = 0) -> dict:
    key_of = jax.random.split(jax.random.key(seed), 9)
    return {
        "tokens": gaussian_with(key_of[0], (TOKENS, D), 1.0, 6.0, ((0, 16),), (0, 1, 16, 2.0)),
        "target": bell_draw(key_of[1], (TOKENS, D), 1.0, 6.0, ((0, 16),)),
        "segments": jnp.searchsorted(jnp.cumsum(uneven(key_of[2], SEGMENTS, TOKENS, SEG_MOST, 0)), jnp.arange(TOKENS), side="right").astype(jnp.int32),
        "gate_weight": bell_draw(key_of[3], (D, FF), D ** -0.5, 0.125, ((0, 16), (1, 16))),
        "up_weight": bell_draw(key_of[4], (D, FF), D ** -0.5, 0.125, ((0, 16), (1, 16))),
        "down_weight": bell_draw(key_of[5], (D, FF), FF ** -0.5, 0.046875, ((0, 16), (1, 16))),
        "vector": bell_draw(key_of[6], (D, FF), 1.0, 6.0, ((0, 16), (1, 16))),
        "gradient": bell_draw(key_of[7], (D, FF), 1.0, 6.0, ((0, 16), (1, 16))),
    }


coeff_k = 0.7978845608028654
coeff_c = 0.044715
damping = 0.01
step_size = 0.8


def gelu_parts(pre_act):
    inner_arg = coeff_k * (pre_act + coeff_c * pre_act * pre_act * pre_act)
    tanh_value = jnp.tanh(inner_arg)
    slope_term = coeff_k * (1.0 + 3.0 * coeff_c * pre_act * pre_act)
    curve_term = 6.0 * coeff_k * coeff_c * pre_act
    sech_square = 1.0 - tanh_value * tanh_value
    gelu_value = 0.5 * pre_act * (1.0 + tanh_value)
    gelu_slope = 0.5 * (1.0 + tanh_value) + 0.5 * pre_act * sech_square * slope_term
    gelu_curve = sech_square * (slope_term + 0.5 * pre_act * (curve_term - 2.0 * tanh_value * slope_term * slope_term))
    return gelu_value, gelu_slope, gelu_curve


def reference(tokens, target, segments, gate_weight, up_weight, down_weight, vector, gradient):
    inv_root = float(D) ** -0.5
    pre_gate = jnp.dot(tokens, gate_weight, preferred_element_type=jnp.float32)
    up_act = jnp.dot(tokens, up_weight, preferred_element_type=jnp.float32)
    tangent_gate = jnp.dot(tokens, vector, preferred_element_type=jnp.float32) * inv_root
    gelu_value, gelu_slope, gelu_curve = gelu_parts(pre_gate)
    hidden = (gelu_value * up_act).astype(jnp.bfloat16)
    tangent_hidden = (gelu_slope * tangent_gate * up_act).astype(jnp.bfloat16)
    output = jnp.dot(hidden, down_weight.T, preferred_element_type=jnp.float32)
    out_tangent = jnp.dot(tangent_hidden, down_weight.T, preferred_element_type=jnp.float32)
    same_segment = jnp.concatenate([jnp.zeros((1,), dtype=bool), segments[1:] == segments[:-1]])
    keep_mask = same_segment.astype(jnp.float32)[:, None]
    grad_out = (keep_mask * (output - target.astype(jnp.float32))).astype(jnp.bfloat16)
    tangent_grad = (keep_mask * out_tangent).astype(jnp.bfloat16)
    grad_hidden = jnp.dot(grad_out, down_weight, preferred_element_type=jnp.float32)
    tangent_grad_hidden = jnp.dot(tangent_grad, down_weight, preferred_element_type=jnp.float32)
    tangent_grad_gate = (up_act * (tangent_grad_hidden * gelu_slope + grad_hidden * gelu_curve * tangent_gate)).astype(jnp.bfloat16)
    tok_groups = tokens.reshape(N_DP, TOK_DEV, D)
    grad_groups = tangent_grad_gate.reshape(N_DP, TOK_DEV, FF)

    def add_group(running, group_pair):
        group_term = jnp.dot(group_pair[0].T, group_pair[1], preferred_element_type=jnp.float32) * inv_root
        rounded = lax.optimization_barrier(group_term.astype(jnp.bfloat16))
        return running + rounded.astype(jnp.float32), None

    zero_total = jnp.zeros((D, FF), jnp.float32)
    curvature, _ = lax.scan(add_group, zero_total, (tok_groups, grad_groups))
    updated = gradient.astype(jnp.float32) + (1.0 - damping) * vector.astype(jnp.float32) - step_size * curvature
    return updated.astype(jnp.bfloat16)
```

```python
import functools

import jax
import jax.numpy as jnp
from jax import lax
from jax.experimental import pallas as pl
from jax.experimental.pallas import tpu as pltpu
from jax.sharding import PartitionSpec as P

MESH = pl.DeviceIdType.MESH
coeff_k = 0.7978845608028654
coeff_c = 0.044715
damping = 0.01
step_size = 0.8


def gelu_parts(pre_act):
    inner_arg = coeff_k * (pre_act + coeff_c * pre_act * pre_act * pre_act)
    tanh_value = jnp.tanh(inner_arg)
    slope_term = coeff_k * (1.0 + 3.0 * coeff_c * pre_act * pre_act)
    curve_term = 6.0 * coeff_k * coeff_c * pre_act
    sech_square = 1.0 - tanh_value * tanh_value
    gelu_value = 0.5 * pre_act * (1.0 + tanh_value)
    gelu_slope = 0.5 * (1.0 + tanh_value) + 0.5 * pre_act * sech_square * slope_term
    gelu_curve = sech_square * (
        slope_term + 0.5 * pre_act * (curve_term - 2.0 * tanh_value * slope_term * slope_term)
    )
    return (gelu_value, gelu_slope, gelu_curve)


def remote(src, dst, send_sem, recv_sem, axis, index):
    return pltpu.make_async_remote_copy(
        src_ref=src,
        dst_ref=dst,
        send_sem=send_sem,
        recv_sem=recv_sem,
        device_id={axis: index},
        device_id_type=MESH,
    )


def greet(axis, neighbours):
    barrier = pltpu.get_barrier_semaphore()
    for neighbour in neighbours:
        pl.semaphore_signal(barrier, inc=1, device_id={axis: neighbour}, device_id_type=MESH)
    pl.semaphore_wait(barrier, len(neighbours))


def dp_place():
    me = lax.axis_index("dp")
    y, zl, core = me // 4, (me // 2) % 2, me % 2

    def at(dy, dz, dc):
        return ((y + dy) % 4) * 4 + ((zl + dz) % 2) * 2 + (core + dc) % 2

    return at


GATHER_COPIES = 17


def gather_kernel(count, depth, cut, *refs):
    ins, outs = refs[:count], refs[count : 2 * count]
    send_sem, recv_sem, own_sem = refs[2 * count :]
    at = dp_place()
    sib, up, down, zed = at(0, 0, 1), at(1, 0, 0), at(-1, 0, 0), at(0, 1, 0)
    greet("dp", (sib, up, down, zed))

    def rows(w, owner, part):
        lo, size = {"w": (0, depth), "a": (0, cut), "b": (cut, depth - cut)}[part]
        return outs[w].at[pl.ds(pl.multiple_of(owner * depth + lo, 16), size)]

    me = at(0, 0, 0)
    table = [
        (me, "w", sib, at(0, 0, 1)),
        (me, "w", up, at(-1, 0, 0)),
        (me, "w", down, at(1, 0, 0)),
        (me, "w", zed, at(0, 1, 0)),
        (at(0, 1, 0), "w", up, at(-1, 1, 0)),
        (at(0, 1, 0), "w", down, at(1, 1, 0)),
        (at(0, 1, 0), "w", sib, at(0, 1, 1)),
        (at(-1, 0, 0), "a", up, at(2, 0, 0)),
        (at(1, 0, 0), "b", down, at(2, 0, 0)),
        (at(-1, 0, 0), "w", sib, at(-1, 0, 1)),
        (at(1, 0, 0), "w", sib, at(1, 0, 1)),
        (at(-1, 1, 0), "w", sib, at(-1, 1, 1)),
        (at(1, 1, 0), "w", sib, at(1, 1, 1)),
        (at(2, 0, 0), "a", zed, at(2, 1, 0)),
        (at(2, 0, 0), "b", zed, at(2, 1, 0)),
        (at(2, 0, 0), "w", sib, at(2, 0, 1)),
        (at(2, 1, 0), "w", sib, at(2, 1, 1)),
    ]
    sent = []

    def start(w, *numbers):
        for k in numbers:
            owner, part, target, _ = table[k]
            src = ins[w] if k < 4 else rows(w, owner, part)
            copy = remote(src, rows(w, owner, part), send_sem.at[w, k], recv_sem.at[w, k], "dp", target)
            copy.start()
            sent.append(copy)

    def wait(w, *numbers):
        for k in numbers:
            _, part, target, owner = table[k]
            ref = rows(w, owner, part)
            remote(ref, ref, send_sem.at[w, k], recv_sem.at[w, k], "dp", target).wait_recv()

    own = []
    for s in range(-1, count + 3):
        if s + 1 < count:
            start(s + 1, 1, 2, 3, 0)
            copy = pltpu.make_async_copy(ins[s + 1], rows(s + 1, me, "w"), own_sem.at[s + 1])
            copy.start()
            own.append(copy)
        w = s - 0
        if 0 <= w < count:
            wait(w, 3)
            start(w, 4, 5, 6)
            wait(w, 1)
            start(w, 7, 9)
            wait(w, 2)
            start(w, 8, 10)
        w = s - 1
        if 0 <= w < count:
            wait(w, 7)
            start(w, 13)
            wait(w, 8)
            start(w, 14, 15)
            wait(w, 4)
            start(w, 11)
            wait(w, 5)
            start(w, 12)
        w = s - 2
        if 0 <= w < count:
            wait(w, 13, 14)
            start(w, 16)
    for w in range(count):
        wait(w, 0, 6, 9, 10, 11, 12, 15, 16)
    for copy in own:
        copy.wait()
    for copy in sent:
        copy.wait_send()


def gather(arrays, ident):
    count, (depth, width) = len(arrays), arrays[0].shape
    cut = (depth // 32 + 1) * 16 if depth % 32 else depth // 2
    return pl.pallas_call(
        functools.partial(gather_kernel, count, depth, cut),
        out_shape=[jax.ShapeDtypeStruct((16 * depth, width), a.dtype) for a in arrays],
        in_specs=[pl.BlockSpec(memory_space=pl.ANY)] * count,
        out_specs=[pl.BlockSpec(memory_space=pl.ANY)] * count,
        scratch_shapes=[
            pltpu.SemaphoreType.DMA((count, GATHER_COPIES)),
            pltpu.SemaphoreType.DMA((count, GATHER_COPIES)),
            pltpu.SemaphoreType.DMA((count,)),
        ],
        compiler_params=pltpu.CompilerParams(collective_id=ident, has_side_effects=True),
    )(*arrays)


def plus(a, *more):
    total = a.astype(jnp.float32)
    for b in more:
        total = total + b.astype(jnp.float32)
    return total


PIECES = 3


def sum_kernel(rows, width, p_ref, o_ref, xin, xtx, xc, zin, ztx, sx, rx, sz, rz, s4, r4):
    me = lax.axis_index("shard")
    x, zh = me % 4, me // 4
    right, left = zh * 4 + (x + 1) % 4, zh * 4 + (x + 3) % 4
    above, below = ((zh + 1) % 4) * 4 + x, ((zh + 3) % 4) * 4 + x
    greet("shard", (right, left, above, below))
    quarter, piece = rows // 4, width // PIECES
    sub = quarter // 4
    sent = []

    def go(src, dst, s, r, target):
        copy = remote(src, dst, s, r, "shard", target)
        copy.start()
        sent.append(copy)

    def got(ref, s, r):
        remote(ref, ref, s, r, "shard", right).wait_recv()

    def cols(q):
        return pl.ds(q * piece, piece)

    def ring1(q, src, size, base, k, inbox, s, r, plus1, minus1):
        half = size // 2

        def part(chunk, h):
            return src(q).at[pl.ds(pl.multiple_of(base + ((k + chunk) % 4) * size + h * half, 16), half)]

        go(part(2, 1), inbox.at[q, 0], s.at[q, 0], r.at[q, 0], plus1)
        go(part(2, 0), inbox.at[q, 1], s.at[q, 1], r.at[q, 1], minus1)
        go(part(1, 0), inbox.at[q, 2], s.at[q, 2], r.at[q, 2], plus1)
        go(part(3, 1), inbox.at[q, 5], s.at[q, 5], r.at[q, 5], minus1)

    def ring2(q, src, size, base, k, inbox, out, s, r, plus1, minus1):
        half = size // 2

        def part(chunk, h):
            return src(q)[pl.ds(pl.multiple_of(base + ((k + chunk) % 4) * size + h * half, 16), half)]

        got(inbox.at[q, 0], s.at[q, 0], r.at[q, 0])
        out[q, 0] = plus(part(1, 1), inbox[q, 0]).astype(jnp.bfloat16)
        go(out.at[q, 0], inbox.at[q, 3], s.at[q, 3], r.at[q, 3], plus1)
        got(inbox.at[q, 1], s.at[q, 1], r.at[q, 1])
        out[q, 1] = plus(part(3, 0), inbox[q, 1]).astype(jnp.bfloat16)
        go(out.at[q, 1], inbox.at[q, 4], s.at[q, 4], r.at[q, 4], minus1)

    def ring3(q, src, size, base, k, inbox, s, r):
        half = size // 2
        for i in (2, 5, 3, 4):
            got(inbox.at[q, i], s.at[q, i], r.at[q, i])
        sums = []
        for h in range(2):
            mine = src(q)[pl.ds(pl.multiple_of(base + k * size + h * half, 16), half)]
            sums.append(plus(mine, inbox[q, 2 + h], inbox[q, 4 + h]))
        return sums

    def whole(q):
        return p_ref.at[:, cols(q)]

    def mine(q):
        return xc.at[q]

    def out_rows(start, size, q):
        return o_ref.at[pl.ds(pl.multiple_of(start, 16), size), cols(q)]

    def step(i, q):
        half, shalf = quarter // 2, sub // 2
        if i == 0:
            ring1(q, whole, quarter, 0, x, xin, sx, rx, right, left)
        if i == 1:
            ring2(q, whole, quarter, 0, x, xin, xtx, sx, rx, right, left)
        if i == 2:
            sums = ring3(q, whole, quarter, 0, x, xin, sx, rx)
            for h in range(2):
                xc[q, h * half : (h + 1) * half] = sums[h].astype(jnp.bfloat16)
            ring1(q, mine, sub, 0, zh, zin, sz, rz, above, below)
        if i == 3:
            ring2(q, mine, sub, 0, zh, zin, ztx, sz, rz, above, below)
        base = x * quarter
        if i == 4:
            sums = ring3(q, mine, sub, 0, zh, zin, sz, rz)
            for h in range(2):
                out_rows(base + zh * sub + h * shalf, shalf, q)[...] = sums[h].astype(jnp.bfloat16)
            ref = out_rows(base + zh * sub, sub, q)
            go(ref, ref, s4.at[q, 0], r4.at[q, 0], above)
            go(ref, ref, s4.at[q, 1], r4.at[q, 1], below)
        if i == 5:
            lo, hi = base + ((zh + 3) % 4) * sub, base + ((zh + 1) % 4) * sub
            got(out_rows(lo, sub, q), s4.at[q, 0], r4.at[q, 0])
            ref = out_rows(lo, shalf, q)
            go(ref, ref, s4.at[q, 2], r4.at[q, 2], above)
            got(out_rows(hi, sub, q), s4.at[q, 1], r4.at[q, 1])
            ref = out_rows(hi + shalf, shalf, q)
            go(ref, ref, s4.at[q, 3], r4.at[q, 3], below)
        if i == 6:
            far = base + ((zh + 2) % 4) * sub
            got(out_rows(far, shalf, q), s4.at[q, 2], r4.at[q, 2])
            got(out_rows(far + shalf, shalf, q), s4.at[q, 3], r4.at[q, 3])
            ref = out_rows(base, quarter, q)
            go(ref, ref, s4.at[q, 4], r4.at[q, 4], right)
            go(ref, ref, s4.at[q, 5], r4.at[q, 5], left)
        if i == 7:
            lo, hi = ((x + 3) % 4) * quarter, ((x + 1) % 4) * quarter
            got(out_rows(lo, quarter, q), s4.at[q, 4], r4.at[q, 4])
            ref = out_rows(lo, half, q)
            go(ref, ref, s4.at[q, 6], r4.at[q, 6], right)
            got(out_rows(hi, quarter, q), s4.at[q, 5], r4.at[q, 5])
            ref = out_rows(hi + half, half, q)
            go(ref, ref, s4.at[q, 7], r4.at[q, 7], left)
        if i == 8:
            far = ((x + 2) % 4) * quarter
            got(out_rows(far, half, q), s4.at[q, 6], r4.at[q, 6])
            got(out_rows(far + half, half, q), s4.at[q, 7], r4.at[q, 7])

    for t in range(9 + PIECES - 1):
        for q in range(PIECES):
            if 0 <= t - q < 9:
                step(t - q, q)
    for copy in sent:
        copy.wait_send()


def sum_over_shard(partial, ident):
    rows, width = partial.shape
    piece = width // PIECES
    quarter = rows // 4
    sub = quarter // 4
    bf = jnp.bfloat16
    return pl.pallas_call(
        functools.partial(sum_kernel, rows, width),
        out_shape=jax.ShapeDtypeStruct((rows, width), bf),
        in_specs=[pl.BlockSpec(memory_space=pltpu.VMEM)],
        out_specs=pl.BlockSpec(memory_space=pltpu.VMEM),
        scratch_shapes=[
            pltpu.VMEM((PIECES, 6, quarter // 2, piece), bf),
            pltpu.VMEM((PIECES, 2, quarter // 2, piece), bf),
            pltpu.VMEM((PIECES, quarter, piece), bf),
            pltpu.VMEM((PIECES, 6, sub // 2, piece), bf),
            pltpu.VMEM((PIECES, 2, sub // 2, piece), bf),
        ]
        + [pltpu.SemaphoreType.DMA((PIECES, 6))] * 4
        + [pltpu.SemaphoreType.DMA((PIECES, 8))] * 2,
        compiler_params=pltpu.CompilerParams(
            collective_id=ident, has_side_effects=True, vmem_limit_bytes=40 * 2**20
        ),
    )(partial)


PARTS = 3


def scatter_kernel(depth, cut, width, p_ref, g_ref, v_ref, o_ref, inbox, out, ss, rs):
    at = dp_place()
    up, down, zed = at(1, 0, 0), at(-1, 0, 0), at(0, 1, 0)
    greet("dp", (up, down, zed))
    part_width = width // PARTS
    sent = []

    def chip(dy, dz):
        return at(dy, dz, 0) // 2

    def cols(q):
        return pl.ds(q * part_width, part_width)

    def block(dy, dz, q, lo=0, size=depth):
        return p_ref.at[pl.ds(pl.multiple_of(chip(dy, dz) * depth + lo, 16), size), cols(q)]

    def half(slot, lo, size, q):
        return inbox.at[slot, pl.ds(lo, size), cols(q)]

    def go(src, dst, k, q, target):
        copy = remote(src, dst, ss.at[q, k], rs.at[q, k], "dp", target)
        copy.start()
        sent.append(copy)

    def got(ref, k, q):
        remote(ref, ref, ss.at[q, k], rs.at[q, k], "dp", zed).wait_recv()

    def whole(slot, q):
        return half(slot, 0, depth, q)

    rest = depth - cut

    def step(i, q):
        if i == 0:
            go(block(2, 1, q), whole(0, q), 0, q, zed)
            go(block(1, 1, q), whole(1, q), 1, q, up)
            go(block(-1, 1, q), whole(2, q), 2, q, down)
        if i == 1:
            got(whole(0, q), 0, q)
            out[0, :, cols(q)] = plus(block(2, 0, q)[...], inbox[0, :, cols(q)]).astype(jnp.bfloat16)
            go(out.at[0, pl.ds(0, cut), cols(q)], half(3, 0, cut, q), 3, q, up)
            go(out.at[0, pl.ds(cut, rest), cols(q)], half(3, cut, rest, q), 4, q, down)
            got(whole(1, q), 1, q)
            got(whole(2, q), 2, q)
            out[1, :, cols(q)] = plus(
                block(0, 1, q)[...], inbox[1, :, cols(q)], inbox[2, :, cols(q)]
            ).astype(jnp.bfloat16)
            go(out.at[1, :, cols(q)], whole(4, q), 5, q, zed)
        if i == 2:
            got(half(3, 0, cut, q), 3, q)
            out[2, :cut, cols(q)] = plus(
                block(1, 0, q, 0, cut)[...], inbox[3, :cut, cols(q)]
            ).astype(jnp.bfloat16)
            out[2, cut:, cols(q)] = block(1, 0, q, cut, rest)[...]
            go(out.at[2, :, cols(q)], whole(5, q), 6, q, up)
            got(half(3, cut, rest, q), 4, q)
            out[3, cut:, cols(q)] = plus(
                block(-1, 0, q, cut, rest)[...], inbox[3, cut:, cols(q)]
            ).astype(jnp.bfloat16)
            out[3, :cut, cols(q)] = block(-1, 0, q, 0, cut)[...]
            go(out.at[3, :, cols(q)], whole(6, q), 7, q, down)
        if i == 3:
            got(whole(4, q), 5, q)
            got(whole(5, q), 6, q)
            got(whole(6, q), 7, q)
            total = plus(
                block(0, 0, q)[...], inbox[4, :, cols(q)], inbox[5, :, cols(q)], inbox[6, :, cols(q)]
            )
            o_ref[:, cols(q)] = (
                g_ref[:, cols(q)].astype(jnp.float32)
                + (1.0 - damping) * v_ref[:, cols(q)].astype(jnp.float32)
                - step_size * total
            ).astype(jnp.bfloat16)

    for t in range(4 + PARTS - 1):
        for q in range(PARTS):
            if 0 <= t - q < 4:
                step(t - q, q)
    for copy in sent:
        copy.wait_send()


def scatter_update(partial, gradient, vector, ident):
    depth, width = gradient.shape
    cut = (depth // 32 + 1) * 16 if depth % 32 else depth // 2
    bf = jnp.bfloat16
    vmem = pl.BlockSpec(memory_space=pltpu.VMEM)
    return pl.pallas_call(
        functools.partial(scatter_kernel, depth, cut, width),
        out_shape=jax.ShapeDtypeStruct((depth, width), bf),
        in_specs=[vmem] * 3,
        out_specs=vmem,
        scratch_shapes=[
            pltpu.VMEM((7, depth, width), bf),
            pltpu.VMEM((4, depth, width), bf),
            pltpu.SemaphoreType.DMA((PARTS, 8)),
            pltpu.SemaphoreType.DMA((PARTS, 8)),
        ],
        compiler_params=pltpu.CompilerParams(
            collective_id=ident, has_side_effects=True, vmem_limit_bytes=40 * 2**20
        ),
    )(partial, gradient, vector)


def shifted(block, axis, distance):
    devices = range(lax.axis_size(axis))
    route = [(i - distance, i) for i in devices if i - distance in devices]
    return lax.ppermute(block, axis, route)


def swapped(block):
    return lax.ppermute(block, "dp", [(i, i ^ 1) for i in range(16)])


def per_device(tokens, target, segments, gate_weight, up_weight, down_weight, vector, gradient):
    tok_rows, full_width = tokens.shape
    depth = gate_weight.shape[0]
    inv_root = float(full_width) ** (-0.5)
    core = lax.axis_index("dp") % 2
    other_tokens = swapped(tokens)
    last_id = segments[-1:] + 1
    before_id = shifted(last_id, "dp", 1) - 1
    gate_full, up_full, vector_full, down_full = gather(
        (gate_weight, up_weight, vector, down_weight), 1
    )
    pre_gate = jnp.dot(tokens, gate_full, preferred_element_type=jnp.float32)
    up_act = jnp.dot(tokens, up_full, preferred_element_type=jnp.float32)
    tangent_raw = jnp.dot(tokens, vector_full, preferred_element_type=jnp.float32)
    tangent_gate = tangent_raw * inv_root
    gelu_value, gelu_slope, gelu_curve = gelu_parts(pre_gate)
    hidden = (gelu_value * up_act).astype(jnp.bfloat16)
    tangent_hidden = (gelu_slope * tangent_gate * up_act).astype(jnp.bfloat16)
    stacked = jnp.concatenate([hidden, tangent_hidden], axis=0)
    partial_out = lax.dot_general(
        stacked, down_full, (((1,), (1,)), ((), ())), preferred_element_type=jnp.float32
    )
    previous = jnp.concatenate([before_id, segments[:-1]])
    keep_mask = (segments == previous).astype(jnp.float32)[:, None]
    summed = sum_over_shard(partial_out.astype(jnp.bfloat16), 2).astype(jnp.float32)
    grad_out = (keep_mask * (summed[:tok_rows] - target.astype(jnp.float32))).astype(jnp.bfloat16)
    tangent_grad = (keep_mask * summed[tok_rows:]).astype(jnp.bfloat16)
    returned = jnp.concatenate([grad_out, tangent_grad], axis=0)
    back_hidden = jnp.dot(returned, down_full, preferred_element_type=jnp.float32)
    grad_hidden = back_hidden[:tok_rows]
    tangent_grad_hidden = back_hidden[tok_rows:]
    tangent_grad_gate = (
        up_act * (tangent_grad_hidden * gelu_slope + grad_hidden * gelu_curve * tangent_gate)
    ).astype(jnp.bfloat16)

    def own_columns(block):
        cut = block.reshape(tok_rows, 8, 2, depth)
        return lax.dynamic_index_in_dim(cut, core, 2, keepdims=False).reshape(tok_rows, 8 * depth)

    both_tokens = jnp.concatenate([own_columns(tokens), own_columns(other_tokens)], axis=0)
    both_grads = jnp.concatenate([tangent_grad_gate, swapped(tangent_grad_gate)], axis=0)
    partial_curvature = (
        lax.dot_general(
            both_tokens, both_grads, (((0,), (0,)), ((), ())), preferred_element_type=jnp.float32
        )
        * inv_root
    ).astype(jnp.bfloat16)
    return scatter_update(partial_curvature, gradient, vector, 3)


def solution(mesh):
    return jax.shard_map(
        per_device,
        mesh=mesh,
        in_specs=(
            P("dp", None),
            P("dp", None),
            P("dp"),
            P("dp", "shard"),
            P("dp", "shard"),
            P("dp", "shard"),
            P("dp", "shard"),
            P("dp", "shard"),
        ),
        out_specs=P("dp", "shard"),
        check_vma=False,
    )
```

```python
import functools

import jax
import jax.numpy as jnp
from jax import lax
from jax.experimental import pallas as pl
from jax.experimental.pallas import tpu as pltpu
from jax.sharding import PartitionSpec as P

MESH = pl.DeviceIdType.MESH
coeff_k = 0.7978845608028654
coeff_c = 0.044715
damping = 0.01
step_size = 0.8


def gelu_parts(pre_act):
    inner_arg = coeff_k * (pre_act + coeff_c * pre_act * pre_act * pre_act)
    tanh_value = jnp.tanh(inner_arg)
    slope_term = coeff_k * (1.0 + 3.0 * coeff_c * pre_act * pre_act)
    curve_term = 6.0 * coeff_k * coeff_c * pre_act
    sech_square = 1.0 - tanh_value * tanh_value
    gelu_value = 0.5 * pre_act * (1.0 + tanh_value)
    gelu_slope = 0.5 * (1.0 + tanh_value) + 0.5 * pre_act * sech_square * slope_term
    gelu_curve = sech_square * (
        slope_term + 0.5 * pre_act * (curve_term - 2.0 * tanh_value * slope_term * slope_term)
    )
    return (gelu_value, gelu_slope, gelu_curve)


def remote(src, dst, send_sem, recv_sem, axis, index):
    return pltpu.make_async_remote_copy(
        src_ref=src,
        dst_ref=dst,
        send_sem=send_sem,
        recv_sem=recv_sem,
        device_id={axis: index},
        device_id_type=MESH,
    )


GATHER_COPIES = 17
PARTS = 3


def plus(a, *more):
    total = a.astype(jnp.float32)
    for b in more:
        total = total + b.astype(jnp.float32)
    return total


def dot_nn(a, b):
    return jnp.dot(a, b, preferred_element_type=jnp.float32)


def dot_nt(a, b):
    return lax.dot_general(a, b, (((1,), (1,)), ((), ())), preferred_element_type=jnp.float32)


def dot_tn(a, b):
    return lax.dot_general(a, b, (((0,), (0,)), ((), ())), preferred_element_type=jnp.float32)


def step_kernel(
    dims, tok_hbm, tgt_hbm, seg_hbm, gate_hbm, up_hbm, vec_hbm, down_hbm, grad_hbm, o_ref,
    full, tok, tgt, tok4, tok_t, tok_t2, tgt_t, seg, seg_prev, keep, acc, stacked, p, back, gt,
    xin, xtx, xc, zin, ztx, tgg, tgg2, cp, cin, cout, grad,
    gs, gr, sx, rx, sz, rz, s4, r4, cs, cr, ms, mr, ls,
):
    tok_rows, width, depth, cols = dims
    bf = jnp.bfloat16
    d, sh = lax.axis_index("dp"), lax.axis_index("shard")
    y, zl, core = d // 4, (d // 2) % 2, d % 2
    x, zh = sh % 4, sh // 4
    piece = 4 * depth
    cut = (depth // 32 + 1) * 16
    part = cols // PARTS
    inv_root = float(width) ** (-0.5)

    def at(dy, dz, dc):
        return ((y + dy) % 4) * 4 + ((zl + dz) % 2) * 2 + (core + dc) % 2

    sib, up, down, zed = at(0, 0, 1), at(1, 0, 0), at(-1, 0, 0), at(0, 1, 0)
    right, left = zh * 4 + (x + 1) % 4, zh * 4 + (x + 3) % 4
    above, below = ((zh + 1) % 4) * 4 + x, ((zh + 3) % 4) * 4 + x
    after, before = (d + 1) % 16, (d + 15) % 16
    barrier = pltpu.get_barrier_semaphore()
    for axis, targets in (("dp", (sib, up, down, zed, after, before)), ("shard", (right, left, above, below))):
        for t in targets:
            pl.semaphore_signal(barrier, inc=1, device_id={axis: t}, device_id_type=MESH)

    loads = [
        pltpu.make_async_copy(src, dst, ls.at[i])
        for i, (src, dst) in enumerate(((tok_hbm, tok), (tgt_hbm, tgt), (seg_hbm, seg), (grad_hbm, grad)))
    ]
    for copy in loads:
        copy.start()
    pl.semaphore_wait(barrier, 10)

    sent = []

    def go(src, dst, s, r, axis, target):
        copy = remote(src, dst, s, r, axis, target)
        copy.start()
        sent.append(copy)

    def got(ref, s, r):
        remote(ref, ref, s, r, "dp", sib).wait_recv()

    def rows(w, owner, which):
        lo, size = {"w": (0, depth), "a": (0, cut), "b": (cut, depth - cut)}[which]
        return full.at[w, pl.ds(pl.multiple_of(owner * depth + lo, 16), size)]

    me = at(0, 0, 0)
    table = [
        (me, "w", sib, at(0, 0, 1)),
        (me, "w", up, at(-1, 0, 0)),
        (me, "w", down, at(1, 0, 0)),
        (me, "w", zed, at(0, 1, 0)),
        (at(0, 1, 0), "w", up, at(-1, 1, 0)),
        (at(0, 1, 0), "w", down, at(1, 1, 0)),
        (at(0, 1, 0), "w", sib, at(0, 1, 1)),
        (at(-1, 0, 0), "a", up, at(2, 0, 0)),
        (at(1, 0, 0), "b", down, at(2, 0, 0)),
        (at(-1, 0, 0), "w", sib, at(-1, 0, 1)),
        (at(1, 0, 0), "w", sib, at(1, 0, 1)),
        (at(-1, 1, 0), "w", sib, at(-1, 1, 1)),
        (at(1, 1, 0), "w", sib, at(1, 1, 1)),
        (at(2, 0, 0), "a", zed, at(2, 1, 0)),
        (at(2, 0, 0), "b", zed, at(2, 1, 0)),
        (at(2, 0, 0), "w", sib, at(2, 0, 1)),
        (at(2, 1, 0), "w", sib, at(2, 1, 1)),
    ]
    ins = (gate_hbm, up_hbm, vec_hbm, down_hbm)

    def start(w, *numbers):
        for k in numbers:
            owner, which, target, _ = table[k]
            src = ins[w] if k < 4 else rows(w, owner, which)
            go(src, rows(w, owner, which), gs.at[w, k], gr.at[w, k], "dp", target)

    def wait(w, *numbers):
        for k in numbers:
            _, which, _, owner = table[k]
            got(rows(w, owner, which), gs.at[w, k], gr.at[w, k])

    own_copies = [pltpu.make_async_copy(ins[w], rows(w, me, "w"), ls.at[4 + w]) for w in range(4)]

    def stage_a(w):
        wait(w, 3)
        start(w, 4, 5, 6)
        wait(w, 1)
        start(w, 7, 9)
        wait(w, 2)
        start(w, 8, 10)

    def stage_b(w):
        wait(w, 7)
        start(w, 13)
        wait(w, 8)
        start(w, 14, 15)
        wait(w, 4)
        start(w, 11)
        wait(w, 5)
        start(w, 12)

    def stage_c(w):
        wait(w, 13, 14)
        start(w, 16)

    late = {0: (0, 6), -1: (9, 11), 1: (10, 12), 2: (15, 16)}

    def piece_of(rel):
        return (y + rel) % 4

    def piece_rows(rel):
        return pl.ds(pl.multiple_of(piece_of(rel) * piece, 16), piece)

    def use(w, rel):
        wait(w, *late[rel])
        if rel == 0:
            own_copies[w].wait()

        def chunk(n, _):
            c = pl.ds(pl.multiple_of(n * 384, 128), 384)
            term = dot_nn(tok4[piece_of(rel)], full[w, piece_rows(rel), c])
            if rel == 0:
                acc[w, :, c] = term
            else:
                acc[w, :, c] += term
            return 0

        lax.fori_loop(0, cols // 384, chunk, 0)

    start(0, 1, 2, 3, 0)
    own_copies[0].start()
    go(seg_hbm, seg_prev, ms.at[0], mr.at[0], "dp", after)
    start(1, 1, 2, 3, 0)
    own_copies[1].start()

    loads[0].wait()
    for r in range(4):
        tok4[r] = tok[:, r * piece : (r + 1) * piece]

    def turn(src, dst):
        def body(j, _):
            c = pl.ds(pl.multiple_of(j * 128, 128), 128)
            dst[c, :] = src[:, c].astype(jnp.float32).T.astype(bf)
            return 0

        lax.fori_loop(0, width // 128, body, 0)

    turn(tok, tok_t)
    go(tok_t, tok_t2, ms.at[1], mr.at[1], "dp", sib)
    loads[1].wait()
    turn(tgt, tgt_t)

    stage_a(0)
    start(2, 1, 2, 3, 0)
    own_copies[2].start()
    stage_a(1)
    stage_b(0)
    use(0, 0)
    stage_a(2)
    start(3, 1, 2)
    own_copies[3].start()
    stage_b(1)
    use(1, 0)
    stage_c(0)
    use(0, -1)
    use(0, 1)
    stage_b(2)
    start(3, 3, 0)
    use(2, 0)
    stage_c(1)
    use(1, -1)
    use(1, 1)
    use(0, 2)
    use(2, -1)
    use(2, 1)
    use(1, 2)
    stage_c(2)
    stage_a(3)
    use(2, 2)

    loads[2].wait()
    got(seg_prev, ms.at[0], mr.at[0])
    lane = lax.broadcasted_iota(jnp.int32, (8, tok_rows), 1)
    here = jnp.broadcast_to(seg[...], (8, tok_rows))
    previous = jnp.where(
        lane == 0,
        pltpu.roll(jnp.broadcast_to(seg_prev[...], (8, tok_rows)), 1, 1),
        pltpu.roll(here, 1, 1),
    )
    first = (lane + d) == 0
    keep[...] = jnp.where(first, 0.0, jnp.where(here == previous, 1.0, 0.0))

    def pointwise(i, _):
        r = pl.ds(pl.multiple_of(i * 16, 16), 16)
        r2 = pl.ds(pl.multiple_of(tok_rows + i * 16, 16), 16)
        value, slope, curve = gelu_parts(acc[0, r])
        up_act = acc[1, r]
        tangent = acc[2, r] * inv_root
        stacked[r] = (value * up_act).astype(bf)
        stacked[r2] = (slope * tangent * up_act).astype(bf)
        acc[0, r] = up_act * slope
        acc[1, r] = up_act * curve * tangent
        return 0

    lax.fori_loop(0, tok_rows // 16, pointwise, 0)

    order = (0, -1, 1, 2)

    def out_piece(rel):
        wait(3, *late[rel])
        if rel == 0:
            own_copies[3].wait()

        def chunk(n, _):
            r = pl.ds(pl.multiple_of(piece_of(rel) * piece + n * depth, 16), depth)
            p[r] = dot_nt(full[3, r], stacked[...]).astype(bf)
            return 0

        lax.fori_loop(0, 4, chunk, 0)

    def x_src(q):
        def src(chunk, lo, size):
            r = pl.ds(pl.multiple_of(piece_of(order[q]) * piece + lo, 16), size)
            return p.at[r, pl.ds(pl.multiple_of(((x + chunk) % 4) * 128, 128), 128)]

        return src

    def z_src(q):
        def src(chunk, lo, size):
            return xc.at[q, pl.ds(pl.multiple_of(((zh + chunk) % 4) * depth + lo, 16), size)]

        return src

    def ring1(q, src, size, mid, inbox, s, r, plus1, minus1):
        rest = size - mid
        for i, (dst, frm, lo, n, target) in enumerate((
            (0, 2, mid, rest, plus1), (0, 2, 0, mid, minus1), (1, 1, 0, mid, plus1), (2, 3, mid, rest, minus1),
        )):
            go(src(frm, lo, n), inbox.at[q, dst, pl.ds(lo, n)], s.at[q, i], r.at[q, i], "shard", target)

    def ring2(q, src, size, mid, inbox, out, s, r, plus1, minus1):
        rest = size - mid
        for i, (dst, frm, lo, n, target) in enumerate(((1, 1, mid, rest, plus1), (2, 3, 0, mid, minus1))):
            came = inbox.at[q, 0, pl.ds(lo, n)]
            got(came, s.at[q, i], r.at[q, i])
            out[q, lo : lo + n] = plus(src(frm, lo, n)[...], came[...]).astype(bf)
            go(out.at[q, pl.ds(lo, n)], inbox.at[q, dst, pl.ds(lo, n)], s.at[q, 4 + i], r.at[q, 4 + i], "shard", target)

    def ring3(q, src, size, mid, inbox, s, r):
        got(inbox.at[q, 1, pl.ds(0, mid)], s.at[q, 2], r.at[q, 2])
        got(inbox.at[q, 2, pl.ds(mid, size - mid)], s.at[q, 3], r.at[q, 3])
        got(inbox.at[q, 1, pl.ds(mid, size - mid)], s.at[q, 4], r.at[q, 4])
        got(inbox.at[q, 2, pl.ds(0, mid)], s.at[q, 5], r.at[q, 5])
        return plus(src(0, 0, size)[...], inbox[q, 1], inbox[q, 2])

    def g_block(q, lo, size, chunk):
        r = pl.ds(pl.multiple_of(piece_of(order[q]) * piece + lo, 16), size)
        return gt.at[r, pl.ds(pl.multiple_of(((x + chunk) % 4) * 128, 128), 128)]

    def send_g(q, i, ref, target):
        go(ref, ref, s4.at[q, i], r4.at[q, i], "shard", target)

    def got_g(q, i, ref):
        got(ref, s4.at[q, i], r4.at[q, i])

    def step(i, q):
        half = piece // 2
        if i == 0:
            ring1(q, x_src(q), piece, half, xin, sx, rx, right, left)
        if i == 1:
            ring2(q, x_src(q), piece, half, xin, xtx, sx, rx, right, left)
        if i == 2:
            xc[q] = ring3(q, x_src(q), piece, half, xin, sx, rx).astype(bf)
            ring1(q, z_src(q), depth, cut, zin, sz, rz, above, below)
        if i == 3:
            ring2(q, z_src(q), depth, cut, zin, ztx, sz, rz, above, below)
        if i == 4:
            total = ring3(q, z_src(q), depth, cut, zin, sz, rz)
            lanes = pl.ds(pl.multiple_of((x % 2) * 128, 128), 128)
            r = pl.ds(pl.multiple_of(piece_of(order[q]) * piece + zh * depth, 16), depth)
            is_out = (1 - x // 2).astype(jnp.float32)
            wanted = tgt_t[r, lanes].astype(jnp.float32) * is_out
            mine = g_block(q, zh * depth, depth, 0)
            mine[...] = (keep[0:1, lanes] * (total - wanted)).astype(bf)
            send_g(q, 0, mine, above)
            send_g(q, 1, mine, below)
        if i == 5:
            lo, hi = ((zh + 3) % 4) * depth, ((zh + 1) % 4) * depth
            got_g(q, 0, g_block(q, lo, depth, 0))
            send_g(q, 2, g_block(q, lo, cut, 0), above)
            got_g(q, 1, g_block(q, hi, depth, 0))
            send_g(q, 3, g_block(q, hi + cut, depth - cut, 0), below)
        if i == 6:
            far = ((zh + 2) % 4) * depth
            got_g(q, 2, g_block(q, far, cut, 0))
            got_g(q, 3, g_block(q, far + cut, depth - cut, 0))
            send_g(q, 4, g_block(q, 0, piece, 0), right)
            send_g(q, 5, g_block(q, 0, piece, 0), left)
        if i == 7:
            got_g(q, 4, g_block(q, 0, piece, 3))
            send_g(q, 6, g_block(q, 0, half, 3), right)
            got_g(q, 5, g_block(q, 0, piece, 1))
            send_g(q, 7, g_block(q, half, half, 1), left)
        if i == 8:
            got_g(q, 6, g_block(q, 0, half, 2))
            got_g(q, 7, g_block(q, half, half, 2))

            def chunk(n, _):
                c = pl.ds(pl.multiple_of(n * 384, 128), 384)
                term = dot_tn(gt[piece_rows(order[q])], full[3, piece_rows(order[q]), c])
                if q == 0:
                    back[:, c] = term
                else:
                    back[:, c] += term
                return 0

            lax.fori_loop(0, cols // 384, chunk, 0)

    out_piece(0)
    step(0, 0)
    stage_b(3)
    out_piece(-1)
    step(0, 1)
    step(1, 0)
    out_piece(1)
    step(0, 2)
    step(1, 1)
    step(2, 0)
    stage_c(3)
    step(3, 0)
    step(2, 1)
    step(1, 2)
    out_piece(2)
    step(0, 3)
    for t in range(4, 12):
        for q in range(4):
            i = t - q
            if 0 <= i < 9:
                step(i, q)

    loads[3].wait()
    got(tok_t2, ms.at[1], mr.at[1])

    def pc(q):
        return pl.ds(q * part, part)

    def chip(dy, dz):
        return at(dy, dz, 0) // 2

    def c_block(dy, dz, q, lo=0, size=depth):
        return cp.at[pl.ds(pl.multiple_of(chip(dy, dz) * depth + lo, 16), size), pc(q)]

    def make(q, *which):
        for dy, dz in which:
            r = pl.ds(pl.multiple_of(at(dy, dz, 0) * depth, 16), depth)
            total = dot_nn(tok_t[r], tgg[:, pc(q)]) + dot_nn(tok_t2[r], tgg2[:, pc(q)])
            c_block(dy, dz, q)[...] = (total * inv_root).astype(bf)

    def box(slot, q, lo=0, size=depth):
        return cin.at[slot, pl.ds(lo, size), pc(q)]

    def send_c(src, dst, k, q, target):
        go(src, dst, cs.at[q, k], cr.at[q, k], "dp", target)

    def got_c(ref, k, q):
        got(ref, cs.at[q, k], cr.at[q, k])

    rest = depth - cut

    def reduce_step(i, q):
        if i == 0:
            got(tgg2.at[:, pc(q)], ms.at[2 + q], mr.at[2 + q])
            make(q, (2, 1), (1, 1), (-1, 1))
            send_c(c_block(2, 1, q), box(0, q), 0, q, zed)
            send_c(c_block(1, 1, q), box(1, q), 1, q, up)
            send_c(c_block(-1, 1, q), box(2, q), 2, q, down)
            make(q, (2, 0), (0, 1), (1, 0), (-1, 0), (0, 0))
        if i == 1:
            got_c(box(0, q), 0, q)
            cout[0, :, pc(q)] = plus(c_block(2, 0, q)[...], box(0, q)[...]).astype(bf)
            send_c(cout.at[0, pl.ds(0, cut), pc(q)], box(3, q, 0, cut), 3, q, up)
            send_c(cout.at[0, pl.ds(cut, rest), pc(q)], box(3, q, cut, rest), 4, q, down)
            got_c(box(1, q), 1, q)
            got_c(box(2, q), 2, q)
            cout[1, :, pc(q)] = plus(c_block(0, 1, q)[...], box(1, q)[...], box(2, q)[...]).astype(bf)
            send_c(cout.at[1, :, pc(q)], box(4, q), 5, q, zed)
        if i == 2:
            got_c(box(3, q, 0, cut), 3, q)
            cout[2, :cut, pc(q)] = plus(c_block(1, 0, q, 0, cut)[...], box(3, q, 0, cut)[...]).astype(bf)
            cout[2, cut:, pc(q)] = c_block(1, 0, q, cut, rest)[...]
            send_c(cout.at[2, :, pc(q)], box(5, q), 6, q, up)
            got_c(box(3, q, cut, rest), 4, q)
            cout[3, cut:, pc(q)] = plus(c_block(-1, 0, q, cut, rest)[...], box(3, q, cut, rest)[...]).astype(bf)
            cout[3, :cut, pc(q)] = c_block(-1, 0, q, 0, cut)[...]
            send_c(cout.at[3, :, pc(q)], box(6, q), 7, q, down)
        if i == 3:
            got_c(box(4, q), 5, q)
            got_c(box(5, q), 6, q)
            got_c(box(6, q), 7, q)
            total = plus(c_block(0, 0, q)[...], box(4, q)[...], box(5, q)[...], box(6, q)[...])
            own = full[2, pl.ds(pl.multiple_of(me * depth, 16), depth), pc(q)]
            o_ref[:, pc(q)] = (
                grad[:, pc(q)].astype(jnp.float32)
                + (1.0 - damping) * own.astype(jnp.float32)
                - step_size * total
            ).astype(bf)

    for q in range(PARTS):

        def combine(i, _):
            r = pl.ds(pl.multiple_of(i * 32, 16), 32)
            r2 = pl.ds(pl.multiple_of(tok_rows + i * 32, 16), 32)
            tgg[r, pc(q)] = (acc[0, r, pc(q)] * back[r2, pc(q)] + acc[1, r, pc(q)] * back[r, pc(q)]).astype(bf)
            return 0

        lax.fori_loop(0, tok_rows // 32, combine, 0)
        go(tgg.at[:, pc(q)], tgg2.at[:, pc(q)], ms.at[2 + q], mr.at[2 + q], "dp", sib)
    for t in range(4 + PARTS - 1):
        for q in range(PARTS):
            if 0 <= t - q < 4:
                reduce_step(t - q, q)
    for copy in sent:
        copy.wait_send()


def per_device(tokens, target, segments, gate_weight, up_weight, down_weight, vector, gradient):
    tok_rows, width = tokens.shape
    depth, cols = gate_weight.shape
    bf, f32 = jnp.bfloat16, jnp.float32
    piece = 4 * depth
    cut = (depth // 32 + 1) * 16
    vm, dma = pltpu.VMEM, pltpu.SemaphoreType.DMA
    anywhere = pl.BlockSpec(memory_space=pl.ANY)
    scratch = [
        vm((4, width, cols), bf),
        vm((tok_rows, width), bf),
        vm((tok_rows, width), bf),
        vm((4, tok_rows, piece), bf),
        vm((width, tok_rows), bf),
        vm((width, tok_rows), bf),
        vm((width, tok_rows), bf),
        vm((1, tok_rows), jnp.int32),
        vm((1, tok_rows), jnp.int32),
        vm((8, tok_rows), f32),
        vm((3, tok_rows, cols), f32),
        vm((2 * tok_rows, cols), bf),
        vm((width, 2 * tok_rows), bf),
        vm((2 * tok_rows, cols), f32),
        vm((width, 2 * tok_rows), bf),
        vm((4, 3, piece, 128), bf),
        vm((4, piece, 128), bf),
        vm((4, piece, 128), bf),
        vm((4, 3, depth, 128), bf),
        vm((4, depth, 128), bf),
        vm((tok_rows, cols), bf),
        vm((tok_rows, cols), bf),
        vm((8 * depth, cols), bf),
        vm((7, depth, cols), bf),
        vm((4, depth, cols), bf),
        vm((depth, cols), bf),
        dma((4, GATHER_COPIES)),
        dma((4, GATHER_COPIES)),
        dma((4, 6)),
        dma((4, 6)),
        dma((4, 6)),
        dma((4, 6)),
        dma((4, 8)),
        dma((4, 8)),
        dma((PARTS, 8)),
        dma((PARTS, 8)),
        dma((2 + PARTS,)),
        dma((2 + PARTS,)),
        dma((8,)),
    ]
    return pl.pallas_call(
        functools.partial(step_kernel, (tok_rows, width, depth, cols)),
        out_shape=jax.ShapeDtypeStruct((depth, cols), bf),
        in_specs=[anywhere] * 8,
        out_specs=pl.BlockSpec(memory_space=pltpu.VMEM),
        scratch_shapes=scratch,
        compiler_params=pltpu.CompilerParams(
            collective_id=1, has_side_effects=True, vmem_limit_bytes=62 * 2**20
        ),
    )(tokens, target, segments[None], gate_weight, up_weight, vector, down_weight, gradient)


def solution(mesh):
    return jax.shard_map(
        per_device,
        mesh=mesh,
        in_specs=(
            P("dp", None),
            P("dp", None),
            P("dp"),
            P("dp", "shard"),
            P("dp", "shard"),
            P("dp", "shard"),
            P("dp", "shard"),
            P("dp", "shard"),
        ),
        out_specs=P("dp", "shard"),
        check_vma=False,
    )
```

```python
import functools

import jax
import jax.numpy as jnp
from jax import lax
from jax.experimental import pallas as pl
from jax.experimental.pallas import tpu as pltpu
from jax.sharding import PartitionSpec as P

MESH = pl.DeviceIdType.MESH
coeff_k = 0.7978845608028654
coeff_c = 0.044715
damping = 0.01
step_size = 0.8


def gelu_parts(pre_act):
    inner_arg = coeff_k * (pre_act + coeff_c * pre_act * pre_act * pre_act)
    tanh_value = jnp.tanh(inner_arg)
    slope_term = coeff_k * (1.0 + 3.0 * coeff_c * pre_act * pre_act)
    curve_term = 6.0 * coeff_k * coeff_c * pre_act
    sech_square = 1.0 - tanh_value * tanh_value
    gelu_value = 0.5 * pre_act * (1.0 + tanh_value)
    gelu_slope = 0.5 * (1.0 + tanh_value) + 0.5 * pre_act * sech_square * slope_term
    gelu_curve = sech_square * (
        slope_term + 0.5 * pre_act * (curve_term - 2.0 * tanh_value * slope_term * slope_term)
    )
    return (gelu_value, gelu_slope, gelu_curve)


def remote(src, dst, send_sem, recv_sem, axis, index):
    return pltpu.make_async_remote_copy(
        src_ref=src,
        dst_ref=dst,
        send_sem=send_sem,
        recv_sem=recv_sem,
        device_id={axis: index},
        device_id_type=MESH,
    )


GATHER_COPIES = 19
PARTS = 3


def plus(a, *more):
    total = a.astype(jnp.float32)
    for b in more:
        total = total + b.astype(jnp.float32)
    return total


def dot_nn(a, b):
    return jnp.dot(a, b, preferred_element_type=jnp.float32)


def dot_nt(a, b):
    return lax.dot_general(a, b, (((1,), (1,)), ((), ())), preferred_element_type=jnp.float32)


def dot_tn(a, b):
    return lax.dot_general(a, b, (((0,), (0,)), ((), ())), preferred_element_type=jnp.float32)


def step_kernel(
    dims, tok_hbm, tgt_hbm, seg_hbm, gate_hbm, up_hbm, vec_hbm, down_hbm, grad_hbm, o_ref,
    full, tok, tgt, tok4, tok_t, tok_t2, tgt_t, seg, seg_prev, keep, acc, stacked, p, back, gt,
    xin, xtx, xc, zin, tgg, tgg2, cp, cin, cout, grad,
    gs, gr, sx, rx, sz, rz, s4, r4, cs, cr, ms, mr, ls,
):
    tok_rows, width, depth, cols = dims
    bf = jnp.bfloat16
    d, sh = lax.axis_index("dp"), lax.axis_index("shard")
    y, zl, core = d // 4, (d // 2) % 2, d % 2
    x, zh = sh % 4, sh // 4
    piece = 4 * depth
    cut = (depth // 32 + 1) * 16
    part = cols // PARTS
    inv_root = float(width) ** (-0.5)

    def at(dy, dz, dc):
        return ((y + dy) % 4) * 4 + ((zl + dz) % 2) * 2 + (core + dc) % 2

    sib, up, down, zed = at(0, 0, 1), at(1, 0, 0), at(-1, 0, 0), at(0, 1, 0)
    right, left = zh * 4 + (x + 1) % 4, zh * 4 + (x + 3) % 4
    above, below = ((zh + 1) % 4) * 4 + x, ((zh + 3) % 4) * 4 + x
    across = ((zh + 2) % 4) * 4 + x
    after, before = (d + 1) % 16, (d + 15) % 16
    barrier = pltpu.get_barrier_semaphore()
    for axis, targets in (("dp", (sib, up, down, zed, after, before)), ("shard", (right, left, above, below, across))):
        for t in targets:
            pl.semaphore_signal(barrier, inc=1, device_id={axis: t}, device_id_type=MESH)

    loads = [
        pltpu.make_async_copy(src, dst, ls.at[i])
        for i, (src, dst) in enumerate(((tok_hbm, tok), (tgt_hbm, tgt), (seg_hbm, seg), (grad_hbm, grad)))
    ]
    for copy in loads:
        copy.start()
    pl.semaphore_wait(barrier, 11)

    sent = []

    def go(src, dst, s, r, axis, target):
        copy = remote(src, dst, s, r, axis, target)
        copy.start()
        sent.append(copy)

    def got(ref, s, r):
        remote(ref, ref, s, r, "dp", sib).wait_recv()

    def place(dy, dz, dc):
        return {0: 2 * dz, -1: 4 + 4 * dz, 1: 6 + 4 * dz, 2: 12 + 2 * dz}[dy] + dc

    def rows(w, rel, which):
        lo, size = {"w": (0, depth), "a": (0, cut), "b": (cut, depth - cut)}[which]
        base = place(*rel) if w == 3 else at(*rel)
        return full.at[w, pl.ds(pl.multiple_of(base * depth + lo, 16), size)]

    me = at(0, 0, 0)
    table = [
        ((0, 0, 0), "w", sib, (0, 0, 1)),
        ((0, 0, 0), "w", up, (-1, 0, 0)),
        ((0, 0, 0), "w", down, (1, 0, 0)),
        ((0, 0, 0), "w", zed, (0, 1, 0)),
        ((0, 1, 0), "w", up, (-1, 1, 0)),
        ((0, 1, 0), "w", down, (1, 1, 0)),
        ((0, 1, 0), "w", sib, (0, 1, 1)),
        ((-1, 0, 0), "a", up, (2, 0, 0)),
        ((1, 0, 0), "b", down, (2, 0, 0)),
        ((-1, 0, 0), "w", sib, (-1, 0, 1)),
        ((1, 0, 0), "w", sib, (1, 0, 1)),
        ((-1, 1, 0), "w", sib, (-1, 1, 1)),
        ((1, 1, 0), "w", sib, (1, 1, 1)),
        ((2, 0, 0), "a", zed, (2, 1, 0)),
        ((2, 0, 0), "b", zed, (2, 1, 0)),
        ((2, 0, 0), "w", sib, (2, 0, 1)),
        ((2, 1, 0), "w", sib, (2, 1, 1)),
    ]
    halves = {
        1: ((0, 0, 0), "a", up, (-1, 0, 0)),
        2: ((0, 0, 0), "b", down, (1, 0, 0)),
        17: ((0, 0, 0), "b", up, (-1, 0, 0)),
        18: ((0, 0, 0), "a", down, (1, 0, 0)),
    }
    ins = (gate_hbm, up_hbm, vec_hbm, down_hbm)

    def entry(w, k):
        return halves[k] if w == 3 and k in halves else table[k]

    def start(w, *numbers):
        for k in numbers:
            mine, which, target, theirs = entry(w, k)
            src = rows(w, mine, which)
            if mine == (0, 0, 0):
                src = ins[w].at[pl.ds({"w": 0, "a": 0, "b": cut}[which], {"w": depth, "a": cut, "b": depth - cut}[which])]
            dst = rows(w, theirs if w == 3 else mine, which)
            go(src, dst, gs.at[w, k], gr.at[w, k], "dp", target)

    def wait(w, *numbers):
        for k in numbers:
            _, which, _, came = entry(w, k)
            got(rows(w, came, which), gs.at[w, k], gr.at[w, k])

    own_copies = [pltpu.make_async_copy(ins[w], rows(w, (0, 0, 0), "w"), ls.at[4 + w]) for w in range(4)]

    late = {0: (0, 6), -1: (9, 11), 1: (10, 12), 2: (15, 16)}

    def piece_of(rel):
        return (y + rel) % 4

    def piece_rows(rel):
        return pl.ds(pl.multiple_of(piece_of(rel) * piece, 16), piece)

    def use(w, rel):
        wait(w, *late[rel])
        if rel == 0:
            own_copies[w].wait()

        def chunk(n, _):
            c = pl.ds(pl.multiple_of(n * 384, 128), 384)
            term = dot_nn(tok4[piece_of(rel)], full[w, piece_rows(rel), c])
            if rel == 0:
                acc[w, :, c] = term
            else:
                acc[w, :, c] += term
            return 0

        lax.fori_loop(0, cols // 384, chunk, 0)

    start(0, 1, 2, 3, 0)
    own_copies[0].start()
    start(1, 1, 2, 3, 0)
    own_copies[1].start()
    go(seg_hbm, seg_prev, ms.at[0], mr.at[0], "dp", after)

    loads[0].wait()
    for r in range(4):
        tok4[r] = tok[:, r * piece : (r + 1) * piece]

    def turn(src, dst):
        def body(j, _):
            c = pl.ds(pl.multiple_of(j * 128, 128), 128)
            dst[c, :] = src[:, c].astype(jnp.float32).T.astype(bf)
            return 0

        lax.fori_loop(0, width // 128, body, 0)

    turn(tok, tok_t)
    go(tok_t, tok_t2, ms.at[1], mr.at[1], "dp", sib)
    loads[1].wait()
    turn(tgt, tgt_t)

    def near(w):
        wait(w, 1)
        start(w, 7, 9)
        wait(w, 2)
        start(w, 8, 10)
        wait(w, 3)
        start(w, 6)

    def far(w):
        wait(w, 7)
        start(w, 13)
        wait(w, 8)
        start(w, 14, 15)

    def diagonal(w):
        wait(w, 4)
        start(w, 11)
        wait(w, 5)
        start(w, 12)

    def last(w):
        wait(w, 13, 14)
        start(w, 16)

    near(0)
    start(0, 4, 5)
    start(2, 1, 2, 3, 0)
    own_copies[2].start()
    start(3, 3, 0)
    own_copies[3].start()
    near(1)
    far(0)
    diagonal(0)
    use(0, 0)
    near(2)
    start(1, 4, 5)
    start(2, 4, 5)
    start(3, 1, 2, 17, 18)
    far(1)
    use(1, 0)
    last(0)
    use(0, -1)
    use(0, 1)
    far(2)
    use(0, 2)
    use(2, 0)
    diagonal(1)
    wait(3, 3)
    start(3, 6)
    last(1)
    use(1, -1)
    use(1, 1)
    use(1, 2)
    diagonal(2)
    last(2)
    use(2, -1)
    use(2, 1)
    use(2, 2)
    wait(3, 1)
    start(3, 7)
    wait(3, 2)
    start(3, 8)

    loads[2].wait()
    got(seg_prev, ms.at[0], mr.at[0])
    lane = lax.broadcasted_iota(jnp.int32, (8, tok_rows), 1)
    here = jnp.broadcast_to(seg[...], (8, tok_rows))
    previous = jnp.where(
        lane == 0,
        pltpu.roll(jnp.broadcast_to(seg_prev[...], (8, tok_rows)), 1, 1),
        pltpu.roll(here, 1, 1),
    )
    first = (lane + d) == 0
    keep[...] = jnp.where(first, 0.0, jnp.where(here == previous, 1.0, 0.0))

    def pointwise(i, _):
        r = pl.ds(pl.multiple_of(i * 16, 16), 16)
        r2 = pl.ds(pl.multiple_of(tok_rows + i * 16, 16), 16)
        value, slope, curve = gelu_parts(acc[0, r])
        up_act = acc[1, r]
        tangent = acc[2, r] * inv_root
        stacked[r] = (value * up_act).astype(bf)
        stacked[r2] = (slope * tangent * up_act).astype(bf)
        acc[0, r] = up_act * slope
        acc[1, r] = up_act * curve * tangent
        return 0

    lax.fori_loop(0, tok_rows // 16, pointwise, 0)

    def out_piece(q):
        if q == 0:
            own_copies[3].wait()
            wait(3, 0, 6)
        else:
            wait(3, *{1: (9, 10), 2: (11, 12), 3: (15, 16)}[q])

        def chunk(n, _):
            r = pl.ds(pl.multiple_of(q * piece + n * 2 * depth, 16), 2 * depth)
            p[r] = dot_nt(full[3, r], stacked[...]).astype(bf)
            return 0

        lax.fori_loop(0, 2, chunk, 0)

    def x_src(q):
        def src(chunk, lo, size):
            return p.at[pl.ds(q * piece + lo, size), pl.ds(pl.multiple_of(((x + chunk) % 4) * 128, 128), 128)]

        return src

    def z_src(q):
        def src(chunk, lo, size):
            return xc.at[q, pl.ds(pl.multiple_of(((zh + chunk) % 4) * depth + lo, 16), size)]

        return src

    def block_owner(q, j):
        hi, lo = j // 2, j % 2
        if q == 0:
            return at(0, hi, lo)
        if q == 3:
            return at(2, hi, lo)
        return at(2 * hi - 1, q - 1, lo)

    def ring1(q, src, size, mid, inbox, s, r, plus1, minus1):
        rest = size - mid
        for i, (dst, frm, lo, n, target) in enumerate((
            (0, 2, mid, rest, plus1), (0, 2, 0, mid, minus1), (1, 1, 0, mid, plus1), (2, 3, mid, rest, minus1),
        )):
            go(src(frm, lo, n), inbox.at[q, dst, pl.ds(lo, n)], s.at[q, i], r.at[q, i], "shard", target)

    def ring2(q, src, size, mid, inbox, out, s, r, plus1, minus1):
        rest = size - mid
        for i, (dst, frm, lo, n, target) in enumerate(((1, 1, mid, rest, plus1), (2, 3, 0, mid, minus1))):
            came = inbox.at[q, 0, pl.ds(lo, n)]
            got(came, s.at[q, i], r.at[q, i])
            out[q, lo : lo + n] = plus(src(frm, lo, n)[...], came[...]).astype(bf)
            go(out.at[q, pl.ds(lo, n)], inbox.at[q, dst, pl.ds(lo, n)], s.at[q, 4 + i], r.at[q, 4 + i], "shard", target)

    def ring3(q, src, size, mid, inbox, s, r):
        got(inbox.at[q, 1, pl.ds(0, mid)], s.at[q, 2], r.at[q, 2])
        got(inbox.at[q, 2, pl.ds(mid, size - mid)], s.at[q, 3], r.at[q, 3])
        got(inbox.at[q, 1, pl.ds(mid, size - mid)], s.at[q, 4], r.at[q, 4])
        got(inbox.at[q, 2, pl.ds(0, mid)], s.at[q, 5], r.at[q, 5])
        return plus(src(0, 0, size)[...], inbox[q, 1], inbox[q, 2])

    def g_block(q, lo, size, chunk):
        r = pl.ds(pl.multiple_of(q * piece + lo, 16), size)
        return gt.at[r, pl.ds(pl.multiple_of(((x + chunk) % 4) * 128, 128), 128)]

    def send_g(q, i, ref, target):
        go(ref, ref, s4.at[q, i], r4.at[q, i], "shard", target)

    def got_g(q, i, ref):
        got(ref, s4.at[q, i], r4.at[q, i])

    def z_peer(k):
        return (zh + k) % 4

    def step(i, q):
        half = piece // 2
        if i == 0:
            ring1(q, x_src(q), piece, half, xin, sx, rx, right, left)
        if i == 1:
            ring2(q, x_src(q), piece, half, xin, xtx, sx, rx, right, left)
        if i == 2:
            xc[q] = ring3(q, x_src(q), piece, half, xin, sx, rx).astype(bf)
            for k in (2, 1, 3):
                go(z_src(q)(k, 0, depth), zin.at[q, k - 1], sz.at[q, k], rz.at[q, k], "shard", z_peer(k) * 4 + x)
        if i == 3:
            for k in (1, 3, 2):
                got(zin.at[q, k - 1], sz.at[q, k], rz.at[q, k])
            total = plus(z_src(q)(0, 0, depth)[...], zin[q, 0], zin[q, 1], zin[q, 2])
            lanes = pl.ds(pl.multiple_of((x % 2) * 128, 128), 128)
            r = pl.ds(pl.multiple_of(block_owner(q, zh) * depth, 16), depth)
            is_out = (1 - x // 2).astype(jnp.float32)
            wanted = tgt_t[r, lanes].astype(jnp.float32) * is_out
            mine = g_block(q, zh * depth, depth, 0)
            mine[...] = (keep[0:1, lanes] * (total - wanted)).astype(bf)
            for k in (2, 1, 3):
                send_g(q, k, mine, z_peer(k) * 4 + x)
        if i == 4:
            for k in (1, 3, 2):
                got_g(q, k, g_block(q, z_peer(4 - k) * depth, depth, 0))
            send_g(q, 4, g_block(q, 0, piece, 0), right)
            send_g(q, 5, g_block(q, 0, piece, 0), left)
        if i == 5:
            got_g(q, 4, g_block(q, 0, piece, 3))
            send_g(q, 6, g_block(q, 0, half, 3), right)
            got_g(q, 5, g_block(q, 0, piece, 1))
            send_g(q, 7, g_block(q, half, half, 1), left)
        if i == 6:
            got_g(q, 6, g_block(q, 0, half, 2))
            got_g(q, 7, g_block(q, half, half, 2))

    def back_piece(q):
        def chunk(n, _):
            c = pl.ds(pl.multiple_of(n * 384, 128), 384)
            term = dot_tn(gt[q * piece : (q + 1) * piece], full[3, q * piece : (q + 1) * piece, c])
            if q == 0:
                back[:, c] = term
            else:
                back[:, c] += term
            return 0

        lax.fori_loop(0, cols // 384, chunk, 0)

    out_piece(0)
    step(0, 0)
    wait(3, 17)
    start(3, 9)
    wait(3, 18)
    start(3, 10)
    start(3, 4, 5)
    out_piece(1)
    step(1, 0)
    step(0, 1)
    far(3)
    step(2, 0)
    step(1, 1)
    diagonal(3)
    out_piece(2)
    step(0, 2)
    last(3)
    step(2, 1)
    out_piece(3)
    step(0, 3)
    step(3, 0)
    step(1, 2)
    step(3, 1)
    step(1, 3)
    step(2, 2)
    step(4, 0)
    step(4, 1)
    step(2, 3)
    step(3, 2)
    step(5, 0)
    step(3, 3)
    step(5, 1)
    step(6, 0)
    back_piece(0)
    step(4, 2)
    step(6, 1)
    back_piece(1)
    step(4, 3)
    step(5, 2)
    step(5, 3)
    step(6, 2)
    back_piece(2)
    step(6, 3)
    back_piece(3)

    loads[3].wait()
    got(tok_t2, ms.at[1], mr.at[1])

    def pc(q):
        return pl.ds(q * part, part)

    def chip(dy, dz):
        return at(dy, dz, 0) // 2

    def c_block(dy, dz, q, lo=0, size=depth):
        return cp.at[pl.ds(pl.multiple_of(chip(dy, dz) * depth + lo, 16), size), pc(q)]

    def make(q, *which):
        for dy, dz in which:
            r = pl.ds(pl.multiple_of(at(dy, dz, 0) * depth, 16), depth)
            total = dot_nn(tok_t[r], tgg[:, pc(q)]) + dot_nn(tok_t2[r], tgg2[:, pc(q)])
            c_block(dy, dz, q)[...] = (total * inv_root).astype(bf)

    def box(slot, q, lo=0, size=depth):
        return cin.at[slot, pl.ds(lo, size), pc(q)]

    def send_c(src, dst, k, q, target):
        go(src, dst, cs.at[q, k], cr.at[q, k], "dp", target)

    def got_c(ref, k, q):
        got(ref, cs.at[q, k], cr.at[q, k])

    rest = depth - cut

    def reduce_step(i, q):
        if i == 0:
            got(tgg2.at[:, pc(q)], ms.at[2 + q], mr.at[2 + q])
            make(q, (2, 1), (1, 1), (-1, 1))
            send_c(c_block(2, 1, q), box(0, q), 0, q, zed)
            send_c(c_block(1, 1, q), box(1, q), 1, q, up)
            send_c(c_block(-1, 1, q), box(2, q), 2, q, down)
            make(q, (2, 0), (0, 1), (1, 0), (-1, 0), (0, 0))
        if i == 1:
            got_c(box(0, q), 0, q)
            cout[0, :, pc(q)] = plus(c_block(2, 0, q)[...], box(0, q)[...]).astype(bf)
            send_c(cout.at[0, pl.ds(0, cut), pc(q)], box(3, q, 0, cut), 3, q, up)
            send_c(cout.at[0, pl.ds(cut, rest), pc(q)], box(3, q, cut, rest), 4, q, down)
            got_c(box(1, q), 1, q)
            got_c(box(2, q), 2, q)
            cout[1, :, pc(q)] = plus(c_block(0, 1, q)[...], box(1, q)[...], box(2, q)[...]).astype(bf)
            send_c(cout.at[1, :, pc(q)], box(4, q), 5, q, zed)
        if i == 2:
            got_c(box(3, q, 0, cut), 3, q)
            cout[2, :cut, pc(q)] = plus(c_block(1, 0, q, 0, cut)[...], box(3, q, 0, cut)[...]).astype(bf)
            cout[2, cut:, pc(q)] = c_block(1, 0, q, cut, rest)[...]
            send_c(cout.at[2, :, pc(q)], box(5, q), 6, q, up)
            got_c(box(3, q, cut, rest), 4, q)
            cout[3, cut:, pc(q)] = plus(c_block(-1, 0, q, cut, rest)[...], box(3, q, cut, rest)[...]).astype(bf)
            cout[3, :cut, pc(q)] = c_block(-1, 0, q, 0, cut)[...]
            send_c(cout.at[3, :, pc(q)], box(6, q), 7, q, down)
        if i == 3:
            got_c(box(4, q), 5, q)
            got_c(box(5, q), 6, q)
            got_c(box(6, q), 7, q)
            total = plus(c_block(0, 0, q)[...], box(4, q)[...], box(5, q)[...], box(6, q)[...])
            own = full[2, pl.ds(pl.multiple_of(me * depth, 16), depth), pc(q)]
            o_ref[:, pc(q)] = (
                grad[:, pc(q)].astype(jnp.float32)
                + (1.0 - damping) * own.astype(jnp.float32)
                - step_size * total
            ).astype(bf)

    for q in range(PARTS):

        def combine(i, _):
            r = pl.ds(pl.multiple_of(i * 32, 16), 32)
            r2 = pl.ds(pl.multiple_of(tok_rows + i * 32, 16), 32)
            tgg[r, pc(q)] = (acc[0, r, pc(q)] * back[r2, pc(q)] + acc[1, r, pc(q)] * back[r, pc(q)]).astype(bf)
            return 0

        lax.fori_loop(0, tok_rows // 32, combine, 0)
        go(tgg.at[:, pc(q)], tgg2.at[:, pc(q)], ms.at[2 + q], mr.at[2 + q], "dp", sib)
    for q in range(PARTS):
        reduce_step(0, q)
    for q in range(PARTS):
        reduce_step(1, q)
    for q in range(PARTS):
        reduce_step(2, q)
    for q in range(PARTS):
        reduce_step(3, q)
    for copy in sent:
        copy.wait_send()


def per_device(tokens, target, segments, gate_weight, up_weight, down_weight, vector, gradient):
    tok_rows, width = tokens.shape
    depth, cols = gate_weight.shape
    bf, f32 = jnp.bfloat16, jnp.float32
    piece = 4 * depth
    cut = (depth // 32 + 1) * 16
    vm, dma = pltpu.VMEM, pltpu.SemaphoreType.DMA
    anywhere = pl.BlockSpec(memory_space=pltpu.HBM)
    scratch = [
        vm((4, width, cols), bf),
        vm((tok_rows, width), bf),
        vm((tok_rows, width), bf),
        vm((4, tok_rows, piece), bf),
        vm((width, tok_rows), bf),
        vm((width, tok_rows), bf),
        vm((width, tok_rows), bf),
        vm((1, tok_rows), jnp.int32),
        vm((1, tok_rows), jnp.int32),
        vm((8, tok_rows), f32),
        vm((3, tok_rows, cols), f32),
        vm((2 * tok_rows, cols), bf),
        vm((width, 2 * tok_rows), bf),
        vm((2 * tok_rows, cols), f32),
        vm((width, 2 * tok_rows), bf),
        vm((4, 3, piece, 128), bf),
        vm((4, piece, 128), bf),
        vm((4, piece, 128), bf),
        vm((4, 3, depth, 128), bf),
        vm((tok_rows, cols), bf),
        vm((tok_rows, cols), bf),
        vm((8 * depth, cols), bf),
        vm((7, depth, cols), bf),
        vm((4, depth, cols), bf),
        vm((depth, cols), bf),
        dma((4, GATHER_COPIES)),
        dma((4, GATHER_COPIES)),
        dma((4, 6)),
        dma((4, 6)),
        dma((4, 6)),
        dma((4, 6)),
        dma((4, 8)),
        dma((4, 8)),
        dma((PARTS, 8)),
        dma((PARTS, 8)),
        dma((2 + PARTS,)),
        dma((2 + PARTS,)),
        dma((8,)),
    ]
    return pl.pallas_call(
        functools.partial(step_kernel, (tok_rows, width, depth, cols)),
        out_shape=jax.ShapeDtypeStruct((depth, cols), bf),
        in_specs=[anywhere] * 8,
        out_specs=pl.BlockSpec(memory_space=pltpu.VMEM),
        scratch_shapes=scratch,
        compiler_params=pltpu.CompilerParams(
            collective_id=1, has_side_effects=True, vmem_limit_bytes=56 * 2**20
        ),
    )(tokens, target, segments[None], gate_weight, up_weight, vector, down_weight, gradient)


def solution(mesh):
    return jax.shard_map(
        per_device,
        mesh=mesh,
        in_specs=(
            P("dp", None),
            P("dp", None),
            P("dp"),
            P("dp", "shard"),
            P("dp", "shard"),
            P("dp", "shard"),
            P("dp", "shard"),
            P("dp", "shard"),
        ),
        out_specs=P("dp", "shard"),
        check_vma=False,
    )
```

```python
import functools

import jax
import jax.numpy as jnp
from jax import lax
from jax.experimental import pallas as pl
from jax.experimental.pallas import tpu as pltpu
from jax.sharding import PartitionSpec as P

MESH = pl.DeviceIdType.MESH
coeff_k = 0.7978845608028654
coeff_c = 0.044715
damping = 0.01
step_size = 0.8


def gelu_parts(pre_act):
    inner_arg = coeff_k * (pre_act + coeff_c * pre_act * pre_act * pre_act)
    tanh_value = jnp.tanh(inner_arg)
    slope_term = coeff_k * (1.0 + 3.0 * coeff_c * pre_act * pre_act)
    curve_term = 6.0 * coeff_k * coeff_c * pre_act
    sech_square = 1.0 - tanh_value * tanh_value
    gelu_value = 0.5 * pre_act * (1.0 + tanh_value)
    gelu_slope = 0.5 * (1.0 + tanh_value) + 0.5 * pre_act * sech_square * slope_term
    gelu_curve = sech_square * (
        slope_term + 0.5 * pre_act * (curve_term - 2.0 * tanh_value * slope_term * slope_term)
    )
    return (gelu_value, gelu_slope, gelu_curve)


def remote(src, dst, send_sem, recv_sem, axis, index):
    return pltpu.make_async_remote_copy(
        src_ref=src,
        dst_ref=dst,
        send_sem=send_sem,
        recv_sem=recv_sem,
        device_id={axis: index},
        device_id_type=MESH,
    )


GATHER_COPIES = 19
PARTS = 3


def plus(a, *more):
    total = a.astype(jnp.float32)
    for b in more:
        total = total + b.astype(jnp.float32)
    return total


def dot_nn(a, b):
    return jnp.dot(a, b, preferred_element_type=jnp.float32)


def dot_nt(a, b):
    return lax.dot_general(a, b, (((1,), (1,)), ((), ())), preferred_element_type=jnp.float32)


def dot_tn(a, b):
    return lax.dot_general(a, b, (((0,), (0,)), ((), ())), preferred_element_type=jnp.float32)


def step_kernel(
    dims, tok_hbm, tgt_hbm, seg_hbm, gate_hbm, up_hbm, vec_hbm, down_hbm, grad_hbm, o_ref,
    half, full, tok, tgt, tok4, tokp, tok_t, tok_t2, tgt_t, seg, seg_prev, keep, acc, accp, resb, resr, fac, stacked, p, back, gt,
    xin, xtx, xc, zin, tgg, tgg2, cp, cin, cout, grad, vec,
    gs, gr, sx, rx, sz, rz, s4, r4, cs, cr, ms, mr, ts, tr, ls,
):
    tok_rows, width, depth, cols = dims
    bf = jnp.bfloat16
    d, sh = lax.axis_index("dp"), lax.axis_index("shard")
    y, zl, core = d // 4, (d // 2) % 2, d % 2
    x, zh = sh % 4, sh // 4
    piece = 4 * depth
    cut = (depth // 32 + 1) * 16
    wide = -(-cols // 256) * 128
    rem = cols - wide
    part = cols // PARTS
    inv_root = float(width) ** (-0.5)

    def at(dy, dz, dc):
        return ((y + dy) % 4) * 4 + ((zl + dz) % 2) * 2 + (core + dc) % 2

    sib, up, down, zed = at(0, 0, 1), at(1, 0, 0), at(-1, 0, 0), at(0, 1, 0)
    right, left = zh * 4 + (x + 1) % 4, zh * 4 + (x + 3) % 4
    above, below = ((zh + 1) % 4) * 4 + x, ((zh + 3) % 4) * 4 + x
    across = ((zh + 2) % 4) * 4 + x
    after, before = (d + 1) % 16, (d + 15) % 16
    barrier = pltpu.get_barrier_semaphore()
    for axis, targets in (("dp", (sib, up, down, zed, after, before)), ("shard", (right, left, above, below, across))):
        for t in targets:
            pl.semaphore_signal(barrier, inc=1, device_id={axis: t}, device_id_type=MESH)

    loads = [
        pltpu.make_async_copy(src, dst, ls.at[i])
        for i, (src, dst) in enumerate(((tok_hbm, tok), (tgt_hbm, tgt), (seg_hbm, seg), (grad_hbm, grad), (vec_hbm, vec)))
    ]
    for copy in loads:
        copy.start()
    pl.semaphore_wait(barrier, 11)

    sent = []

    def go(src, dst, s, r, axis, target):
        copy = remote(src, dst, s, r, axis, target)
        copy.start()
        sent.append(copy)

    def got(ref, s, r):
        remote(ref, ref, s, r, "dp", sib).wait_recv()

    def place(dy, dz, dc):
        return {0: 2 * dz, -1: 4 + 4 * dz, 1: 6 + 4 * dz, 2: 12 + 2 * dz}[dy] + dc

    extent = {"w": (0, depth), "a": (0, cut), "b": (cut, depth - cut)}

    def rows(w, rel, which):
        lo, size = extent[which]
        base = place(*rel) if w == 3 else at(*rel)
        r = pl.ds(pl.multiple_of(base * depth + lo, 16), size)
        return full.at[r] if w == 3 else half.at[w, r]

    def own_part(w, which, z_of):
        lo, size = extent[which]
        if w == 3:
            return ins[w].at[pl.ds(lo, size)]
        return ins[w].at[pl.ds(lo, size), pl.ds(pl.multiple_of(z_of * rem, 128), wide)]

    me = at(0, 0, 0)
    table = [
        ((0, 0, 0), "w", sib, (0, 0, 1)),
        ((0, 0, 0), "w", up, (-1, 0, 0)),
        ((0, 0, 0), "w", down, (1, 0, 0)),
        ((0, 0, 0), "w", zed, (0, 1, 0)),
        ((0, 1, 0), "w", up, (-1, 1, 0)),
        ((0, 1, 0), "w", down, (1, 1, 0)),
        ((0, 1, 0), "w", sib, (0, 1, 1)),
        ((-1, 0, 0), "a", up, (2, 0, 0)),
        ((1, 0, 0), "b", down, (2, 0, 0)),
        ((-1, 0, 0), "w", sib, (-1, 0, 1)),
        ((1, 0, 0), "w", sib, (1, 0, 1)),
        ((-1, 1, 0), "w", sib, (-1, 1, 1)),
        ((1, 1, 0), "w", sib, (1, 1, 1)),
        ((2, 0, 0), "a", zed, (2, 1, 0)),
        ((2, 0, 0), "b", zed, (2, 1, 0)),
        ((2, 0, 0), "w", sib, (2, 0, 1)),
        ((2, 1, 0), "w", sib, (2, 1, 1)),
    ]
    special_down = {
        1: ((0, 0, 0), "a", up, (-1, 0, 0)),
        2: ((0, 0, 0), "b", down, (1, 0, 0)),
        17: ((0, 0, 0), "b", up, (-1, 0, 0)),
        18: ((0, 0, 0), "a", down, (1, 0, 0)),
    }
    ins = (gate_hbm, up_hbm, vec_hbm, down_hbm)

    special_half = {
        13: ((-1, 1, 0), "a", up, (2, 1, 0)),
        14: ((1, 1, 0), "b", down, (2, 1, 0)),
    }

    def entry(w, k):
        special = special_down if w == 3 else special_half
        return special[k] if k in special else table[k]

    def start(w, *numbers):
        for k in numbers:
            mine, which, target, theirs = entry(w, k)
            src = rows(w, mine, which)
            if mine == (0, 0, 0):
                src = own_part(w, which, (zl + (k == 3)) % 2)
            dst = rows(w, theirs if w == 3 else mine, which)
            go(src, dst, gs.at[w, k], gr.at[w, k], "dp", target)

    def wait(w, *numbers):
        for k in numbers:
            _, which, _, came = entry(w, k)
            got(rows(w, came, which), gs.at[w, k], gr.at[w, k])

    own_copies = [pltpu.make_async_copy(own_part(w, "w", zl), rows(w, (0, 0, 0), "w"), ls.at[5 + w]) for w in range(4)]

    late = {0: (0, 6), -1: (9, 11), 1: (10, 12), 2: (15, 16)}

    def piece_of(rel):
        return (y + rel) % 4

    def piece_rows(rel):
        return pl.ds(pl.multiple_of(piece_of(rel) * piece, 16), piece)

    came_in = set()

    def settle(w, rel):
        if (w, rel) in came_in:
            return
        came_in.add((w, rel))
        wait(w, *late[rel])
        if rel == 0:
            own_copies[w].wait()

    def use(w, rel):
        settle(w, rel)
        for c in (slice(0, 384), slice(384, wide)):
            term = dot_nn(tok4[piece_of(rel)], half[w, piece_rows(rel), c])
            if rel == 0:
                acc[w, :, c] = term
            else:
                acc[w, :, c] += term

    def use_for_partner(w, rel):
        settle(w, rel)

        def chunk(n, _):
            c = pl.ds(pl.multiple_of(n * (rem // 2), 128), rem // 2)
            c2 = pl.ds(pl.multiple_of(zl * (wide - rem) + n * (rem // 2), 128), rem // 2)
            term = dot_nn(tokp[piece_of(rel)], half[w, piece_rows(rel), c2])
            if rel == 0:
                accp[w, :, c] = term
            else:
                accp[w, :, c] += term
            if rel == 2:
                resb[w, :, c] = accp[w, :, c].astype(bf)
            return 0

        lax.fori_loop(0, 2, chunk, 0)
        if rel == 2:
            go(resb.at[w], resr.at[w], ts.at[5 + w], tr.at[5 + w], "dp", zed)

    start(0, 1, 2, 3, 0)
    own_copies[0].start()
    start(1, 1, 2, 3, 0)
    own_copies[1].start()
    go(seg_hbm, seg_prev, ms.at[0], mr.at[0], "dp", after)

    loads[0].wait()
    for r in range(4):
        tok4[r] = tok[:, r * piece : (r + 1) * piece]
    go(tok4.at[x], tokp.at[x], ts.at[0], tr.at[0], "dp", zed)
    start(2, 3, 0)
    own_copies[2].start()
    start(3, 3, 0)
    own_copies[3].start()

    def turn(src, dst):
        def body(j, _):
            c = pl.ds(pl.multiple_of(j * 128, 128), 128)
            dst[c, :] = src[:, c].astype(jnp.float32).T.astype(bf)
            return 0

        lax.fori_loop(0, width // 128, body, 0)

    turn(tok, tok_t)
    go(tok_t, tok_t2, ms.at[1], mr.at[1], "dp", sib)

    def tokens_start():
        got(tokp.at[x], ts.at[0], tr.at[0])
        go(tokp.at[x], tokp.at[x], ts.at[1], tr.at[1], "shard", right)
        go(tokp.at[x], tokp.at[x], ts.at[2], tr.at[2], "shard", left)

    def tokens_relay():
        h = tok_rows // 2
        got(tokp.at[(x + 3) % 4], ts.at[1], tr.at[1])
        ref = tokp.at[(x + 3) % 4, pl.ds(0, h)]
        go(ref, ref, ts.at[3], tr.at[3], "shard", right)
        got(tokp.at[(x + 1) % 4], ts.at[2], tr.at[2])
        ref = tokp.at[(x + 1) % 4, pl.ds(h, h)]
        go(ref, ref, ts.at[4], tr.at[4], "shard", left)

    def tokens_end():
        h = tok_rows // 2
        got(tokp.at[(x + 2) % 4, pl.ds(0, h)], ts.at[3], tr.at[3])
        got(tokp.at[(x + 2) % 4, pl.ds(h, h)], ts.at[4], tr.at[4])

    def near_z(w):
        wait(w, 3)
        start(w, 4, 5, 6)

    def near(w):
        wait(w, 1)
        start(w, 7, 9)
        wait(w, 2)
        start(w, 8, 10)

    def diagonal(w):
        wait(w, 4)
        start(w, 11)
        wait(w, 5)
        start(w, 12)

    def round_z(w):
        wait(w, 4)
        start(w, 13, 11)
        wait(w, 5)
        start(w, 14, 12)

    def far(w):
        wait(w, 7, 8)
        start(w, 15)

    def last(w):
        wait(w, 13, 14)
        start(w, 16)

    near_z(0)
    near(0)
    start(2, 1, 2)
    loads[1].wait()
    turn(tgt, tgt_t)
    round_z(0)
    near_z(1)
    near(1)
    tokens_start()
    near_z(2)
    use(0, 0)
    far(0)
    use(0, -1)
    use(0, 1)
    last(0)
    round_z(1)
    near(2)
    tokens_relay()
    use(0, 2)
    use(1, 0)
    round_z(2)
    start(3, 1, 2, 17, 18)
    far(1)
    tokens_end()
    use_for_partner(0, 0)
    use_for_partner(0, -1)
    use_for_partner(0, 1)
    use_for_partner(0, 2)
    last(1)
    far(2)
    use_for_partner(1, 0)
    use_for_partner(1, -1)
    use_for_partner(1, 1)
    use_for_partner(1, 2)
    last(2)
    use_for_partner(2, 0)
    use_for_partner(2, -1)
    use_for_partner(2, 1)
    use_for_partner(2, 2)
    use(1, -1)
    use(1, 1)
    use(1, 2)
    use(2, 0)
    use(2, -1)
    use(2, 1)
    use(2, 2)
    wait(3, 3)
    start(3, 6)

    loads[2].wait()
    got(seg_prev, ms.at[0], mr.at[0])
    lane = lax.broadcasted_iota(jnp.int32, (8, tok_rows), 1)
    here = jnp.broadcast_to(seg[...], (8, tok_rows))
    previous = jnp.where(
        lane == 0,
        pltpu.roll(jnp.broadcast_to(seg_prev[...], (8, tok_rows)), 1, 1),
        pltpu.roll(here, 1, 1),
    )
    first = (lane + d) == 0
    keep[...] = jnp.where(first, 0.0, jnp.where(here == previous, 1.0, 0.0))

    def pointwise(c, parts_of):
        def body(i, _):
            r = pl.ds(pl.multiple_of(i * 16, 16), 16)
            r2 = pl.ds(pl.multiple_of(tok_rows + i * 16, 16), 16)
            pre_gate, up_act, tangent_raw = parts_of(r)
            value, slope, curve = gelu_parts(pre_gate)
            tangent = tangent_raw * inv_root
            stacked[r, c] = (value * up_act).astype(bf)
            stacked[r2, c] = (slope * tangent * up_act).astype(bf)
            fac[0, r, c] = up_act * slope
            fac[1, r, c] = up_act * curve * tangent
            return 0

        lax.fori_loop(0, tok_rows // 16, body, 0)

    pointwise(
        pl.ds(pl.multiple_of(zl * rem, 128), wide), lambda r: [acc[w, r] for w in range(3)]
    )
    wait(3, 1)
    start(3, 7)
    wait(3, 2)
    start(3, 8)
    start(3, 4, 5)
    wait(3, 17)
    start(3, 9)
    wait(3, 18)
    start(3, 10)
    for w in range(3):
        got(resr.at[w], ts.at[5 + w], tr.at[5 + w])
    pointwise(
        pl.ds(pl.multiple_of((1 - zl) * wide, 128), rem),
        lambda r: [resr[w, r].astype(jnp.float32) for w in range(3)],
    )

    def out_piece(q):
        if q == 0:
            own_copies[3].wait()
            wait(3, 0, 6)
        else:
            wait(3, *{1: (9, 10), 2: (11, 12), 3: (15, 16)}[q])

        def chunk(n, _):
            r = pl.ds(pl.multiple_of(q * piece + n * 2 * depth, 16), 2 * depth)
            p[r] = dot_nt(full[r], stacked[...]).astype(bf)
            return 0

        lax.fori_loop(0, 2, chunk, 0)

    def x_src(q):
        def src(chunk, lo, size):
            return p.at[pl.ds(q * piece + lo, size), pl.ds(pl.multiple_of(((x + chunk) % 4) * 128, 128), 128)]

        return src

    def z_src(q):
        def src(chunk, lo, size):
            return xc.at[q, pl.ds(pl.multiple_of(((zh + chunk) % 4) * depth + lo, 16), size)]

        return src

    def block_owner(q, j):
        hi, lo = j // 2, j % 2
        if q == 0:
            return at(0, hi, lo)
        if q == 3:
            return at(2, hi, lo)
        return at(2 * hi - 1, q - 1, lo)

    def ring1(q, src, size, mid, inbox, s, r, plus1, minus1):
        rest = size - mid
        for i, (dst, frm, lo, n, target) in enumerate((
            (0, 2, mid, rest, plus1), (0, 2, 0, mid, minus1), (1, 1, 0, mid, plus1), (2, 3, mid, rest, minus1),
        )):
            go(src(frm, lo, n), inbox.at[q, dst, pl.ds(lo, n)], s.at[q, i], r.at[q, i], "shard", target)

    def ring2(q, src, size, mid, inbox, out, s, r, plus1, minus1):
        rest = size - mid
        for i, (dst, frm, lo, n, target) in enumerate(((1, 1, mid, rest, plus1), (2, 3, 0, mid, minus1))):
            came = inbox.at[q, 0, pl.ds(lo, n)]
            got(came, s.at[q, i], r.at[q, i])
            out[q, lo : lo + n] = plus(src(frm, lo, n)[...], came[...]).astype(bf)
            go(out.at[q, pl.ds(lo, n)], inbox.at[q, dst, pl.ds(lo, n)], s.at[q, 4 + i], r.at[q, 4 + i], "shard", target)

    def ring3(q, src, size, mid, inbox, s, r):
        got(inbox.at[q, 1, pl.ds(0, mid)], s.at[q, 2], r.at[q, 2])
        got(inbox.at[q, 2, pl.ds(mid, size - mid)], s.at[q, 3], r.at[q, 3])
        got(inbox.at[q, 1, pl.ds(mid, size - mid)], s.at[q, 4], r.at[q, 4])
        got(inbox.at[q, 2, pl.ds(0, mid)], s.at[q, 5], r.at[q, 5])
        return plus(src(0, 0, size)[...], inbox[q, 1], inbox[q, 2])

    def g_block(q, lo, size, chunk):
        r = pl.ds(pl.multiple_of(q * piece + lo, 16), size)
        return gt.at[r, pl.ds(pl.multiple_of(((x + chunk) % 4) * 128, 128), 128)]

    def send_g(q, i, ref, target):
        go(ref, ref, s4.at[q, i], r4.at[q, i], "shard", target)

    def got_g(q, i, ref):
        got(ref, s4.at[q, i], r4.at[q, i])

    def z_peer(k):
        return (zh + k) % 4

    def step(i, q):
        half = piece // 2
        if i == 0:
            ring1(q, x_src(q), piece, half, xin, sx, rx, right, left)
        if i == 1:
            ring2(q, x_src(q), piece, half, xin, xtx, sx, rx, right, left)
        if i == 2:
            xc[q] = ring3(q, x_src(q), piece, half, xin, sx, rx).astype(bf)
            for k in (2, 1, 3):
                go(z_src(q)(k, 0, depth), zin.at[q, k - 1], sz.at[q, k], rz.at[q, k], "shard", z_peer(k) * 4 + x)
        if i == 3:
            for k in (1, 3, 2):
                got(zin.at[q, k - 1], sz.at[q, k], rz.at[q, k])
            total = plus(z_src(q)(0, 0, depth)[...], zin[q, 0], zin[q, 1], zin[q, 2])
            lanes = pl.ds(pl.multiple_of((x % 2) * 128, 128), 128)
            r = pl.ds(pl.multiple_of(block_owner(q, zh) * depth, 16), depth)
            is_out = (1 - x // 2).astype(jnp.float32)
            wanted = tgt_t[r, lanes].astype(jnp.float32) * is_out
            mine = g_block(q, zh * depth, depth, 0)
            mine[...] = (keep[0:1, lanes] * (total - wanted)).astype(bf)
            for k in (2, 1, 3):
                send_g(q, k, mine, z_peer(k) * 4 + x)
        if i == 4:
            for k in (1, 3, 2):
                got_g(q, k, g_block(q, z_peer(4 - k) * depth, depth, 0))
            send_g(q, 4, g_block(q, 0, piece, 0), right)
            send_g(q, 5, g_block(q, 0, piece, 0), left)
        if i == 5:
            got_g(q, 4, g_block(q, 0, piece, 3))
            send_g(q, 6, g_block(q, 0, half, 3), right)
            got_g(q, 5, g_block(q, 0, piece, 1))
            send_g(q, 7, g_block(q, half, half, 1), left)
        if i == 6:
            got_g(q, 6, g_block(q, 0, half, 2))
            got_g(q, 7, g_block(q, half, half, 2))

    def back_piece(q):
        def chunk(n, _):
            c = pl.ds(pl.multiple_of(n * 384, 128), 384)
            term = dot_tn(gt[q * piece : (q + 1) * piece], full[q * piece : (q + 1) * piece, c])
            if q == 0:
                back[:, c] = term
            else:
                back[:, c] += term
            return 0

        lax.fori_loop(0, cols // 384, chunk, 0)

    out_piece(0)
    step(0, 0)
    out_piece(1)
    step(0, 1)
    wait(3, 7)
    start(3, 13)
    wait(3, 8)
    start(3, 14, 15)
    step(1, 0)
    step(2, 0)
    diagonal(3)
    step(1, 1)
    out_piece(2)
    step(0, 2)
    step(2, 1)
    last(3)
    step(3, 0)
    out_piece(3)
    step(0, 3)
    step(1, 2)
    step(3, 1)
    step(1, 3)
    step(2, 2)
    step(4, 0)
    step(4, 1)
    step(2, 3)
    step(3, 2)
    step(5, 0)
    step(3, 3)
    step(5, 1)
    step(6, 0)
    step(4, 2)
    back_piece(0)
    step(6, 1)
    step(4, 3)
    back_piece(1)
    step(5, 2)
    step(5, 3)
    step(6, 2)
    back_piece(2)
    step(6, 3)
    back_piece(3)

    loads[3].wait()
    loads[4].wait()
    got(tok_t2, ms.at[1], mr.at[1])

    def pc(q):
        return pl.ds(q * part, part)

    def chip(dy, dz):
        return at(dy, dz, 0) // 2

    def c_block(dy, dz, q, lo=0, size=depth):
        return cp.at[pl.ds(pl.multiple_of(chip(dy, dz) * depth + lo, 16), size), pc(q)]

    def make(q, *which):
        for dy, dz in which:
            r = pl.ds(pl.multiple_of(at(dy, dz, 0) * depth, 16), depth)
            total = dot_nn(tok_t[r], tgg[:, pc(q)]) + dot_nn(tok_t2[r], tgg2[:, pc(q)])
            c_block(dy, dz, q)[...] = (total * inv_root).astype(bf)

    def box(slot, q, lo=0, size=depth):
        return cin.at[slot, pl.ds(lo, size), pc(q)]

    def send_c(src, dst, k, q, target):
        go(src, dst, cs.at[q, k], cr.at[q, k], "dp", target)

    def got_c(ref, k, q):
        got(ref, cs.at[q, k], cr.at[q, k])

    rest = depth - cut

    def reduce_step(i, q):
        if i == 0:
            got(tgg2.at[:, pc(q)], ms.at[2 + q], mr.at[2 + q])
            make(q, (2, 1), (1, 1), (-1, 1))
            send_c(c_block(2, 1, q), box(0, q), 0, q, zed)
            send_c(c_block(1, 1, q), box(1, q), 1, q, up)
            send_c(c_block(-1, 1, q), box(2, q), 2, q, down)
            make(q, (2, 0), (0, 1), (1, 0), (-1, 0), (0, 0))
        if i == 1:
            got_c(box(0, q), 0, q)
            cout[0, :, pc(q)] = plus(c_block(2, 0, q)[...], box(0, q)[...]).astype(bf)
            send_c(cout.at[0, pl.ds(0, cut), pc(q)], box(3, q, 0, cut), 3, q, up)
            send_c(cout.at[0, pl.ds(cut, rest), pc(q)], box(3, q, cut, rest), 4, q, down)
            got_c(box(1, q), 1, q)
            got_c(box(2, q), 2, q)
            cout[1, :, pc(q)] = plus(c_block(0, 1, q)[...], box(1, q)[...], box(2, q)[...]).astype(bf)
            send_c(cout.at[1, :, pc(q)], box(4, q), 5, q, zed)
        if i == 2:
            got_c(box(3, q, 0, cut), 3, q)
            cout[2, :cut, pc(q)] = plus(c_block(1, 0, q, 0, cut)[...], box(3, q, 0, cut)[...]).astype(bf)
            cout[2, cut:, pc(q)] = c_block(1, 0, q, cut, rest)[...]
            send_c(cout.at[2, :, pc(q)], box(5, q), 6, q, up)
            got_c(box(3, q, cut, rest), 4, q)
            cout[3, cut:, pc(q)] = plus(c_block(-1, 0, q, cut, rest)[...], box(3, q, cut, rest)[...]).astype(bf)
            cout[3, :cut, pc(q)] = c_block(-1, 0, q, 0, cut)[...]
            send_c(cout.at[3, :, pc(q)], box(6, q), 7, q, down)
        if i == 3:
            got_c(box(4, q), 5, q)
            got_c(box(5, q), 6, q)
            got_c(box(6, q), 7, q)
            total = plus(c_block(0, 0, q)[...], box(4, q)[...], box(5, q)[...], box(6, q)[...])
            own = vec[:, pc(q)]
            o_ref[:, pc(q)] = (
                grad[:, pc(q)].astype(jnp.float32)
                + (1.0 - damping) * own.astype(jnp.float32)
                - step_size * total
            ).astype(bf)

    for q in range(PARTS):

        def combine(i, _):
            r = pl.ds(pl.multiple_of(i * 32, 16), 32)
            r2 = pl.ds(pl.multiple_of(tok_rows + i * 32, 16), 32)
            tgg[r, pc(q)] = (fac[0, r, pc(q)] * back[r2, pc(q)] + fac[1, r, pc(q)] * back[r, pc(q)]).astype(bf)
            return 0

        lax.fori_loop(0, tok_rows // 32, combine, 0)
        go(tgg.at[:, pc(q)], tgg2.at[:, pc(q)], ms.at[2 + q], mr.at[2 + q], "dp", sib)
    for q in range(PARTS):
        reduce_step(0, q)
    for q in range(PARTS):
        reduce_step(1, q)
    for q in range(PARTS):
        reduce_step(2, q)
    for q in range(PARTS):
        reduce_step(3, q)
    for copy in sent:
        copy.wait_send()


def per_device(tokens, target, segments, gate_weight, up_weight, down_weight, vector, gradient):
    tok_rows, width = tokens.shape
    depth, cols = gate_weight.shape
    bf, f32 = jnp.bfloat16, jnp.float32
    piece = 4 * depth
    cut = (depth // 32 + 1) * 16
    wide = -(-cols // 256) * 128
    vm, dma = pltpu.VMEM, pltpu.SemaphoreType.DMA
    anywhere = pl.BlockSpec(memory_space=pltpu.HBM)
    scratch = [
        vm((3, width, wide), bf),
        vm((width, cols), bf),
        vm((tok_rows, width), bf),
        vm((tok_rows, width), bf),
        vm((4, tok_rows, piece), bf),
        vm((4, tok_rows, piece), bf),
        vm((width, tok_rows), bf),
        vm((width, tok_rows), bf),
        vm((width, tok_rows), bf),
        vm((1, tok_rows), jnp.int32),
        vm((1, tok_rows), jnp.int32),
        vm((8, tok_rows), f32),
        vm((3, tok_rows, wide), f32),
        vm((3, tok_rows, cols - wide), f32),
        vm((3, tok_rows, cols - wide), bf),
        vm((3, tok_rows, cols - wide), bf),
        vm((2, tok_rows, cols), f32),
        vm((2 * tok_rows, cols), bf),
        vm((width, 2 * tok_rows), bf),
        vm((2 * tok_rows, cols), f32),
        vm((width, 2 * tok_rows), bf),
        vm((4, 3, piece, 128), bf),
        vm((4, piece, 128), bf),
        vm((4, piece, 128), bf),
        vm((4, 3, depth, 128), bf),
        vm((tok_rows, cols), bf),
        vm((tok_rows, cols), bf),
        vm((8 * depth, cols), bf),
        vm((7, depth, cols), bf),
        vm((4, depth, cols), bf),
        vm((depth, cols), bf),
        vm((depth, cols), bf),
        dma((4, GATHER_COPIES)),
        dma((4, GATHER_COPIES)),
        dma((4, 6)),
        dma((4, 6)),
        dma((4, 6)),
        dma((4, 6)),
        dma((4, 8)),
        dma((4, 8)),
        dma((PARTS, 8)),
        dma((PARTS, 8)),
        dma((2 + PARTS,)),
        dma((2 + PARTS,)),
        dma((8,)),
        dma((8,)),
        dma((9,)),
    ]
    return pl.pallas_call(
        functools.partial(step_kernel, (tok_rows, width, depth, cols)),
        out_shape=jax.ShapeDtypeStruct((depth, cols), bf),
        in_specs=[anywhere] * 8,
        out_specs=pl.BlockSpec(memory_space=pltpu.VMEM),
        scratch_shapes=scratch,
        compiler_params=pltpu.CompilerParams(
            collective_id=1, has_side_effects=True, vmem_limit_bytes=56 * 2**20
        ),
    )(tokens, target, segments[None], gate_weight, up_weight, vector, down_weight, gradient)


def solution(mesh):
    return jax.shard_map(
        per_device,
        mesh=mesh,
        in_specs=(
            P("dp", None),
            P("dp", None),
            P("dp"),
            P("dp", "shard"),
            P("dp", "shard"),
            P("dp", "shard"),
            P("dp", "shard"),
            P("dp", "shard"),
        ),
        out_specs=P("dp", "shard"),
        check_vma=False,
    )
```

```python
import functools

import jax
import jax.numpy as jnp
from jax import lax
from jax.experimental import pallas as pl
from jax.experimental.pallas import tpu as pltpu
from jax.sharding import PartitionSpec as P

MESH = pl.DeviceIdType.MESH
coeff_k = 0.7978845608028654
coeff_c = 0.044715
damping = 0.01
step_size = 0.8


def gelu_parts(pre_act):
    inner_arg = coeff_k * (pre_act + coeff_c * pre_act * pre_act * pre_act)
    tanh_value = jnp.tanh(inner_arg)
    slope_term = coeff_k * (1.0 + 3.0 * coeff_c * pre_act * pre_act)
    curve_term = 6.0 * coeff_k * coeff_c * pre_act
    sech_square = 1.0 - tanh_value * tanh_value
    gelu_value = 0.5 * pre_act * (1.0 + tanh_value)
    gelu_slope = 0.5 * (1.0 + tanh_value) + 0.5 * pre_act * sech_square * slope_term
    gelu_curve = sech_square * (
        slope_term + 0.5 * pre_act * (curve_term - 2.0 * tanh_value * slope_term * slope_term)
    )
    return (gelu_value, gelu_slope, gelu_curve)


def remote(src, dst, send_sem, recv_sem, axis, index):
    return pltpu.make_async_remote_copy(
        src_ref=src,
        dst_ref=dst,
        send_sem=send_sem,
        recv_sem=recv_sem,
        device_id={axis: index},
        device_id_type=MESH,
    )


GATHER_COPIES = 19
PARTS = 3
PIECES = ((0, 4), (4, 4), (8, 4), (12, 4), (16, 4), (20, 4), (24, 4), (28, 4), (32, 4), (36, 4), (40, 4), (44, 4))


def plus(a, *more):
    total = a.astype(jnp.float32)
    for b in more:
        total = total + b.astype(jnp.float32)
    return total


def dot_nn(a, b):
    return jnp.dot(a, b, preferred_element_type=jnp.float32)


def dot_nt(a, b):
    return lax.dot_general(a, b, (((1,), (1,)), ((), ())), preferred_element_type=jnp.float32)


def dot_tn(a, b):
    return lax.dot_general(a, b, (((0,), (0,)), ((), ())), preferred_element_type=jnp.float32)


def step_kernel(
    dims, tok_hbm, tgt_hbm, seg_hbm, gate_hbm, up_hbm, vec_hbm, down_hbm, grad_hbm, o_ref,
    half, full, tok, tgt, tok4, tokp, tok_t, tok_t2, tgt_t, seg, seg_prev, keep, acc, accp, resb, resr, fac, stacked, p, back, gt,
    xin, xtx, xc, zin, tgg, tgg2, cp, cin, cout, grad, vec,
    gs, gr, sx, rx, cs, cr, ms, mr, ts, tr, ls,
):
    tok_rows, width, depth, cols = dims
    bf = jnp.bfloat16
    d, sh = lax.axis_index("dp"), lax.axis_index("shard")
    y, zl, core = d // 4, (d // 2) % 2, d % 2
    x, zh = sh % 4, sh // 4
    piece = 4 * depth
    cut = (depth // 32 + 1) * 16
    wide = -(-cols // 256) * 128
    rem = cols - wide
    part = cols // PARTS
    inv_root = float(width) ** (-0.5)

    def at(dy, dz, dc):
        return ((y + dy) % 4) * 4 + ((zl + dz) % 2) * 2 + (core + dc) % 2

    sib, up, down, zed = at(0, 0, 1), at(1, 0, 0), at(-1, 0, 0), at(0, 1, 0)
    right, left = zh * 4 + (x + 1) % 4, zh * 4 + (x + 3) % 4
    above, below = ((zh + 1) % 4) * 4 + x, ((zh + 3) % 4) * 4 + x
    across = ((zh + 2) % 4) * 4 + x
    after, before = (d + 1) % 16, (d + 15) % 16
    barrier = pltpu.get_barrier_semaphore()
    for axis, targets in (("dp", (sib, up, down, zed, after, before)), ("shard", (right, left, above, below, across))):
        for t in targets:
            pl.semaphore_signal(barrier, inc=1, device_id={axis: t}, device_id_type=MESH)

    loads = [
        pltpu.make_async_copy(src, dst, ls.at[i])
        for i, (src, dst) in enumerate(((tok_hbm, tok), (tgt_hbm, tgt), (seg_hbm, seg), (grad_hbm, grad), (vec_hbm, vec)))
    ]
    for copy in loads:
        copy.start()
    pl.semaphore_wait(barrier, 11)

    sent = []

    def go(src, dst, s, r, axis, target, kept=True):
        copy = remote(src, dst, s, r, axis, target)
        copy.start()
        if kept:
            sent.append(copy)

    def got(ref, s, r):
        remote(ref, ref, s, r, "dp", sib).wait_recv()

    def place(dy, dz, dc):
        return {0: 2 * dz, -1: 4 + 4 * dz, 1: 6 + 4 * dz, 2: 12 + 2 * dz}[dy] + dc

    extent = {"w": (0, depth), "a": (0, cut), "b": (cut, depth - cut)}

    def rows(w, rel, which):
        lo, size = extent[which]
        base = place(*rel) if w == 3 else at(*rel)
        r = pl.ds(pl.multiple_of(base * depth + lo, 16), size)
        return full.at[r] if w == 3 else half.at[w, r]

    def own_part(w, which, z_of):
        lo, size = extent[which]
        if w == 3:
            return ins[w].at[pl.ds(lo, size)]
        return ins[w].at[pl.ds(lo, size), pl.ds(pl.multiple_of(z_of * rem, 128), wide)]

    me = at(0, 0, 0)
    table = [
        ((0, 0, 0), "w", sib, (0, 0, 1)),
        ((0, 0, 0), "w", up, (-1, 0, 0)),
        ((0, 0, 0), "w", down, (1, 0, 0)),
        ((0, 0, 0), "w", zed, (0, 1, 0)),
        ((0, 1, 0), "w", up, (-1, 1, 0)),
        ((0, 1, 0), "w", down, (1, 1, 0)),
        ((0, 1, 0), "w", sib, (0, 1, 1)),
        ((-1, 0, 0), "a", up, (2, 0, 0)),
        ((1, 0, 0), "b", down, (2, 0, 0)),
        ((-1, 0, 0), "w", sib, (-1, 0, 1)),
        ((1, 0, 0), "w", sib, (1, 0, 1)),
        ((-1, 1, 0), "w", sib, (-1, 1, 1)),
        ((1, 1, 0), "w", sib, (1, 1, 1)),
        ((2, 0, 0), "a", zed, (2, 1, 0)),
        ((2, 0, 0), "b", zed, (2, 1, 0)),
        ((2, 0, 0), "w", sib, (2, 0, 1)),
        ((2, 1, 0), "w", sib, (2, 1, 1)),
    ]
    special_down = {
        1: ((0, 0, 0), "a", up, (-1, 0, 0)),
        2: ((0, 0, 0), "b", down, (1, 0, 0)),
        17: ((0, 0, 0), "b", up, (-1, 0, 0)),
        18: ((0, 0, 0), "a", down, (1, 0, 0)),
    }
    ins = (gate_hbm, up_hbm, vec_hbm, down_hbm)

    special_half = {
        13: ((-1, 1, 0), "a", up, (2, 1, 0)),
        14: ((1, 1, 0), "b", down, (2, 1, 0)),
    }

    def entry(w, k):
        special = special_down if w == 3 else special_half
        return special[k] if k in special else table[k]

    def start(w, *numbers):
        for k in numbers:
            mine, which, target, theirs = entry(w, k)
            src = rows(w, mine, which)
            if mine == (0, 0, 0):
                src = own_part(w, which, (zl + (k == 3)) % 2)
            dst = rows(w, theirs if w == 3 else mine, which)
            go(src, dst, gs.at[w], gr.at[w, k], "dp", target, False)

    def wait(w, *numbers):
        for k in numbers:
            _, which, _, came = entry(w, k)
            got(rows(w, came, which), gs.at[w], gr.at[w, k])

    own_copies = [pltpu.make_async_copy(own_part(w, "w", zl), rows(w, (0, 0, 0), "w"), ls.at[5 + w]) for w in range(4)]

    late = {0: (0, 6), -1: (9, 11), 1: (10, 12), 2: (15, 16)}

    def piece_of(rel):
        return (y + rel) % 4

    def piece_rows(rel):
        return pl.ds(pl.multiple_of(piece_of(rel) * piece, 16), piece)

    came_in = set()

    def settle(w, rel):
        if (w, rel) in came_in:
            return
        came_in.add((w, rel))
        wait(w, *late[rel])
        if rel == 0:
            own_copies[w].wait()

    def use(w, rel):
        settle(w, rel)
        for c in (slice(0, 384), slice(384, wide)):
            term = dot_nn(tok4[piece_of(rel)], half[w, piece_rows(rel), c])
            if rel == 0:
                acc[w, :, c] = term
            else:
                acc[w, :, c] += term

    def use_for_partner(w, rel):
        settle(w, rel)

        def chunk(n, _):
            c = pl.ds(pl.multiple_of(n * (rem // 2), 128), rem // 2)
            c2 = pl.ds(pl.multiple_of(zl * (wide - rem) + n * (rem // 2), 128), rem // 2)
            term = dot_nn(tokp[piece_of(rel)], half[w, piece_rows(rel), c2])
            if rel == 0:
                accp[w, :, c] = term
            else:
                accp[w, :, c] += term
            if rel == 2:
                resb[w, :, c] = accp[w, :, c].astype(bf)
            return 0

        lax.fori_loop(0, 2, chunk, 0)
        if rel == 2:
            go(resb.at[w], resr.at[w], ts.at[5 + w], tr.at[5 + w], "dp", zed)

    start(0, 1, 2, 3, 0)
    own_copies[0].start()
    start(1, 1, 2, 0)
    own_copies[1].start()
    go(seg_hbm, seg_prev, ms.at[0], mr.at[0], "dp", after)

    loads[0].wait()
    for r in range(4):
        tok4[r] = tok[:, r * piece : (r + 1) * piece]
    go(tok4.at[x], tokp.at[x], ts.at[0], tr.at[0], "dp", zed)
    start(1, 3)
    start(2, 3, 0)
    own_copies[2].start()
    start(3, 3, 0)
    own_copies[3].start()

    def turn(src, dst):
        def body(j, _):
            c = pl.ds(pl.multiple_of(j * 128, 128), 128)
            dst[c, :] = src[:, c].astype(jnp.float32).T.astype(bf)
            return 0

        lax.fori_loop(0, width // 128, body, 0)

    turn(tok, tok_t)
    go(tok_t, tok_t2, ms.at[1], mr.at[1], "dp", sib)

    def tokens_start():
        got(tokp.at[x], ts.at[0], tr.at[0])
        go(tokp.at[x], tokp.at[x], ts.at[1], tr.at[1], "shard", right)
        go(tokp.at[x], tokp.at[x], ts.at[2], tr.at[2], "shard", left)

    def tokens_relay():
        h = tok_rows // 2
        got(tokp.at[(x + 3) % 4], ts.at[1], tr.at[1])
        ref = tokp.at[(x + 3) % 4, pl.ds(0, h)]
        go(ref, ref, ts.at[3], tr.at[3], "shard", right)
        got(tokp.at[(x + 1) % 4], ts.at[2], tr.at[2])
        ref = tokp.at[(x + 1) % 4, pl.ds(h, h)]
        go(ref, ref, ts.at[4], tr.at[4], "shard", left)

    def tokens_end():
        h = tok_rows // 2
        got(tokp.at[(x + 2) % 4, pl.ds(0, h)], ts.at[3], tr.at[3])
        got(tokp.at[(x + 2) % 4, pl.ds(h, h)], ts.at[4], tr.at[4])

    def near_z(w):
        wait(w, 3)
        start(w, 4, 5, 6)

    def near(w):
        wait(w, 1)
        start(w, 7, 9)
        wait(w, 2)
        start(w, 8, 10)

    def diagonal(w):
        wait(w, 4)
        start(w, 11)
        wait(w, 5)
        start(w, 12)

    def round_z(w):
        wait(w, 4)
        start(w, 13, 11)
        wait(w, 5)
        start(w, 14, 12)

    def far(w):
        wait(w, 7, 8)
        start(w, 15)

    def last(w):
        wait(w, 13, 14)
        start(w, 16)

    near_z(0)
    near(0)
    start(2, 1, 2)
    loads[1].wait()
    turn(tgt, tgt_t)
    tokens_start()
    round_z(0)
    near(1)
    near_z(1)
    use(0, 0)
    far(0)
    use(0, -1)
    use(0, 1)
    tokens_relay()
    round_z(1)
    near_z(2)
    last(0)
    near(2)
    use(1, 0)
    use(2, 0)
    use(1, -1)
    far(1)
    tokens_end()
    use_for_partner(0, 0)
    use_for_partner(0, -1)
    use_for_partner(0, 1)
    use_for_partner(0, 2)
    last(1)
    use_for_partner(1, 0)
    use_for_partner(1, -1)
    use_for_partner(1, 1)
    use_for_partner(1, 2)
    use_for_partner(2, 0)
    round_z(2)
    start(3, 1, 2, 17, 18)
    use(0, 2)
    use(1, 1)
    use(1, 2)
    far(2)
    use_for_partner(2, -1)
    use_for_partner(2, 1)
    last(2)
    use(2, -1)
    use(2, 1)
    use_for_partner(2, 2)
    use(2, 2)
    wait(3, 3)
    start(3, 6)
    wait(3, 1)
    start(3, 7)
    wait(3, 2)
    start(3, 8)
    start(3, 4, 5)

    loads[2].wait()
    got(seg_prev, ms.at[0], mr.at[0])
    lane = lax.broadcasted_iota(jnp.int32, (8, tok_rows), 1)
    here = jnp.broadcast_to(seg[...], (8, tok_rows))
    previous = jnp.where(
        lane == 0,
        pltpu.roll(jnp.broadcast_to(seg_prev[...], (8, tok_rows)), 1, 1),
        pltpu.roll(here, 1, 1),
    )
    first = (lane + d) == 0
    keep[...] = jnp.where(first, 0.0, jnp.where(here == previous, 1.0, 0.0))

    def pointwise(c, parts_of):
        def body(i, _):
            r = pl.ds(pl.multiple_of(i * 16, 16), 16)
            r2 = pl.ds(pl.multiple_of(tok_rows + i * 16, 16), 16)
            pre_gate, up_act, tangent_raw = parts_of(r)
            value, slope, curve = gelu_parts(pre_gate)
            tangent = tangent_raw * inv_root
            stacked[r, c] = (value * up_act).astype(bf)
            stacked[r2, c] = (slope * tangent * up_act).astype(bf)
            fac[0, r, c] = up_act * slope
            fac[1, r, c] = up_act * curve * tangent
            return 0

        lax.fori_loop(0, tok_rows // 16, body, 0)

    pointwise(
        pl.ds(pl.multiple_of(zl * rem, 128), wide), lambda r: [acc[w, r] for w in range(3)]
    )
    wait(3, 17)
    start(3, 9)
    wait(3, 18)
    start(3, 10)
    for w in range(3):
        got(resr.at[w], ts.at[5 + w], tr.at[5 + w])
    pointwise(
        pl.ds(pl.multiple_of((1 - zl) * wide, 128), rem),
        lambda r: [resr[w, r].astype(jnp.float32) for w in range(3)],
    )

    ready = set()

    def out_piece(q):
        row0, size = PIECES[q][0] * 48, PIECES[q][1] * 48
        group = row0 // piece
        if group not in ready:
            ready.add(group)
            if group == 0:
                own_copies[3].wait()
            wait(3, *{0: (0, 6), 1: (9, 10), 2: (11, 12), 3: (15, 16)}[group])
        if size < piece:
            r = pl.ds(row0, size)
            p[r] = dot_nt(full[r], stacked[...]).astype(bf)
            return

        def chunk(n, _):
            r = pl.ds(pl.multiple_of(row0 + n * 2 * depth, 16), 2 * depth)
            p[r] = dot_nt(full[r], stacked[...]).astype(bf)
            return 0

        lax.fori_loop(0, 2, chunk, 0)

    def x_src(row0):
        def src(chunk, lo, size):
            return p.at[pl.ds(row0 + lo, size), pl.ds(pl.multiple_of(((x + chunk) % 4) * 128, 128), 128)]

        return src

    def z_src(row0, size):
        def src(chunk):
            return xc.at[pl.ds(pl.multiple_of(row0 + ((zh + chunk) % 4) * size, 16), size)]

        return src

    def block_owner(group, j):
        hi, lo = j // 2, j % 2
        if group == 0:
            return at(0, hi, lo)
        if group == 3:
            return at(2, hi, lo)
        return at(2 * hi - 1, group - 1, lo)

    def g_block(lo, size, chunk):
        return gt.at[pl.ds(pl.multiple_of(lo, 16), size), pl.ds(pl.multiple_of(((x + chunk) % 4) * 128, 128), 128)]

    def z_peer(k):
        return (zh + k) % 4

    def step(i, q):
        row0, size = PIECES[q][0] * 48, PIECES[q][1] * 48
        group, mid, sub = row0 // piece, size // 2, size // 4
        src, zsrc = x_src(row0), z_src(row0, sub)
        lower, upper = (0, mid), (mid, mid)

        def inbox(dst, part):
            return xin.at[dst, pl.ds(row0 + part[0], part[1])]

        def send(k, frm, dst, target):
            go(frm, dst, sx.at[0], rx.at[q, k], "shard", target, False)

        def came(k, ref):
            got(ref, sx.at[0], rx.at[q, k])

        def zbox(k):
            return zin.at[k - 1, pl.ds(row0 // 4, sub)]

        two = xin.at[pl.ds(1, 2), pl.ds(row0, size)]
        one = xin.at[0, pl.ds(row0, size)]
        three = zin.at[:, pl.ds(row0 // 4, sub)]

        if i == 0:
            send(0, src(2, *upper), inbox(0, upper), right)
            send(0, src(2, *lower), inbox(0, lower), left)
            send(1, src(1, *lower), inbox(1, lower), right)
            send(1, src(3, *upper), inbox(2, upper), left)
        if i == 1:
            came(0, one)
            for part, frm, dst, target in ((upper, 1, 1, right), (lower, 3, 2, left)):
                out = xtx.at[pl.ds(row0 + part[0], part[1])]
                out[...] = plus(src(frm, *part)[...], inbox(0, part)[...]).astype(bf)
                send(1, out, inbox(dst, part), target)
        if i == 2:
            came(1, two)
            both = (0, size)
            xc[row0 : row0 + size] = plus(src(0, *both)[...], inbox(1, both)[...], inbox(2, both)[...]).astype(bf)
            for k in (2, 1, 3):
                send(2, zsrc(k), zbox(k), z_peer(k) * 4 + x)
        if i == 3:
            came(2, three)
            total = plus(zsrc(0)[...], zbox(1)[...], zbox(2)[...], zbox(3)[...])
            lanes = pl.ds(pl.multiple_of((x % 2) * 128, 128), 128)
            row = row0 - group * piece + zh * sub
            block = row // depth
            r = pl.ds(pl.multiple_of(block_owner(group, block) * depth + row - block * depth, 16), sub)
            is_out = (1 - x // 2).astype(jnp.float32)
            wanted = tgt_t[r, lanes].astype(jnp.float32) * is_out
            mine = g_block(row0 + zh * sub, sub, 0)
            mine[...] = (keep[0:1, lanes] * (total - wanted)).astype(bf)
            for k in (2, 1, 3):
                send(3, mine, mine, z_peer(k) * 4 + x)
        if i == 4:
            came(3, three)
            ref = g_block(row0, size, 0)
            send(4, ref, ref, right)
            send(4, ref, ref, left)
        if i == 5:
            came(4, two)
            ref = g_block(row0, mid, 3)
            send(5, ref, ref, right)
            ref = g_block(row0 + mid, mid, 1)
            send(5, ref, ref, left)
        if i == 6:
            came(5, one)

    def back_chunk(group, c):
        r = slice(group * piece, (group + 1) * piece)
        term = dot_tn(gt[r], full[r, c])
        if group == 0:
            back[:, c] = term
        else:
            back[:, c] += term

    def back_piece(group):
        def chunk(n, _):
            back_chunk(group, pl.ds(pl.multiple_of(n * part, 128), part))
            return 0

        lax.fori_loop(0, PARTS, chunk, 0)

    out_piece(0)
    step(0, 0)
    wait(3, 7)
    start(3, 13)
    wait(3, 8)
    start(3, 14, 15)
    out_piece(1)
    step(0, 1)
    out_piece(2)
    step(0, 2)
    out_piece(3)
    step(0, 3)
    out_piece(4)
    out_piece(5)
    step(1, 0)
    step(0, 5)
    step(1, 1)
    diagonal(3)
    step(1, 2)
    step(0, 4)
    step(1, 3)
    step(2, 0)
    step(1, 5)
    out_piece(6)
    step(2, 1)
    step(0, 6)
    out_piece(7)
    last(3)
    step(2, 2)
    step(1, 4)
    out_piece(8)
    step(0, 8)
    step(0, 7)
    step(2, 3)
    step(2, 5)
    step(3, 0)
    step(1, 6)
    out_piece(9)
    step(0, 9)
    step(3, 1)
    out_piece(10)
    step(0, 10)
    out_piece(11)
    step(2, 4)
    step(0, 11)
    step(3, 3)
    step(3, 2)
    step(1, 7)
    step(1, 8)
    step(1, 9)
    step(2, 6)
    step(3, 5)
    step(4, 0)
    step(1, 10)
    step(1, 11)
    step(3, 4)
    step(4, 1)
    step(2, 7)
    step(2, 8)
    step(4, 3)
    step(4, 2)
    step(2, 9)
    step(5, 0)
    step(2, 11)
    step(2, 10)
    step(4, 5)
    step(5, 1)
    step(4, 4)
    step(3, 6)
    step(5, 3)
    step(3, 8)
    step(3, 7)
    step(5, 2)
    step(3, 9)
    step(5, 5)
    step(6, 0)
    step(6, 1)
    step(5, 4)
    step(6, 3)
    step(3, 10)
    step(3, 11)
    step(4, 6)
    step(6, 2)
    step(4, 8)
    back_piece(0)
    step(4, 7)
    step(6, 4)
    step(4, 9)
    step(6, 5)
    step(4, 10)
    step(4, 11)
    step(5, 6)
    back_piece(1)
    step(5, 8)
    step(5, 7)
    step(5, 9)
    step(5, 10)
    step(5, 11)
    step(6, 6)
    step(6, 8)
    step(6, 7)
    back_piece(2)
    step(6, 9)
    step(6, 10)
    step(6, 11)

    loads[3].wait()
    loads[4].wait()
    got(tok_t2, ms.at[1], mr.at[1])

    def pc(q):
        return pl.ds(q * part, part)

    def chip(dy, dz):
        return at(dy, dz, 0) // 2

    def c_block(dy, dz, q, lo=0, size=depth):
        return cp.at[pl.ds(pl.multiple_of(chip(dy, dz) * depth + lo, 16), size), pc(q)]

    def make(q, *which):
        for dy, dz in which:
            r = pl.ds(pl.multiple_of(at(dy, dz, 0) * depth, 16), depth)
            total = dot_nn(tok_t[r], tgg[:, pc(q)]) + dot_nn(tok_t2[r], tgg2[:, pc(q)])
            c_block(dy, dz, q)[...] = (total * inv_root).astype(bf)

    def box(slot, q, lo=0, size=depth):
        return cin.at[slot, pl.ds(lo, size), pc(q)]

    def send_c(src, dst, k, q, target):
        go(src, dst, cs.at[0], cr.at[q, k], "dp", target, False)

    def got_c(ref, k, q):
        got(ref, cs.at[0], cr.at[q, k])

    rest = depth - cut

    def reduce_step(i, q):
        if i == 0:
            got(tgg2.at[:, pc(q)], ms.at[2 + q], mr.at[2 + q])
            make(q, (2, 1), (1, 1), (-1, 1))
            send_c(c_block(2, 1, q), box(0, q), 0, q, zed)
            send_c(c_block(1, 1, q), box(1, q), 1, q, up)
            send_c(c_block(-1, 1, q), box(2, q), 2, q, down)
            make(q, (2, 0), (0, 1), (1, 0), (-1, 0), (0, 0))
        if i == 1:
            got_c(box(0, q), 0, q)
            cout[0, :, pc(q)] = plus(c_block(2, 0, q)[...], box(0, q)[...]).astype(bf)
            send_c(cout.at[0, pl.ds(0, cut), pc(q)], box(3, q, 0, cut), 3, q, up)
            send_c(cout.at[0, pl.ds(cut, rest), pc(q)], box(3, q, cut, rest), 4, q, down)
            got_c(box(1, q), 1, q)
            got_c(box(2, q), 2, q)
            cout[1, :, pc(q)] = plus(c_block(0, 1, q)[...], box(1, q)[...], box(2, q)[...]).astype(bf)
            send_c(cout.at[1, :, pc(q)], box(4, q), 5, q, zed)
        if i == 2:
            got_c(box(3, q, 0, cut), 3, q)
            cout[2, :cut, pc(q)] = plus(c_block(1, 0, q, 0, cut)[...], box(3, q, 0, cut)[...]).astype(bf)
            cout[2, cut:, pc(q)] = c_block(1, 0, q, cut, rest)[...]
            send_c(cout.at[2, :, pc(q)], box(5, q), 6, q, up)
            got_c(box(3, q, cut, rest), 4, q)
            cout[3, cut:, pc(q)] = plus(c_block(-1, 0, q, cut, rest)[...], box(3, q, cut, rest)[...]).astype(bf)
            cout[3, :cut, pc(q)] = c_block(-1, 0, q, 0, cut)[...]
            send_c(cout.at[3, :, pc(q)], box(6, q), 7, q, down)
        if i == 3:
            got_c(box(4, q), 5, q)
            got_c(box(5, q), 6, q)
            got_c(box(6, q), 7, q)
            total = plus(c_block(0, 0, q)[...], box(4, q)[...], box(5, q)[...], box(6, q)[...])
            own = vec[:, pc(q)]
            o_ref[:, pc(q)] = (
                grad[:, pc(q)].astype(jnp.float32)
                + (1.0 - damping) * own.astype(jnp.float32)
                - step_size * total
            ).astype(bf)

    for q in range(PARTS):

        def combine(i, _):
            r = pl.ds(pl.multiple_of(i * 32, 16), 32)
            r2 = pl.ds(pl.multiple_of(tok_rows + i * 32, 16), 32)
            tgg[r, pc(q)] = (fac[0, r, pc(q)] * back[r2, pc(q)] + fac[1, r, pc(q)] * back[r, pc(q)]).astype(bf)
            return 0

        back_chunk(3, pc(q))
        lax.fori_loop(0, tok_rows // 32, combine, 0)
        go(tgg.at[:, pc(q)], tgg2.at[:, pc(q)], ms.at[2 + q], mr.at[2 + q], "dp", sib)
    for q in range(PARTS):
        reduce_step(0, q)
    for q in range(PARTS):
        reduce_step(1, q)
    for q in range(PARTS):
        reduce_step(2, q)
    for q in range(PARTS):
        reduce_step(3, q)
    for w in range(4):
        ref = full if w == 3 else half.at[w]
        ref = ref.at[pl.ds(0, 15 * depth)]
        pltpu.make_async_copy(ref, ref, gs.at[w]).wait()
    ref = full.at[pl.ds(0, width * 15 * 128 // (2 * cols))]
    pltpu.make_async_copy(ref, ref, sx.at[0]).wait()
    ref = full.at[pl.ds(0, 7 * depth)]
    pltpu.make_async_copy(ref, ref, cs.at[0]).wait()
    for copy in sent:
        copy.wait_send()


def per_device(tokens, target, segments, gate_weight, up_weight, down_weight, vector, gradient):
    tok_rows, width = tokens.shape
    depth, cols = gate_weight.shape
    bf, f32 = jnp.bfloat16, jnp.float32
    piece = 4 * depth
    cut = (depth // 32 + 1) * 16
    wide = -(-cols // 256) * 128
    vm, dma = pltpu.VMEM, pltpu.SemaphoreType.DMA
    anywhere = pl.BlockSpec(memory_space=pltpu.HBM)
    scratch = [
        vm((3, width, wide), bf),
        vm((width, cols), bf),
        vm((tok_rows, width), bf),
        vm((tok_rows, width), bf),
        vm((4, tok_rows, piece), bf),
        vm((4, tok_rows, piece), bf),
        vm((width, tok_rows), bf),
        vm((width, tok_rows), bf),
        vm((width, tok_rows), bf),
        vm((1, tok_rows), jnp.int32),
        vm((1, tok_rows), jnp.int32),
        vm((8, tok_rows), f32),
        vm((3, tok_rows, wide), f32),
        vm((3, tok_rows, cols - wide), f32),
        vm((3, tok_rows, cols - wide), bf),
        vm((3, tok_rows, cols - wide), bf),
        vm((2, tok_rows, cols), f32),
        vm((2 * tok_rows, cols), bf),
        vm((width, 2 * tok_rows), bf),
        vm((2 * tok_rows, cols), f32),
        vm((width, 2 * tok_rows), bf),
        vm((3, width, 128), bf),
        vm((width, 128), bf),
        vm((width, 128), bf),
        vm((3, width // 4, 128), bf),
        vm((tok_rows, cols), bf),
        vm((tok_rows, cols), bf),
        vm((8 * depth, cols), bf),
        vm((7, depth, cols), bf),
        vm((4, depth, cols), bf),
        vm((depth, cols), bf),
        vm((depth, cols), bf),
        dma((4,)),
        dma((4, GATHER_COPIES)),
        dma((1,)),
        dma((len(PIECES), 6)),
        dma((1,)),
        dma((PARTS, 8)),
        dma((2 + PARTS,)),
        dma((2 + PARTS,)),
        dma((8,)),
        dma((8,)),
        dma((9,)),
    ]
    return pl.pallas_call(
        functools.partial(step_kernel, (tok_rows, width, depth, cols)),
        out_shape=jax.ShapeDtypeStruct((depth, cols), bf),
        in_specs=[anywhere] * 8,
        out_specs=pl.BlockSpec(memory_space=pltpu.VMEM),
        scratch_shapes=scratch,
        compiler_params=pltpu.CompilerParams(
            collective_id=1, has_side_effects=True, vmem_limit_bytes=56 * 2**20
        ),
    )(tokens, target, segments[None], gate_weight, up_weight, vector, down_weight, gradient)


def solution(mesh):
    return jax.shard_map(
        per_device,
        mesh=mesh,
        in_specs=(
            P("dp", None),
            P("dp", None),
            P("dp"),
            P("dp", "shard"),
            P("dp", "shard"),
            P("dp", "shard"),
            P("dp", "shard"),
            P("dp", "shard"),
        ),
        out_specs=P("dp", "shard"),
        check_vma=False,
    )
```

```python
import functools

import jax
import jax.numpy as jnp
from jax import lax
from jax.experimental import pallas as pl
from jax.experimental.pallas import tpu as pltpu
from jax.sharding import PartitionSpec as P

MESH = pl.DeviceIdType.MESH
coeff_k = 0.7978845608028654
coeff_c = 0.044715
damping = 0.01
step_size = 0.8


def gelu_parts(pre_act):
    inner_arg = coeff_k * (pre_act + coeff_c * pre_act * pre_act * pre_act)
    tanh_value = jnp.tanh(inner_arg)
    slope_term = coeff_k * (1.0 + 3.0 * coeff_c * pre_act * pre_act)
    curve_term = 6.0 * coeff_k * coeff_c * pre_act
    sech_square = 1.0 - tanh_value * tanh_value
    gelu_value = 0.5 * pre_act * (1.0 + tanh_value)
    gelu_slope = 0.5 * (1.0 + tanh_value) + 0.5 * pre_act * sech_square * slope_term
    gelu_curve = sech_square * (
        slope_term + 0.5 * pre_act * (curve_term - 2.0 * tanh_value * slope_term * slope_term)
    )
    return (gelu_value, gelu_slope, gelu_curve)


def remote(src, dst, send_sem, recv_sem, axis, index):
    return pltpu.make_async_remote_copy(
        src_ref=src,
        dst_ref=dst,
        send_sem=send_sem,
        recv_sem=recv_sem,
        device_id={axis: index},
        device_id_type=MESH,
    )


GATHER_COPIES = 19
PARTS = ((0, 256), (256, 384), (640, 256), (896, 256))
PIECES = ((0, 4), (4, 4), (8, 4), (12, 4), (16, 4), (20, 4), (24, 4), (28, 4), (32, 4), (36, 4), (40, 4), (44, 4))


def plus(a, *more):
    total = a.astype(jnp.float32)
    for b in more:
        total = total + b.astype(jnp.float32)
    return total


def dot_nn(a, b):
    return jnp.dot(a, b, preferred_element_type=jnp.float32)


def dot_nt(a, b):
    return lax.dot_general(a, b, (((1,), (1,)), ((), ())), preferred_element_type=jnp.float32)


def dot_tn(a, b):
    return lax.dot_general(a, b, (((0,), (0,)), ((), ())), preferred_element_type=jnp.float32)


def step_kernel(
    dims, tok_hbm, tgt_hbm, seg_hbm, gate_hbm, up_hbm, vec_hbm, down_hbm, grad_hbm, o_ref,
    half, full, tok, tgt, tok4, tokp, tok_t, tok_t2, tgt_t, seg, seg_prev, keep, acc, accp, resb, resr, fac, stacked, p, back, gt,
    xin, xtx, xc, zin, tgg, tgg2, cp, cin, cout, grad, vec,
    gs, gr, sx, rx, cs, cr, ms, mr, ts, tr, ls,
):
    tok_rows, width, depth, cols = dims
    bf = jnp.bfloat16
    d, sh = lax.axis_index("dp"), lax.axis_index("shard")
    y, zl, core = d // 4, (d // 2) % 2, d % 2
    x, zh = sh % 4, sh // 4
    piece = 4 * depth
    cut = (depth // 32 + 1) * 16
    wide = -(-cols // 256) * 128
    rem = cols - wide
    third = cols // 3
    inv_root = float(width) ** (-0.5)

    def at(dy, dz, dc):
        return ((y + dy) % 4) * 4 + ((zl + dz) % 2) * 2 + (core + dc) % 2

    sib, up, down, zed = at(0, 0, 1), at(1, 0, 0), at(-1, 0, 0), at(0, 1, 0)
    right, left = zh * 4 + (x + 1) % 4, zh * 4 + (x + 3) % 4
    above, below = ((zh + 1) % 4) * 4 + x, ((zh + 3) % 4) * 4 + x
    across = ((zh + 2) % 4) * 4 + x
    after, before = (d + 1) % 16, (d + 15) % 16
    barrier = pltpu.get_barrier_semaphore()
    for axis, targets in (("dp", (sib, up, down, zed, after, before)), ("shard", (right, left, above, below, across))):
        for t in targets:
            pl.semaphore_signal(barrier, inc=1, device_id={axis: t}, device_id_type=MESH)

    loads = [
        pltpu.make_async_copy(src, dst, ls.at[i])
        for i, (src, dst) in enumerate(((tok_hbm, tok), (tgt_hbm, tgt), (seg_hbm, seg), (grad_hbm, grad), (vec_hbm, vec)))
    ]
    for copy in loads:
        copy.start()
    pl.semaphore_wait(barrier, 11)

    sent = []

    def go(src, dst, s, r, axis, target, kept=True):
        copy = remote(src, dst, s, r, axis, target)
        copy.start()
        if kept:
            sent.append(copy)

    def got(ref, s, r):
        remote(ref, ref, s, r, "dp", sib).wait_recv()

    def place(dy, dz, dc):
        return {0: 2 * dz, -1: 4 + 4 * dz, 1: 6 + 4 * dz, 2: 12 + 2 * dz}[dy] + dc

    extent = {"w": (0, depth), "a": (0, cut), "b": (cut, depth - cut)}

    def rows(w, rel, which):
        lo, size = extent[which]
        base = place(*rel) if w == 3 else at(*rel)
        r = pl.ds(pl.multiple_of(base * depth + lo, 16), size)
        return full.at[r] if w == 3 else half.at[w, r]

    def own_part(w, which, z_of):
        lo, size = extent[which]
        if w == 3:
            return ins[w].at[pl.ds(lo, size)]
        return ins[w].at[pl.ds(lo, size), pl.ds(pl.multiple_of(z_of * rem, 128), wide)]

    me = at(0, 0, 0)
    table = [
        ((0, 0, 0), "w", sib, (0, 0, 1)),
        ((0, 0, 0), "w", up, (-1, 0, 0)),
        ((0, 0, 0), "w", down, (1, 0, 0)),
        ((0, 0, 0), "w", zed, (0, 1, 0)),
        ((0, 1, 0), "w", up, (-1, 1, 0)),
        ((0, 1, 0), "w", down, (1, 1, 0)),
        ((0, 1, 0), "w", sib, (0, 1, 1)),
        ((-1, 0, 0), "a", up, (2, 0, 0)),
        ((1, 0, 0), "b", down, (2, 0, 0)),
        ((-1, 0, 0), "w", sib, (-1, 0, 1)),
        ((1, 0, 0), "w", sib, (1, 0, 1)),
        ((-1, 1, 0), "w", sib, (-1, 1, 1)),
        ((1, 1, 0), "w", sib, (1, 1, 1)),
        ((2, 0, 0), "a", zed, (2, 1, 0)),
        ((2, 0, 0), "b", zed, (2, 1, 0)),
        ((2, 0, 0), "w", sib, (2, 0, 1)),
        ((2, 1, 0), "w", sib, (2, 1, 1)),
    ]
    special_down = {
        1: ((0, 0, 0), "a", up, (-1, 0, 0)),
        2: ((0, 0, 0), "b", down, (1, 0, 0)),
        17: ((0, 0, 0), "b", up, (-1, 0, 0)),
        18: ((0, 0, 0), "a", down, (1, 0, 0)),
    }
    ins = (gate_hbm, up_hbm, vec_hbm, down_hbm)

    special_half = {
        13: ((-1, 1, 0), "a", up, (2, 1, 0)),
        14: ((1, 1, 0), "b", down, (2, 1, 0)),
    }

    def entry(w, k):
        special = special_down if w == 3 else special_half
        return special[k] if k in special else table[k]

    def start(w, *numbers):
        for k in numbers:
            mine, which, target, theirs = entry(w, k)
            src = rows(w, mine, which)
            if mine == (0, 0, 0):
                src = own_part(w, which, (zl + (k == 3)) % 2)
            dst = rows(w, theirs if w == 3 else mine, which)
            go(src, dst, gs.at[w], gr.at[w, k], "dp", target, False)

    def wait(w, *numbers):
        for k in numbers:
            _, which, _, came = entry(w, k)
            got(rows(w, came, which), gs.at[w], gr.at[w, k])

    own_copies = [pltpu.make_async_copy(own_part(w, "w", zl), rows(w, (0, 0, 0), "w"), ls.at[5 + w]) for w in range(4)]

    late = {0: (0, 6), -1: (9, 11), 1: (10, 12), 2: (15, 16)}

    def piece_of(rel):
        return (y + rel) % 4

    def piece_rows(rel):
        return pl.ds(pl.multiple_of(piece_of(rel) * piece, 16), piece)

    came_in = set()

    def settle(w, rel):
        if (w, rel) in came_in:
            return
        came_in.add((w, rel))
        wait(w, *late[rel])
        if rel == 0:
            own_copies[w].wait()

    def use(w, rel):
        settle(w, rel)
        for c in (slice(0, 384), slice(384, wide)):
            term = dot_nn(tok4[piece_of(rel)], half[w, piece_rows(rel), c])
            if rel == 0:
                acc[w, :, c] = term
            else:
                acc[w, :, c] += term

    def use_for_partner(w, rel):
        settle(w, rel)

        def chunk(n, _):
            c = pl.ds(pl.multiple_of(n * (rem // 2), 128), rem // 2)
            c2 = pl.ds(pl.multiple_of(zl * (wide - rem) + n * (rem // 2), 128), rem // 2)
            term = dot_nn(tokp[piece_of(rel)], half[w, piece_rows(rel), c2])
            if rel == 0:
                accp[w, :, c] = term
            else:
                accp[w, :, c] += term
            if rel == 2:
                resb[w, :, c] = accp[w, :, c].astype(bf)
            return 0

        lax.fori_loop(0, 2, chunk, 0)
        if rel == 2:
            go(resb.at[w], resr.at[w], ts.at[5 + w], tr.at[5 + w], "dp", zed)

    start(0, 1, 2, 3, 0)
    own_copies[0].start()
    start(1, 1, 2, 0)
    own_copies[1].start()
    go(seg_hbm, seg_prev, ms.at[0], mr.at[0], "dp", after)

    loads[0].wait()
    for r in range(4):
        tok4[r] = tok[:, r * piece : (r + 1) * piece]
    go(tok4.at[x], tokp.at[x], ts.at[0], tr.at[0], "dp", zed)
    start(1, 3)
    start(2, 3, 0)
    own_copies[2].start()
    start(3, 3, 0)
    own_copies[3].start()

    def turn(src, dst):
        def body(j, _):
            c = pl.ds(pl.multiple_of(j * 128, 128), 128)
            dst[c, :] = src[:, c].astype(jnp.float32).T.astype(bf)
            return 0

        lax.fori_loop(0, width // 128, body, 0)

    turn(tok, tok_t)
    go(tok_t, tok_t2, ms.at[1], mr.at[1], "dp", sib)

    def tokens_start():
        got(tokp.at[x], ts.at[0], tr.at[0])
        go(tokp.at[x], tokp.at[x], ts.at[1], tr.at[1], "shard", right)
        go(tokp.at[x], tokp.at[x], ts.at[2], tr.at[2], "shard", left)

    def tokens_relay():
        h = tok_rows // 2
        got(tokp.at[(x + 3) % 4], ts.at[1], tr.at[1])
        ref = tokp.at[(x + 3) % 4, pl.ds(0, h)]
        go(ref, ref, ts.at[3], tr.at[3], "shard", right)
        got(tokp.at[(x + 1) % 4], ts.at[2], tr.at[2])
        ref = tokp.at[(x + 1) % 4, pl.ds(h, h)]
        go(ref, ref, ts.at[4], tr.at[4], "shard", left)

    def tokens_end():
        h = tok_rows // 2
        got(tokp.at[(x + 2) % 4, pl.ds(0, h)], ts.at[3], tr.at[3])
        got(tokp.at[(x + 2) % 4, pl.ds(h, h)], ts.at[4], tr.at[4])

    def near_z(w):
        wait(w, 3)
        start(w, 4, 5, 6)

    def near(w):
        wait(w, 1)
        start(w, 7, 9)
        wait(w, 2)
        start(w, 8, 10)

    def diagonal(w):
        wait(w, 4)
        start(w, 11)
        wait(w, 5)
        start(w, 12)

    def round_z(w):
        wait(w, 4)
        start(w, 13, 11)
        wait(w, 5)
        start(w, 14, 12)

    def far(w):
        wait(w, 7, 8)
        start(w, 15)

    def last(w):
        wait(w, 13, 14)
        start(w, 16)

    near_z(0)
    near(0)
    start(2, 1, 2)
    loads[1].wait()
    turn(tgt, tgt_t)
    tokens_start()
    near_z(1)
    round_z(0)
    near(1)
    use(0, 0)
    far(0)
    use(0, -1)
    use(0, 1)
    tokens_relay()
    round_z(1)
    near_z(2)
    last(0)
    near(2)
    use(1, 0)
    use(2, 0)
    use(1, -1)
    far(1)
    tokens_end()
    use_for_partner(0, 0)
    use_for_partner(0, -1)
    use_for_partner(0, 1)
    use_for_partner(0, 2)
    last(1)
    use_for_partner(1, 0)
    use_for_partner(1, -1)
    use_for_partner(1, 1)
    use_for_partner(1, 2)
    use_for_partner(2, 0)
    round_z(2)
    start(3, 1, 2, 17, 18)
    use(0, 2)
    use(1, 1)
    use(1, 2)
    far(2)
    use_for_partner(2, -1)
    use_for_partner(2, 1)
    last(2)
    use(2, -1)
    use(2, 1)
    use_for_partner(2, 2)
    use(2, 2)
    wait(3, 3)
    start(3, 6)
    wait(3, 1)
    start(3, 7)
    wait(3, 2)
    start(3, 8)
    start(3, 4, 5)

    loads[2].wait()
    got(seg_prev, ms.at[0], mr.at[0])
    lane = lax.broadcasted_iota(jnp.int32, (8, tok_rows), 1)
    here = jnp.broadcast_to(seg[...], (8, tok_rows))
    previous = jnp.where(
        lane == 0,
        pltpu.roll(jnp.broadcast_to(seg_prev[...], (8, tok_rows)), 1, 1),
        pltpu.roll(here, 1, 1),
    )
    first = (lane + d) == 0
    keep[...] = jnp.where(first, 0.0, jnp.where(here == previous, 1.0, 0.0))

    def pointwise(c, parts_of):
        def body(i, _):
            r = pl.ds(pl.multiple_of(i * 16, 16), 16)
            r2 = pl.ds(pl.multiple_of(tok_rows + i * 16, 16), 16)
            pre_gate, up_act, tangent_raw = parts_of(r)
            value, slope, curve = gelu_parts(pre_gate)
            tangent = tangent_raw * inv_root
            stacked[r, c] = (value * up_act).astype(bf)
            stacked[r2, c] = (slope * tangent * up_act).astype(bf)
            fac[0, r, c] = up_act * slope
            fac[1, r, c] = up_act * curve * tangent
            return 0

        lax.fori_loop(0, tok_rows // 16, body, 0)

    pointwise(
        pl.ds(pl.multiple_of(zl * rem, 128), wide), lambda r: [acc[w, r] for w in range(3)]
    )
    wait(3, 17)
    start(3, 9)
    wait(3, 18)
    start(3, 10)
    for w in range(3):
        got(resr.at[w], ts.at[5 + w], tr.at[5 + w])
    pointwise(
        pl.ds(pl.multiple_of((1 - zl) * wide, 128), rem),
        lambda r: [resr[w, r].astype(jnp.float32) for w in range(3)],
    )

    ready = set()

    def out_piece(q):
        row0, size = PIECES[q][0] * 48, PIECES[q][1] * 48
        group = row0 // piece
        if group not in ready:
            ready.add(group)
            if group == 0:
                own_copies[3].wait()
            wait(3, *{0: (0, 6), 1: (9, 10), 2: (11, 12), 3: (15, 16)}[group])
        if size < piece:
            r = pl.ds(row0, size)
            p[r] = dot_nt(full[r], stacked[...]).astype(bf)
            return

        def chunk(n, _):
            r = pl.ds(pl.multiple_of(row0 + n * 2 * depth, 16), 2 * depth)
            p[r] = dot_nt(full[r], stacked[...]).astype(bf)
            return 0

        lax.fori_loop(0, 2, chunk, 0)

    def x_src(row0):
        def src(chunk, lo, size):
            return p.at[pl.ds(row0 + lo, size), pl.ds(pl.multiple_of(((x + chunk) % 4) * 128, 128), 128)]

        return src

    def z_src(row0, size):
        def src(chunk):
            return xc.at[pl.ds(pl.multiple_of(row0 + ((zh + chunk) % 4) * size, 16), size)]

        return src

    def block_owner(group, j):
        hi, lo = j // 2, j % 2
        if group == 0:
            return at(0, hi, lo)
        if group == 3:
            return at(2, hi, lo)
        return at(2 * hi - 1, group - 1, lo)

    def g_block(lo, size, chunk):
        return gt.at[pl.ds(pl.multiple_of(lo, 16), size), pl.ds(pl.multiple_of(((x + chunk) % 4) * 128, 128), 128)]

    def z_peer(k):
        return (zh + k) % 4

    def step(i, q):
        row0, size = PIECES[q][0] * 48, PIECES[q][1] * 48
        group, mid, sub = row0 // piece, size // 2, size // 4
        src, zsrc = x_src(row0), z_src(row0, sub)
        lower, upper = (0, mid), (mid, mid)

        def inbox(dst, part):
            return xin.at[dst, pl.ds(row0 + part[0], part[1])]

        def send(k, frm, dst, target):
            go(frm, dst, sx.at[0], rx.at[q, k], "shard", target, False)

        def came(k, ref):
            got(ref, sx.at[0], rx.at[q, k])

        def zbox(k):
            return zin.at[k - 1, pl.ds(row0 // 4, sub)]

        two = xin.at[pl.ds(1, 2), pl.ds(row0, size)]
        one = xin.at[0, pl.ds(row0, size)]
        three = zin.at[:, pl.ds(row0 // 4, sub)]

        if i == 0:
            send(0, src(2, *upper), inbox(0, upper), right)
            send(0, src(2, *lower), inbox(0, lower), left)
            send(1, src(1, *lower), inbox(1, lower), right)
            send(1, src(3, *upper), inbox(2, upper), left)
        if i == 1:
            came(0, one)
            for part, frm, dst, target in ((upper, 1, 1, right), (lower, 3, 2, left)):
                out = xtx.at[pl.ds(row0 + part[0], part[1])]
                out[...] = plus(src(frm, *part)[...], inbox(0, part)[...]).astype(bf)
                send(1, out, inbox(dst, part), target)
        if i == 2:
            came(1, two)
            both = (0, size)
            xc[row0 : row0 + size] = plus(src(0, *both)[...], inbox(1, both)[...], inbox(2, both)[...]).astype(bf)
            for k in (2, 1, 3):
                send(2, zsrc(k), zbox(k), z_peer(k) * 4 + x)
        if i == 3:
            came(2, three)
            total = plus(zsrc(0)[...], zbox(1)[...], zbox(2)[...], zbox(3)[...])
            lanes = pl.ds(pl.multiple_of((x % 2) * 128, 128), 128)
            row = row0 - group * piece + zh * sub
            block = row // depth
            r = pl.ds(pl.multiple_of(block_owner(group, block) * depth + row - block * depth, 16), sub)
            is_out = (1 - x // 2).astype(jnp.float32)
            wanted = tgt_t[r, lanes].astype(jnp.float32) * is_out
            mine = g_block(row0 + zh * sub, sub, 0)
            mine[...] = (keep[0:1, lanes] * (total - wanted)).astype(bf)
            for k in (2, 1, 3):
                send(3, mine, mine, z_peer(k) * 4 + x)
        if i == 4:
            came(3, three)
            ref = g_block(row0, size, 0)
            send(4, ref, ref, right)
            send(4, ref, ref, left)
        if i == 5:
            came(4, two)
            ref = g_block(row0, mid, 3)
            send(5, ref, ref, right)
            ref = g_block(row0 + mid, mid, 1)
            send(5, ref, ref, left)
        if i == 6:
            came(5, one)

    def back_chunk(group, c):
        r = slice(group * piece, (group + 1) * piece)
        term = dot_tn(gt[r], full[r, c])
        if group == 0:
            back[:, c] = term
        else:
            back[:, c] += term

    def back_piece(group):
        def chunk(n, _):
            back_chunk(group, pl.ds(pl.multiple_of(n * third, 128), third))
            return 0

        lax.fori_loop(0, 3, chunk, 0)

    out_piece(0)
    step(0, 0)
    wait(3, 7)
    start(3, 13)
    wait(3, 8)
    start(3, 14, 15)
    out_piece(1)
    step(0, 1)
    out_piece(2)
    step(0, 2)
    out_piece(3)
    step(0, 3)
    out_piece(4)
    out_piece(5)
    step(1, 0)
    step(0, 5)
    step(1, 1)
    diagonal(3)
    step(1, 2)
    step(0, 4)
    step(1, 3)
    step(2, 0)
    step(1, 5)
    out_piece(6)
    step(2, 1)
    step(0, 6)
    out_piece(7)
    last(3)
    step(2, 2)
    step(1, 4)
    out_piece(8)
    step(0, 8)
    step(0, 7)
    step(2, 3)
    step(2, 5)
    step(3, 0)
    step(1, 6)
    out_piece(9)
    step(0, 9)
    step(3, 1)
    out_piece(10)
    step(0, 10)
    out_piece(11)
    step(2, 4)
    step(0, 11)
    step(3, 3)
    step(3, 2)
    step(1, 7)
    step(1, 8)
    step(1, 9)
    step(2, 6)
    step(3, 5)
    step(4, 0)
    step(1, 10)
    step(1, 11)
    step(3, 4)
    step(4, 1)
    step(2, 7)
    step(2, 8)
    step(4, 3)
    step(4, 2)
    step(2, 9)
    step(5, 0)
    step(2, 11)
    step(2, 10)
    step(4, 5)
    step(5, 1)
    step(4, 4)
    step(3, 6)
    step(5, 3)
    step(3, 8)
    step(3, 7)
    step(5, 2)
    step(3, 9)
    step(5, 5)
    step(6, 0)
    step(6, 1)
    step(5, 4)
    step(6, 3)
    step(3, 10)
    step(3, 11)
    step(4, 6)
    step(6, 2)
    step(4, 8)
    back_piece(0)
    step(4, 7)
    step(6, 4)
    step(4, 9)
    step(6, 5)
    step(4, 10)
    step(4, 11)
    step(5, 6)
    back_piece(1)
    step(5, 8)
    step(5, 7)
    step(5, 9)
    step(5, 10)
    step(5, 11)
    step(6, 6)
    step(6, 8)
    step(6, 7)
    back_piece(2)
    step(6, 9)
    step(6, 10)
    step(6, 11)

    loads[3].wait()
    loads[4].wait()
    got(tok_t2, ms.at[1], mr.at[1])

    def pc(q):
        return pl.ds(*PARTS[q])

    def chip(dy, dz):
        return at(dy, dz, 0) // 2

    def c_block(dy, dz, q, lo=0, size=depth):
        return cp.at[pl.ds(pl.multiple_of(chip(dy, dz) * depth + lo, 16), size), pc(q)]

    def make(q, *which):
        for dy, dz in which:
            r = pl.ds(pl.multiple_of(at(dy, dz, 0) * depth, 16), depth)
            total = dot_nn(tok_t[r], tgg[:, pc(q)]) + dot_nn(tok_t2[r], tgg2[:, pc(q)])
            c_block(dy, dz, q)[...] = (total * inv_root).astype(bf)

    def box(slot, q, lo=0, size=depth):
        return cin.at[slot, pl.ds(lo, size), pc(q)]

    def send_c(src, dst, k, q, target):
        go(src, dst, cs.at[0], cr.at[q, k], "dp", target, False)

    def got_c(ref, k, q):
        got(ref, cs.at[0], cr.at[q, k])

    rest, via_z = depth - cut, 16
    keep_y = depth - via_z

    def reduce_step(i, q):
        if i == 0:
            got(tgg2.at[:, pc(q)], ms.at[2 + q], mr.at[2 + q])
            make(q, (2, 1), (1, 1), (-1, 1))
            send_c(c_block(2, 1, q), box(0, q), 0, q, zed)
            send_c(c_block(1, 1, q, 0, keep_y), box(1, q, 0, keep_y), 1, q, up)
            send_c(c_block(-1, 1, q, 0, keep_y), box(2, q, 0, keep_y), 2, q, down)
            send_c(c_block(1, 1, q, keep_y, via_z), box(1, q, keep_y, via_z), 8, q, zed)
            send_c(c_block(-1, 1, q, keep_y, via_z), box(2, q, keep_y, via_z), 9, q, zed)
            make(q, (2, 0), (0, 1), (1, 0), (-1, 0), (0, 0))
        if i == 1:
            got_c(box(0, q), 0, q)
            cout[0, :, pc(q)] = plus(c_block(2, 0, q)[...], box(0, q)[...]).astype(bf)
            send_c(cout.at[0, pl.ds(0, cut), pc(q)], box(3, q, 0, cut), 3, q, up)
            send_c(cout.at[0, pl.ds(cut, rest), pc(q)], box(3, q, cut, rest), 4, q, down)
            got_c(box(1, q, 0, keep_y), 1, q)
            got_c(box(2, q, 0, keep_y), 2, q)
            cout[1, :keep_y, pc(q)] = plus(
                c_block(0, 1, q, 0, keep_y)[...], box(1, q, 0, keep_y)[...], box(2, q, 0, keep_y)[...]
            ).astype(bf)
            cout[1, keep_y:, pc(q)] = c_block(0, 1, q, keep_y, via_z)[...]
            send_c(cout.at[1, :, pc(q)], box(4, q), 5, q, zed)
        if i == 2:
            got_c(box(3, q, 0, cut), 3, q)
            cout[2, :cut, pc(q)] = plus(c_block(1, 0, q, 0, cut)[...], box(3, q, 0, cut)[...]).astype(bf)
            got_c(box(1, q, keep_y, via_z), 8, q)
            got_c(box(2, q, keep_y, via_z), 9, q)
            cout[2, cut:keep_y, pc(q)] = c_block(1, 0, q, cut, keep_y - cut)[...]
            cout[2, keep_y:, pc(q)] = plus(
                c_block(1, 0, q, keep_y, via_z)[...], box(1, q, keep_y, via_z)[...]
            ).astype(bf)
            send_c(cout.at[2, :, pc(q)], box(5, q), 6, q, up)
            got_c(box(3, q, cut, rest), 4, q)
            cout[3, cut:keep_y, pc(q)] = plus(
                c_block(-1, 0, q, cut, keep_y - cut)[...], box(3, q, cut, keep_y - cut)[...]
            ).astype(bf)
            cout[3, keep_y:, pc(q)] = plus(
                c_block(-1, 0, q, keep_y, via_z)[...],
                box(3, q, keep_y, via_z)[...],
                box(2, q, keep_y, via_z)[...],
            ).astype(bf)
            cout[3, :cut, pc(q)] = c_block(-1, 0, q, 0, cut)[...]
            send_c(cout.at[3, :, pc(q)], box(6, q), 7, q, down)
        if i == 3:
            got_c(box(4, q), 5, q)
            got_c(box(5, q), 6, q)
            got_c(box(6, q), 7, q)
            total = plus(c_block(0, 0, q)[...], box(4, q)[...], box(5, q)[...], box(6, q)[...])
            own = vec[:, pc(q)]
            o_ref[:, pc(q)] = (
                grad[:, pc(q)].astype(jnp.float32)
                + (1.0 - damping) * own.astype(jnp.float32)
                - step_size * total
            ).astype(bf)

    for q in range(len(PARTS)):

        def combine(i, _):
            r = pl.ds(pl.multiple_of(i * 32, 16), 32)
            r2 = pl.ds(pl.multiple_of(tok_rows + i * 32, 16), 32)
            tgg[r, pc(q)] = (fac[0, r, pc(q)] * back[r2, pc(q)] + fac[1, r, pc(q)] * back[r, pc(q)]).astype(bf)
            return 0

        back_chunk(3, pc(q))
        lax.fori_loop(0, tok_rows // 32, combine, 0)
        go(tgg.at[:, pc(q)], tgg2.at[:, pc(q)], ms.at[2 + q], mr.at[2 + q], "dp", sib)
    for q in range(len(PARTS)):
        reduce_step(0, q)
    for q in range(len(PARTS)):
        reduce_step(1, q)
    for q in range(len(PARTS)):
        reduce_step(2, q)
    for q in range(len(PARTS)):
        reduce_step(3, q)
    for w in range(4):
        ref = full if w == 3 else half.at[w]
        ref = ref.at[pl.ds(0, 15 * depth)]
        pltpu.make_async_copy(ref, ref, gs.at[w]).wait()
    ref = full.at[pl.ds(0, width * 15 * 128 // (2 * cols))]
    pltpu.make_async_copy(ref, ref, sx.at[0]).wait()
    ref = full.at[pl.ds(0, 7 * depth)]
    pltpu.make_async_copy(ref, ref, cs.at[0]).wait()
    for copy in sent:
        copy.wait_send()


def per_device(tokens, target, segments, gate_weight, up_weight, down_weight, vector, gradient):
    tok_rows, width = tokens.shape
    depth, cols = gate_weight.shape
    bf, f32 = jnp.bfloat16, jnp.float32
    piece = 4 * depth
    cut = (depth // 32 + 1) * 16
    wide = -(-cols // 256) * 128
    vm, dma = pltpu.VMEM, pltpu.SemaphoreType.DMA
    anywhere = pl.BlockSpec(memory_space=pltpu.HBM)
    scratch = [
        vm((3, width, wide), bf),
        vm((width, cols), bf),
        vm((tok_rows, width), bf),
        vm((tok_rows, width), bf),
        vm((4, tok_rows, piece), bf),
        vm((4, tok_rows, piece), bf),
        vm((width, tok_rows), bf),
        vm((width, tok_rows), bf),
        vm((width, tok_rows), bf),
        vm((1, tok_rows), jnp.int32),
        vm((1, tok_rows), jnp.int32),
        vm((8, tok_rows), f32),
        vm((3, tok_rows, wide), f32),
        vm((3, tok_rows, cols - wide), f32),
        vm((3, tok_rows, cols - wide), bf),
        vm((3, tok_rows, cols - wide), bf),
        vm((2, tok_rows, cols), f32),
        vm((2 * tok_rows, cols), bf),
        vm((width, 2 * tok_rows), bf),
        vm((2 * tok_rows, cols), f32),
        vm((width, 2 * tok_rows), bf),
        vm((3, width, 128), bf),
        vm((width, 128), bf),
        vm((width, 128), bf),
        vm((3, width // 4, 128), bf),
        vm((tok_rows, cols), bf),
        vm((tok_rows, cols), bf),
        vm((8 * depth, cols), bf),
        vm((7, depth, cols), bf),
        vm((4, depth, cols), bf),
        vm((depth, cols), bf),
        vm((depth, cols), bf),
        dma((4,)),
        dma((4, GATHER_COPIES)),
        dma((1,)),
        dma((len(PIECES), 6)),
        dma((1,)),
        dma((len(PARTS), 10)),
        dma((2 + len(PARTS),)),
        dma((2 + len(PARTS),)),
        dma((8,)),
        dma((8,)),
        dma((9,)),
    ]
    return pl.pallas_call(
        functools.partial(step_kernel, (tok_rows, width, depth, cols)),
        out_shape=jax.ShapeDtypeStruct((depth, cols), bf),
        in_specs=[anywhere] * 8,
        out_specs=pl.BlockSpec(memory_space=pltpu.VMEM),
        scratch_shapes=scratch,
        compiler_params=pltpu.CompilerParams(
            collective_id=1, has_side_effects=True, vmem_limit_bytes=107 * 2**19
        ),
    )(tokens, target, segments[None], gate_weight, up_weight, vector, down_weight, gradient)


def solution(mesh):
    return jax.shard_map(
        per_device,
        mesh=mesh,
        in_specs=(
            P("dp", None),
            P("dp", None),
            P("dp"),
            P("dp", "shard"),
            P("dp", "shard"),
            P("dp", "shard"),
            P("dp", "shard"),
            P("dp", "shard"),
        ),
        out_specs=P("dp", "shard"),
        check_vma=False,
    )
```

```python
import functools

import jax
import jax.numpy as jnp
from jax import lax
from jax.experimental import pallas as pl
from jax.experimental.pallas import tpu as pltpu
from jax.sharding import PartitionSpec as P

MESH = pl.DeviceIdType.MESH
coeff_k = 0.7978845608028654
coeff_c = 0.044715
damping = 0.01
step_size = 0.8


def gelu_parts(pre_act):
    inner_arg = coeff_k * (pre_act + coeff_c * pre_act * pre_act * pre_act)
    tanh_value = jnp.tanh(inner_arg)
    slope_term = coeff_k * (1.0 + 3.0 * coeff_c * pre_act * pre_act)
    curve_term = 6.0 * coeff_k * coeff_c * pre_act
    sech_square = 1.0 - tanh_value * tanh_value
    gelu_value = 0.5 * pre_act * (1.0 + tanh_value)
    gelu_slope = 0.5 * (1.0 + tanh_value) + 0.5 * pre_act * sech_square * slope_term
    gelu_curve = sech_square * (
        slope_term + 0.5 * pre_act * (curve_term - 2.0 * tanh_value * slope_term * slope_term)
    )
    return (gelu_value, gelu_slope, gelu_curve)


def remote(src, dst, send_sem, recv_sem, axis, index):
    return pltpu.make_async_remote_copy(
        src_ref=src,
        dst_ref=dst,
        send_sem=send_sem,
        recv_sem=recv_sem,
        device_id={axis: index},
        device_id_type=MESH,
    )


GATHER_COPIES = 19
PARTS = ((0, 128), (128, 384), (512, 384), (896, 256))
PIECES = ((0, 4), (4, 4), (8, 4), (12, 4), (16, 4), (20, 4), (24, 4), (28, 4), (32, 4), (36, 4), (40, 4), (44, 4))


def plus(a, *more):
    total = a.astype(jnp.float32)
    for b in more:
        total = total + b.astype(jnp.float32)
    return total


def dot_nn(a, b):
    return jnp.dot(a, b, preferred_element_type=jnp.float32)


def dot_nt(a, b):
    return lax.dot_general(a, b, (((1,), (1,)), ((), ())), preferred_element_type=jnp.float32)


def dot_tn(a, b):
    return lax.dot_general(a, b, (((0,), (0,)), ((), ())), preferred_element_type=jnp.float32)


def step_kernel(
    dims, tok_hbm, tgt_hbm, seg_hbm, gate_hbm, up_hbm, vec_hbm, down_hbm, grad_hbm, o_ref,
    half, full, tok, tgt, tok4, tokp, tok_t, tok_t2, tgt_t, seg, seg_prev, keep, acc, accp, resb, resr, fac, stacked, p, back, gt,
    xin, xtx, xc, zin, tgg, tgg2, cp, cin, cout, grad, vec,
    gs, gr, sx, rx, cs, cr, ms, mr, ts, tr, ls,
):
    tok_rows, width, depth, cols = dims
    bf = jnp.bfloat16
    d, sh = lax.axis_index("dp"), lax.axis_index("shard")
    y, zl, core = d // 4, (d // 2) % 2, d % 2
    x, zh = sh % 4, sh // 4
    piece = 4 * depth
    cut = (depth // 32 + 1) * 16
    wide = -(-cols // 256) * 128
    rem = cols - wide
    third = cols // 3
    inv_root = float(width) ** (-0.5)

    def at(dy, dz, dc):
        return ((y + dy) % 4) * 4 + ((zl + dz) % 2) * 2 + (core + dc) % 2

    sib, up, down, zed = at(0, 0, 1), at(1, 0, 0), at(-1, 0, 0), at(0, 1, 0)
    right, left = zh * 4 + (x + 1) % 4, zh * 4 + (x + 3) % 4
    above, below = ((zh + 1) % 4) * 4 + x, ((zh + 3) % 4) * 4 + x
    across = ((zh + 2) % 4) * 4 + x
    after, before = (d + 1) % 16, (d + 15) % 16
    barrier = pltpu.get_barrier_semaphore()
    for axis, targets in (("dp", (sib, up, down, zed, after, before)), ("shard", (right, left, above, below, across))):
        for t in targets:
            pl.semaphore_signal(barrier, inc=1, device_id={axis: t}, device_id_type=MESH)

    loads = [
        pltpu.make_async_copy(src, dst, ls.at[i])
        for i, (src, dst) in enumerate(((tok_hbm, tok), (tgt_hbm, tgt), (seg_hbm, seg), (grad_hbm, grad), (vec_hbm, vec)))
    ]
    for copy in loads:
        copy.start()
    pl.semaphore_wait(barrier, 11)

    sent = []

    def go(src, dst, s, r, axis, target, kept=True):
        copy = remote(src, dst, s, r, axis, target)
        copy.start()
        if kept:
            sent.append(copy)

    def got(ref, s, r):
        remote(ref, ref, s, r, "dp", sib).wait_recv()

    def place(dy, dz, dc):
        return {0: 2 * dz, -1: 4 + 4 * dz, 1: 6 + 4 * dz, 2: 12 + 2 * dz}[dy] + dc

    extent = {"w": (0, depth), "a": (0, cut), "b": (cut, depth - cut)}

    def rows(w, rel, which):
        lo, size = extent[which]
        base = place(*rel) if w == 3 else at(*rel)
        r = pl.ds(pl.multiple_of(base * depth + lo, 16), size)
        return full.at[r] if w == 3 else half.at[w, r]

    def own_part(w, which, z_of):
        lo, size = extent[which]
        if w == 3:
            return ins[w].at[pl.ds(lo, size)]
        return ins[w].at[pl.ds(lo, size), pl.ds(pl.multiple_of(z_of * rem, 128), wide)]

    me = at(0, 0, 0)
    table = [
        ((0, 0, 0), "w", sib, (0, 0, 1)),
        ((0, 0, 0), "w", up, (-1, 0, 0)),
        ((0, 0, 0), "w", down, (1, 0, 0)),
        ((0, 0, 0), "w", zed, (0, 1, 0)),
        ((0, 1, 0), "w", up, (-1, 1, 0)),
        ((0, 1, 0), "w", down, (1, 1, 0)),
        ((0, 1, 0), "w", sib, (0, 1, 1)),
        ((-1, 0, 0), "a", up, (2, 0, 0)),
        ((1, 0, 0), "b", down, (2, 0, 0)),
        ((-1, 0, 0), "w", sib, (-1, 0, 1)),
        ((1, 0, 0), "w", sib, (1, 0, 1)),
        ((-1, 1, 0), "w", sib, (-1, 1, 1)),
        ((1, 1, 0), "w", sib, (1, 1, 1)),
        ((2, 0, 0), "a", zed, (2, 1, 0)),
        ((2, 0, 0), "b", zed, (2, 1, 0)),
        ((2, 0, 0), "w", sib, (2, 0, 1)),
        ((2, 1, 0), "w", sib, (2, 1, 1)),
    ]
    special_down = {
        1: ((0, 0, 0), "a", up, (-1, 0, 0)),
        2: ((0, 0, 0), "b", down, (1, 0, 0)),
        17: ((0, 0, 0), "b", up, (-1, 0, 0)),
        18: ((0, 0, 0), "a", down, (1, 0, 0)),
    }
    ins = (gate_hbm, up_hbm, vec_hbm, down_hbm)

    special_half = {
        13: ((-1, 1, 0), "a", up, (2, 1, 0)),
        14: ((1, 1, 0), "b", down, (2, 1, 0)),
    }

    def entry(w, k):
        special = special_down if w == 3 else special_half
        return special[k] if k in special else table[k]

    def start(w, *numbers):
        for k in numbers:
            mine, which, target, theirs = entry(w, k)
            src = rows(w, mine, which)
            if mine == (0, 0, 0):
                src = own_part(w, which, (zl + (k == 3)) % 2)
            dst = rows(w, theirs if w == 3 else mine, which)
            go(src, dst, gs.at[w], gr.at[w, k], "dp", target, False)

    def wait(w, *numbers):
        for k in numbers:
            _, which, _, came = entry(w, k)
            got(rows(w, came, which), gs.at[w], gr.at[w, k])

    own_copies = [pltpu.make_async_copy(own_part(w, "w", zl), rows(w, (0, 0, 0), "w"), ls.at[5 + w]) for w in range(4)]

    late = {0: (0, 6), -1: (9, 11), 1: (10, 12), 2: (15, 16)}

    def piece_of(rel):
        return (y + rel) % 4

    def piece_rows(rel):
        return pl.ds(pl.multiple_of(piece_of(rel) * piece, 16), piece)

    came_in = set()

    def settle(w, rel):
        if (w, rel) in came_in:
            return
        came_in.add((w, rel))
        wait(w, *late[rel])
        if rel == 0:
            own_copies[w].wait()

    def use(w, rel):
        settle(w, rel)
        for c in (slice(0, 384), slice(384, wide)):
            term = dot_nn(tok4[piece_of(rel)], half[w, piece_rows(rel), c])
            if rel == 0:
                acc[w, :, c] = term
            else:
                acc[w, :, c] += term

    def use_for_partner(w, rel):
        settle(w, rel)

        def chunk(n, _):
            c = pl.ds(pl.multiple_of(n * (rem // 2), 128), rem // 2)
            c2 = pl.ds(pl.multiple_of(zl * (wide - rem) + n * (rem // 2), 128), rem // 2)
            term = dot_nn(tokp[piece_of(rel)], half[w, piece_rows(rel), c2])
            if rel == 0:
                accp[w, :, c] = term
            else:
                accp[w, :, c] += term
            if rel == 2:
                resb[w, :, c] = accp[w, :, c].astype(bf)
            return 0

        lax.fori_loop(0, 2, chunk, 0)
        if rel == 2:
            go(resb.at[w], resr.at[w], ts.at[5 + w], tr.at[5 + w], "dp", zed)

    start(0, 1, 2, 3, 0)
    own_copies[0].start()
    start(1, 1, 2, 0)
    own_copies[1].start()
    go(seg_hbm, seg_prev, ms.at[0], mr.at[0], "dp", after)

    loads[0].wait()
    for r in range(4):
        tok4[r] = tok[:, r * piece : (r + 1) * piece]
    go(tok4.at[x], tokp.at[x], ts.at[0], tr.at[0], "dp", zed)
    start(1, 3)
    start(2, 3, 0)
    own_copies[2].start()
    start(3, 3, 0)
    own_copies[3].start()

    def turn(src, dst):
        def body(j, _):
            c = pl.ds(pl.multiple_of(j * 128, 128), 128)
            dst[c, :] = src[:, c].astype(jnp.float32).T.astype(bf)
            return 0

        lax.fori_loop(0, width // 128, body, 0)

    turn(tok, tok_t)
    go(tok_t, tok_t2, ms.at[1], mr.at[1], "dp", sib)

    def tokens_start():
        got(tokp.at[x], ts.at[0], tr.at[0])
        go(tokp.at[x], tokp.at[x], ts.at[1], tr.at[1], "shard", right)
        go(tokp.at[x], tokp.at[x], ts.at[2], tr.at[2], "shard", left)

    def tokens_relay():
        h = tok_rows // 2
        got(tokp.at[(x + 3) % 4], ts.at[1], tr.at[1])
        ref = tokp.at[(x + 3) % 4, pl.ds(0, h)]
        go(ref, ref, ts.at[3], tr.at[3], "shard", right)
        got(tokp.at[(x + 1) % 4], ts.at[2], tr.at[2])
        ref = tokp.at[(x + 1) % 4, pl.ds(h, h)]
        go(ref, ref, ts.at[4], tr.at[4], "shard", left)

    def tokens_end():
        h = tok_rows // 2
        got(tokp.at[(x + 2) % 4, pl.ds(0, h)], ts.at[3], tr.at[3])
        got(tokp.at[(x + 2) % 4, pl.ds(h, h)], ts.at[4], tr.at[4])

    def near_z(w):
        wait(w, 3)
        start(w, 4, 5, 6)

    def near(w):
        wait(w, 1)
        start(w, 7, 9)
        wait(w, 2)
        start(w, 8, 10)

    def diagonal(w):
        wait(w, 4)
        start(w, 11)
        wait(w, 5)
        start(w, 12)

    def round_z(w):
        wait(w, 4)
        start(w, 13, 11)
        wait(w, 5)
        start(w, 14, 12)

    def far(w):
        wait(w, 7, 8)
        start(w, 15)

    def last(w):
        wait(w, 13, 14)
        start(w, 16)

    near_z(0)
    near(0)
    start(2, 1, 2)
    loads[1].wait()
    turn(tgt, tgt_t)
    tokens_start()
    near_z(1)
    round_z(0)
    near(1)
    use(0, 0)
    far(0)
    use(0, -1)
    use(0, 1)
    tokens_relay()
    round_z(1)
    near_z(2)
    last(0)
    near(2)
    use(1, 0)
    use(2, 0)
    use(1, -1)
    far(1)
    tokens_end()
    use_for_partner(0, 0)
    use_for_partner(0, -1)
    use_for_partner(0, 1)
    use_for_partner(0, 2)
    last(1)
    use_for_partner(1, 0)
    use_for_partner(1, -1)
    use_for_partner(1, 1)
    use_for_partner(1, 2)
    use_for_partner(2, 0)
    round_z(2)
    start(3, 1, 2, 17, 18)
    use(0, 2)
    use(1, 1)
    use(1, 2)
    far(2)
    use_for_partner(2, -1)
    use_for_partner(2, 1)
    last(2)
    use(2, -1)
    use(2, 1)
    use_for_partner(2, 2)
    use(2, 2)
    wait(3, 3)
    start(3, 6)
    wait(3, 1)
    start(3, 7)
    wait(3, 2)
    start(3, 8)
    start(3, 4, 5)

    loads[2].wait()
    got(seg_prev, ms.at[0], mr.at[0])
    lane = lax.broadcasted_iota(jnp.int32, (8, tok_rows), 1)
    here = jnp.broadcast_to(seg[...], (8, tok_rows))
    previous = jnp.where(
        lane == 0,
        pltpu.roll(jnp.broadcast_to(seg_prev[...], (8, tok_rows)), 1, 1),
        pltpu.roll(here, 1, 1),
    )
    first = (lane + d) == 0
    keep[...] = jnp.where(first, 0.0, jnp.where(here == previous, 1.0, 0.0))

    def pointwise(c, parts_of):
        def body(i, _):
            r = pl.ds(pl.multiple_of(i * 16, 16), 16)
            r2 = pl.ds(pl.multiple_of(tok_rows + i * 16, 16), 16)
            pre_gate, up_act, tangent_raw = parts_of(r)
            value, slope, curve = gelu_parts(pre_gate)
            tangent = tangent_raw * inv_root
            stacked[r, c] = (value * up_act).astype(bf)
            stacked[r2, c] = (slope * tangent * up_act).astype(bf)
            fac[0, r, c] = up_act * slope
            fac[1, r, c] = up_act * curve * tangent
            return 0

        lax.fori_loop(0, tok_rows // 16, body, 0)

    pointwise(
        pl.ds(pl.multiple_of(zl * rem, 128), wide), lambda r: [acc[w, r] for w in range(3)]
    )
    wait(3, 17)
    start(3, 9)
    wait(3, 18)
    start(3, 10)
    for w in range(3):
        got(resr.at[w], ts.at[5 + w], tr.at[5 + w])
    pointwise(
        pl.ds(pl.multiple_of((1 - zl) * wide, 128), rem),
        lambda r: [resr[w, r].astype(jnp.float32) for w in range(3)],
    )

    ready = set()

    def out_piece(q):
        row0, size = PIECES[q][0] * 48, PIECES[q][1] * 48
        group = row0 // piece
        if group not in ready:
            ready.add(group)
            if group == 0:
                own_copies[3].wait()
            wait(3, *{0: (0, 6), 1: (9, 10), 2: (11, 12), 3: (15, 16)}[group])
        if size < piece:
            r = pl.ds(row0, size)
            p[r] = dot_nt(full[r], stacked[...]).astype(bf)
            return

        def chunk(n, _):
            r = pl.ds(pl.multiple_of(row0 + n * 2 * depth, 16), 2 * depth)
            p[r] = dot_nt(full[r], stacked[...]).astype(bf)
            return 0

        lax.fori_loop(0, 2, chunk, 0)

    def x_src(row0):
        def src(chunk, lo, size):
            return p.at[pl.ds(row0 + lo, size), pl.ds(pl.multiple_of(((x + chunk) % 4) * 128, 128), 128)]

        return src

    def z_src(row0, size):
        def src(chunk):
            return xc.at[pl.ds(pl.multiple_of(row0 + ((zh + chunk) % 4) * size, 16), size)]

        return src

    def block_owner(group, j):
        hi, lo = j // 2, j % 2
        if group == 0:
            return at(0, hi, lo)
        if group == 3:
            return at(2, hi, lo)
        return at(2 * hi - 1, group - 1, lo)

    def g_block(lo, size, chunk):
        return gt.at[pl.ds(pl.multiple_of(lo, 16), size), pl.ds(pl.multiple_of(((x + chunk) % 4) * 128, 128), 128)]

    def z_peer(k):
        return (zh + k) % 4

    def step(i, q):
        row0, size = PIECES[q][0] * 48, PIECES[q][1] * 48
        group, mid, sub = row0 // piece, size // 2, size // 4
        src, zsrc = x_src(row0), z_src(row0, sub)
        lower, upper = (0, mid), (mid, mid)

        def inbox(dst, part):
            return xin.at[dst, pl.ds(row0 + part[0], part[1])]

        def send(k, frm, dst, target):
            go(frm, dst, sx.at[0], rx.at[q, k], "shard", target, False)

        def came(k, ref):
            got(ref, sx.at[0], rx.at[q, k])

        def zbox(k):
            return zin.at[k - 1, pl.ds(row0 // 4, sub)]

        two = xin.at[pl.ds(1, 2), pl.ds(row0, size)]
        one = xin.at[0, pl.ds(row0, size)]
        three = zin.at[:, pl.ds(row0 // 4, sub)]

        if i == 0:
            send(0, src(2, *upper), inbox(0, upper), right)
            send(0, src(2, *lower), inbox(0, lower), left)
            send(1, src(1, *lower), inbox(1, lower), right)
            send(1, src(3, *upper), inbox(2, upper), left)
        if i == 1:
            came(0, one)
            for part, frm, dst, target in ((upper, 1, 1, right), (lower, 3, 2, left)):
                out = xtx.at[pl.ds(row0 + part[0], part[1])]
                out[...] = plus(src(frm, *part)[...], inbox(0, part)[...]).astype(bf)
                send(1, out, inbox(dst, part), target)
        if i == 2:
            came(1, two)
            both = (0, size)
            xc[row0 : row0 + size] = plus(src(0, *both)[...], inbox(1, both)[...], inbox(2, both)[...]).astype(bf)
            for k in (2, 1, 3):
                send(2, zsrc(k), zbox(k), z_peer(k) * 4 + x)
        if i == 3:
            came(2, three)
            total = plus(zsrc(0)[...], zbox(1)[...], zbox(2)[...], zbox(3)[...])
            lanes = pl.ds(pl.multiple_of((x % 2) * 128, 128), 128)
            row = row0 - group * piece + zh * sub
            block = row // depth
            r = pl.ds(pl.multiple_of(block_owner(group, block) * depth + row - block * depth, 16), sub)
            is_out = (1 - x // 2).astype(jnp.float32)
            wanted = tgt_t[r, lanes].astype(jnp.float32) * is_out
            mine = g_block(row0 + zh * sub, sub, 0)
            mine[...] = (keep[0:1, lanes] * (total - wanted)).astype(bf)
            for k in (2, 1, 3):
                send(3, mine, mine, z_peer(k) * 4 + x)
        if i == 4:
            came(3, three)
            ref = g_block(row0, size, 0)
            send(4, ref, ref, right)
            send(4, ref, ref, left)
        if i == 5:
            came(4, two)
            ref = g_block(row0, mid, 3)
            send(5, ref, ref, right)
            ref = g_block(row0 + mid, mid, 1)
            send(5, ref, ref, left)
        if i == 6:
            came(5, one)

    def back_chunk(group, c):
        r = slice(group * piece, (group + 1) * piece)
        term = dot_tn(gt[r], full[r, c])
        if group == 0:
            back[:, c] = term
        else:
            back[:, c] += term

    def back_piece(group):
        def chunk(n, _):
            back_chunk(group, pl.ds(pl.multiple_of(n * third, 128), third))
            return 0

        lax.fori_loop(0, 3, chunk, 0)

    out_piece(5)
    step(0, 5)
    wait(3, 7)
    start(3, 13)
    wait(3, 8)
    start(3, 14, 15)
    out_piece(0)
    step(0, 0)
    out_piece(1)
    out_piece(3)
    step(0, 3)
    step(0, 1)
    out_piece(2)
    step(1, 5)
    step(1, 0)
    step(0, 2)
    out_piece(4)
    diagonal(3)
    step(1, 3)
    step(1, 1)
    step(2, 5)
    step(0, 4)
    step(2, 0)
    out_piece(8)
    step(0, 8)
    out_piece(6)
    step(0, 6)
    step(2, 3)
    last(3)
    out_piece(7)
    step(1, 2)
    step(0, 7)
    step(2, 1)
    step(1, 4)
    step(3, 5)
    step(3, 0)
    step(1, 8)
    out_piece(9)
    step(0, 9)
    step(3, 3)
    out_piece(11)
    step(1, 6)
    step(2, 2)
    step(0, 11)
    step(3, 1)
    out_piece(10)
    step(2, 4)
    step(1, 7)
    step(0, 10)
    step(4, 5)
    step(2, 6)
    step(2, 8)
    step(1, 9)
    step(4, 0)
    step(2, 7)
    step(3, 2)
    step(1, 10)
    step(1, 11)
    step(5, 5)
    step(3, 4)
    step(4, 1)
    step(3, 6)
    step(2, 10)
    step(3, 8)
    step(2, 11)
    step(4, 3)
    step(5, 0)
    step(3, 7)
    step(6, 5)
    step(4, 2)
    step(4, 4)
    step(2, 9)
    step(5, 1)
    step(4, 6)
    step(5, 3)
    step(6, 0)
    step(3, 10)
    step(4, 8)
    step(5, 2)
    step(3, 11)
    step(4, 7)
    step(6, 1)
    step(5, 4)
    step(3, 9)
    step(5, 6)
    step(4, 10)
    step(6, 3)
    step(5, 8)
    step(6, 2)
    step(4, 11)
    back_piece(0)
    step(4, 9)
    step(5, 7)
    step(6, 4)
    back_piece(1)
    step(6, 8)
    step(6, 6)
    step(5, 10)
    step(5, 11)
    step(5, 9)
    step(6, 7)
    back_piece(2)
    step(6, 11)
    step(6, 10)
    step(6, 9)

    loads[3].wait()
    loads[4].wait()
    got(tok_t2, ms.at[1], mr.at[1])

    def pc(q):
        return pl.ds(*PARTS[q])

    def chip(dy, dz):
        return at(dy, dz, 0) // 2

    def c_block(dy, dz, q, lo=0, size=depth):
        return cp.at[pl.ds(pl.multiple_of(chip(dy, dz) * depth + lo, 16), size), pc(q)]

    def make(q, *which):
        for dy, dz in which:
            r = pl.ds(pl.multiple_of(at(dy, dz, 0) * depth, 16), depth)
            total = dot_nn(tok_t[r], tgg[:, pc(q)]) + dot_nn(tok_t2[r], tgg2[:, pc(q)])
            c_block(dy, dz, q)[...] = (total * inv_root).astype(bf)

    def box(slot, q, lo=0, size=depth):
        return cin.at[slot, pl.ds(lo, size), pc(q)]

    def send_c(src, dst, k, q, target):
        go(src, dst, cs.at[0], cr.at[q, k], "dp", target, False)

    def got_c(ref, k, q):
        got(ref, cs.at[0], cr.at[q, k])

    rest, via_z = depth - cut, 16
    keep_y = depth - via_z

    def reduce_step(i, q):
        if i == 0:
            got(tgg2.at[:, pc(q)], ms.at[2 + q], mr.at[2 + q])
            make(q, (2, 1), (1, 1), (-1, 1))
            send_c(c_block(2, 1, q), box(0, q), 0, q, zed)
            send_c(c_block(1, 1, q, 0, keep_y), box(1, q, 0, keep_y), 1, q, up)
            send_c(c_block(-1, 1, q, 0, keep_y), box(2, q, 0, keep_y), 2, q, down)
            send_c(c_block(1, 1, q, keep_y, via_z), box(1, q, keep_y, via_z), 8, q, zed)
            send_c(c_block(-1, 1, q, keep_y, via_z), box(2, q, keep_y, via_z), 9, q, zed)
            make(q, (2, 0), (0, 1), (1, 0), (-1, 0), (0, 0))
        if i == 1:
            got_c(box(0, q), 0, q)
            cout[0, :, pc(q)] = plus(c_block(2, 0, q)[...], box(0, q)[...]).astype(bf)
            send_c(cout.at[0, pl.ds(0, cut), pc(q)], box(3, q, 0, cut), 3, q, up)
            send_c(cout.at[0, pl.ds(cut, rest), pc(q)], box(3, q, cut, rest), 4, q, down)
            got_c(box(1, q, 0, keep_y), 1, q)
            got_c(box(2, q, 0, keep_y), 2, q)
            cout[1, :keep_y, pc(q)] = plus(
                c_block(0, 1, q, 0, keep_y)[...], box(1, q, 0, keep_y)[...], box(2, q, 0, keep_y)[...]
            ).astype(bf)
            cout[1, keep_y:, pc(q)] = c_block(0, 1, q, keep_y, via_z)[...]
            send_c(cout.at[1, :, pc(q)], box(4, q), 5, q, zed)
        if i == 2:
            got_c(box(3, q, 0, cut), 3, q)
            cout[2, :cut, pc(q)] = plus(c_block(1, 0, q, 0, cut)[...], box(3, q, 0, cut)[...]).astype(bf)
            got_c(box(1, q, keep_y, via_z), 8, q)
            got_c(box(2, q, keep_y, via_z), 9, q)
            cout[2, cut:keep_y, pc(q)] = c_block(1, 0, q, cut, keep_y - cut)[...]
            cout[2, keep_y:, pc(q)] = plus(
                c_block(1, 0, q, keep_y, via_z)[...], box(1, q, keep_y, via_z)[...]
            ).astype(bf)
            send_c(cout.at[2, :, pc(q)], box(5, q), 6, q, up)
            got_c(box(3, q, cut, rest), 4, q)
            cout[3, cut:keep_y, pc(q)] = plus(
                c_block(-1, 0, q, cut, keep_y - cut)[...], box(3, q, cut, keep_y - cut)[...]
            ).astype(bf)
            cout[3, keep_y:, pc(q)] = plus(
                c_block(-1, 0, q, keep_y, via_z)[...],
                box(3, q, keep_y, via_z)[...],
                box(2, q, keep_y, via_z)[...],
            ).astype(bf)
            cout[3, :cut, pc(q)] = c_block(-1, 0, q, 0, cut)[...]
            send_c(cout.at[3, :, pc(q)], box(6, q), 7, q, down)
        if i == 3:
            got_c(box(4, q), 5, q)
            got_c(box(5, q), 6, q)
            got_c(box(6, q), 7, q)
            total = plus(c_block(0, 0, q)[...], box(4, q)[...], box(5, q)[...], box(6, q)[...])
            own = vec[:, pc(q)]
            o_ref[:, pc(q)] = (
                grad[:, pc(q)].astype(jnp.float32)
                + (1.0 - damping) * own.astype(jnp.float32)
                - step_size * total
            ).astype(bf)

    for q in range(len(PARTS)):

        def combine(i, _):
            r = pl.ds(pl.multiple_of(i * 32, 16), 32)
            r2 = pl.ds(pl.multiple_of(tok_rows + i * 32, 16), 32)
            tgg[r, pc(q)] = (fac[0, r, pc(q)] * back[r2, pc(q)] + fac[1, r, pc(q)] * back[r, pc(q)]).astype(bf)
            return 0

        back_chunk(3, pc(q))
        lax.fori_loop(0, tok_rows // 32, combine, 0)
        go(tgg.at[:, pc(q)], tgg2.at[:, pc(q)], ms.at[2 + q], mr.at[2 + q], "dp", sib)
    for q in range(len(PARTS)):
        reduce_step(0, q)
    for q in range(len(PARTS)):
        reduce_step(1, q)
    for q in range(len(PARTS)):
        reduce_step(2, q)
    for q in range(len(PARTS)):
        reduce_step(3, q)
    for w in range(4):
        ref = full if w == 3 else half.at[w]
        ref = ref.at[pl.ds(0, 15 * depth)]
        pltpu.make_async_copy(ref, ref, gs.at[w]).wait()
    ref = full.at[pl.ds(0, width * 15 * 128 // (2 * cols))]
    pltpu.make_async_copy(ref, ref, sx.at[0]).wait()
    ref = full.at[pl.ds(0, 7 * depth)]
    pltpu.make_async_copy(ref, ref, cs.at[0]).wait()
    for copy in sent:
        copy.wait_send()


def per_device(tokens, target, segments, gate_weight, up_weight, down_weight, vector, gradient):
    tok_rows, width = tokens.shape
    depth, cols = gate_weight.shape
    bf, f32 = jnp.bfloat16, jnp.float32
    piece = 4 * depth
    cut = (depth // 32 + 1) * 16
    wide = -(-cols // 256) * 128
    vm, dma = pltpu.VMEM, pltpu.SemaphoreType.DMA
    anywhere = pl.BlockSpec(memory_space=pltpu.HBM)
    scratch = [
        vm((3, width, wide), bf),
        vm((width, cols), bf),
        vm((tok_rows, width), bf),
        vm((tok_rows, width), bf),
        vm((4, tok_rows, piece), bf),
        vm((4, tok_rows, piece), bf),
        vm((width, tok_rows), bf),
        vm((width, tok_rows), bf),
        vm((width, tok_rows), bf),
        vm((1, tok_rows), jnp.int32),
        vm((1, tok_rows), jnp.int32),
        vm((8, tok_rows), f32),
        vm((3, tok_rows, wide), f32),
        vm((3, tok_rows, cols - wide), f32),
        vm((3, tok_rows, cols - wide), bf),
        vm((3, tok_rows, cols - wide), bf),
        vm((2, tok_rows, cols), f32),
        vm((2 * tok_rows, cols), bf),
        vm((width, 2 * tok_rows), bf),
        vm((2 * tok_rows, cols), f32),
        vm((width, 2 * tok_rows), bf),
        vm((3, width, 128), bf),
        vm((width, 128), bf),
        vm((width, 128), bf),
        vm((3, width // 4, 128), bf),
        vm((tok_rows, cols), bf),
        vm((tok_rows, cols), bf),
        vm((8 * depth, cols), bf),
        vm((7, depth, cols), bf),
        vm((4, depth, cols), bf),
        vm((depth, cols), bf),
        vm((depth, cols), bf),
        dma((4,)),
        dma((4, GATHER_COPIES)),
        dma((1,)),
        dma((len(PIECES), 6)),
        dma((1,)),
        dma((len(PARTS), 10)),
        dma((2 + len(PARTS),)),
        dma((2 + len(PARTS),)),
        dma((8,)),
        dma((8,)),
        dma((9,)),
    ]
    return pl.pallas_call(
        functools.partial(step_kernel, (tok_rows, width, depth, cols)),
        out_shape=jax.ShapeDtypeStruct((depth, cols), bf),
        in_specs=[anywhere] * 8,
        out_specs=pl.BlockSpec(memory_space=pltpu.VMEM),
        scratch_shapes=scratch,
        compiler_params=pltpu.CompilerParams(
            collective_id=1, has_side_effects=True, vmem_limit_bytes=107 * 2**19
        ),
    )(tokens, target, segments[None], gate_weight, up_weight, vector, down_weight, gradient)


def solution(mesh):
    return jax.shard_map(
        per_device,
        mesh=mesh,
        in_specs=(
            P("dp", None),
            P("dp", None),
            P("dp"),
            P("dp", "shard"),
            P("dp", "shard"),
            P("dp", "shard"),
            P("dp", "shard"),
            P("dp", "shard"),
        ),
        out_specs=P("dp", "shard"),
        check_vma=False,
    )
```

```python
import functools

import jax
import jax.numpy as jnp
from jax import lax
from jax.experimental import pallas as pl
from jax.experimental.pallas import tpu as pltpu
from jax.sharding import PartitionSpec as P

MESH = pl.DeviceIdType.MESH
coeff_k = 0.7978845608028654
coeff_c = 0.044715
damping = 0.01
step_size = 0.8


def gelu_parts(pre_act):
    inner_arg = coeff_k * (pre_act + coeff_c * pre_act * pre_act * pre_act)
    tanh_value = jnp.tanh(inner_arg)
    slope_term = coeff_k * (1.0 + 3.0 * coeff_c * pre_act * pre_act)
    curve_term = 6.0 * coeff_k * coeff_c * pre_act
    sech_square = 1.0 - tanh_value * tanh_value
    gelu_value = 0.5 * pre_act * (1.0 + tanh_value)
    gelu_slope = 0.5 * (1.0 + tanh_value) + 0.5 * pre_act * sech_square * slope_term
    gelu_curve = sech_square * (
        slope_term + 0.5 * pre_act * (curve_term - 2.0 * tanh_value * slope_term * slope_term)
    )
    return (gelu_value, gelu_slope, gelu_curve)


def remote(src, dst, send_sem, recv_sem, axis, index):
    return pltpu.make_async_remote_copy(
        src_ref=src,
        dst_ref=dst,
        send_sem=send_sem,
        recv_sem=recv_sem,
        device_id={axis: index},
        device_id_type=MESH,
    )


GATHER_COPIES = 19
PARTS = ((0, 128), (128, 384), (512, 512), (1024, 128))
PIECES = ((0, 4), (4, 4), (8, 4), (12, 4), (16, 4), (20, 4), (24, 4), (28, 4), (32, 4), (36, 4), (40, 4), (44, 4))


def plus(a, *more):
    total = a.astype(jnp.float32)
    for b in more:
        total = total + b.astype(jnp.float32)
    return total


def dot_nn(a, b):
    return jnp.dot(a, b, preferred_element_type=jnp.float32)


def dot_nt(a, b):
    return lax.dot_general(a, b, (((1,), (1,)), ((), ())), preferred_element_type=jnp.float32)


def dot_tn(a, b):
    return lax.dot_general(a, b, (((0,), (0,)), ((), ())), preferred_element_type=jnp.float32)


def step_kernel(
    dims, tok_hbm, tgt_hbm, seg_hbm, gate_hbm, up_hbm, vec_hbm, down_hbm, grad_hbm, o_ref,
    half, full, tok, tgt, tok4, tokp, tok_t, tok_t2, tgt_t, seg, seg_prev, keep, acc, accp, resb, resr, fac, stacked, p, back, gt,
    xin, xtx, xc, zin, tgg, tgg2, cp, cin, cout, grad, vec,
    gs, gr, sx, rx, cs, cr, ms, mr, ts, tr, ls,
):
    tok_rows, width, depth, cols = dims
    bf = jnp.bfloat16
    d, sh = lax.axis_index("dp"), lax.axis_index("shard")
    y, zl, core = d // 4, (d // 2) % 2, d % 2
    x, zh = sh % 4, sh // 4
    piece = 4 * depth
    cut = (depth // 32 + 1) * 16
    wide = -(-cols // 256) * 128
    rem = cols - wide
    third = cols // 3
    inv_root = float(width) ** (-0.5)

    def at(dy, dz, dc):
        return ((y + dy) % 4) * 4 + ((zl + dz) % 2) * 2 + (core + dc) % 2

    sib, up, down, zed = at(0, 0, 1), at(1, 0, 0), at(-1, 0, 0), at(0, 1, 0)
    right, left = zh * 4 + (x + 1) % 4, zh * 4 + (x + 3) % 4
    above, below = ((zh + 1) % 4) * 4 + x, ((zh + 3) % 4) * 4 + x
    across = ((zh + 2) % 4) * 4 + x
    after, before = (d + 1) % 16, (d + 15) % 16
    barrier = pltpu.get_barrier_semaphore()
    for axis, targets in (("dp", (sib, up, down, zed, after, before)), ("shard", (right, left, above, below, across))):
        for t in targets:
            pl.semaphore_signal(barrier, inc=1, device_id={axis: t}, device_id_type=MESH)

    loads = [
        pltpu.make_async_copy(src, dst, ls.at[i])
        for i, (src, dst) in enumerate(((tok_hbm, tok), (tgt_hbm, tgt), (seg_hbm, seg), (grad_hbm, grad), (vec_hbm, vec)))
    ]
    for copy in loads:
        copy.start()
    pl.semaphore_wait(barrier, 11)

    sent = []

    def go(src, dst, s, r, axis, target, kept=True):
        copy = remote(src, dst, s, r, axis, target)
        copy.start()
        if kept:
            sent.append(copy)

    def got(ref, s, r):
        remote(ref, ref, s, r, "dp", sib).wait_recv()

    def place(dy, dz, dc):
        return {0: 2 * dz, -1: 4 + 4 * dz, 1: 6 + 4 * dz, 2: 12 + 2 * dz}[dy] + dc

    extent = {"w": (0, depth), "a": (0, cut), "b": (cut, depth - cut)}

    def rows(w, rel, which):
        lo, size = extent[which]
        base = place(*rel) if w == 3 else at(*rel)
        r = pl.ds(pl.multiple_of(base * depth + lo, 16), size)
        return full.at[r] if w == 3 else half.at[w, r]

    def own_part(w, which, z_of):
        lo, size = extent[which]
        if w == 3:
            return ins[w].at[pl.ds(lo, size)]
        return ins[w].at[pl.ds(lo, size), pl.ds(pl.multiple_of(z_of * rem, 128), wide)]

    me = at(0, 0, 0)
    table = [
        ((0, 0, 0), "w", sib, (0, 0, 1)),
        ((0, 0, 0), "w", up, (-1, 0, 0)),
        ((0, 0, 0), "w", down, (1, 0, 0)),
        ((0, 0, 0), "w", zed, (0, 1, 0)),
        ((0, 1, 0), "w", up, (-1, 1, 0)),
        ((0, 1, 0), "w", down, (1, 1, 0)),
        ((0, 1, 0), "w", sib, (0, 1, 1)),
        ((-1, 0, 0), "a", up, (2, 0, 0)),
        ((1, 0, 0), "b", down, (2, 0, 0)),
        ((-1, 0, 0), "w", sib, (-1, 0, 1)),
        ((1, 0, 0), "w", sib, (1, 0, 1)),
        ((-1, 1, 0), "w", sib, (-1, 1, 1)),
        ((1, 1, 0), "w", sib, (1, 1, 1)),
        ((2, 0, 0), "a", zed, (2, 1, 0)),
        ((2, 0, 0), "b", zed, (2, 1, 0)),
        ((2, 0, 0), "w", sib, (2, 0, 1)),
        ((2, 1, 0), "w", sib, (2, 1, 1)),
    ]
    special_down = {
        1: ((0, 0, 0), "a", up, (-1, 0, 0)),
        2: ((0, 0, 0), "b", down, (1, 0, 0)),
        17: ((0, 0, 0), "b", up, (-1, 0, 0)),
        18: ((0, 0, 0), "a", down, (1, 0, 0)),
    }
    ins = (gate_hbm, up_hbm, vec_hbm, down_hbm)

    special_half = {
        13: ((-1, 1, 0), "a", up, (2, 1, 0)),
        14: ((1, 1, 0), "b", down, (2, 1, 0)),
    }

    def entry(w, k):
        special = special_down if w == 3 else special_half
        return special[k] if k in special else table[k]

    def start(w, *numbers):
        for k in numbers:
            mine, which, target, theirs = entry(w, k)
            src = rows(w, mine, which)
            if mine == (0, 0, 0):
                src = own_part(w, which, (zl + (k == 3)) % 2)
            dst = rows(w, theirs if w == 3 else mine, which)
            go(src, dst, gs.at[w], gr.at[w, k], "dp", target, False)

    def wait(w, *numbers):
        for k in numbers:
            _, which, _, came = entry(w, k)
            got(rows(w, came, which), gs.at[w], gr.at[w, k])

    own_copies = [pltpu.make_async_copy(own_part(w, "w", zl), rows(w, (0, 0, 0), "w"), ls.at[5 + w]) for w in range(4)]

    late = {0: (0, 6), -1: (9, 11), 1: (10, 12), 2: (15, 16)}

    def piece_of(rel):
        return (y + rel) % 4

    def piece_rows(rel):
        return pl.ds(pl.multiple_of(piece_of(rel) * piece, 16), piece)

    came_in = set()

    def settle(w, rel):
        if (w, rel) in came_in:
            return
        came_in.add((w, rel))
        wait(w, *late[rel])
        if rel == 0:
            own_copies[w].wait()

    def use(w, rel):
        settle(w, rel)
        for c in (slice(0, 384), slice(384, wide)):
            term = dot_nn(tok4[piece_of(rel)], half[w, piece_rows(rel), c])
            if rel == 0:
                acc[w, :, c] = term
            else:
                acc[w, :, c] += term

    def use_for_partner(w, rel):
        settle(w, rel)

        def chunk(n, _):
            c = pl.ds(pl.multiple_of(n * (rem // 2), 128), rem // 2)
            c2 = pl.ds(pl.multiple_of(zl * (wide - rem) + n * (rem // 2), 128), rem // 2)
            term = dot_nn(tokp[piece_of(rel)], half[w, piece_rows(rel), c2])
            if rel == 0:
                accp[w, :, c] = term
            else:
                accp[w, :, c] += term
            if rel == 2:
                resb[w, :, c] = accp[w, :, c].astype(bf)
            return 0

        lax.fori_loop(0, 2, chunk, 0)
        if rel == 2:
            go(resb.at[w], resr.at[w], ts.at[5 + w], tr.at[5 + w], "dp", zed)

    start(0, 1, 2, 3, 0)
    own_copies[0].start()
    start(1, 1, 2, 0)
    own_copies[1].start()
    go(seg_hbm, seg_prev, ms.at[0], mr.at[0], "dp", after)

    loads[0].wait()
    for r in range(4):
        tok4[r] = tok[:, r * piece : (r + 1) * piece]
    go(tok4.at[x], tokp.at[x], ts.at[0], tr.at[0], "dp", zed)
    start(1, 3)
    start(2, 3, 0)
    own_copies[2].start()
    start(3, 3, 0)
    own_copies[3].start()

    def turn(src, dst):
        def body(j, _):
            c = pl.ds(pl.multiple_of(j * 128, 128), 128)
            dst[c, :] = src[:, c].astype(jnp.float32).T.astype(bf)
            return 0

        lax.fori_loop(0, width // 128, body, 0)

    turn(tok, tok_t)
    go(tok_t, tok_t2, ms.at[1], mr.at[1], "dp", sib)

    def tokens_start():
        got(tokp.at[x], ts.at[0], tr.at[0])
        go(tokp.at[x], tokp.at[x], ts.at[1], tr.at[1], "shard", right)
        go(tokp.at[x], tokp.at[x], ts.at[2], tr.at[2], "shard", left)

    def tokens_relay():
        h = tok_rows // 2
        got(tokp.at[(x + 3) % 4], ts.at[1], tr.at[1])
        ref = tokp.at[(x + 3) % 4, pl.ds(0, h)]
        go(ref, ref, ts.at[3], tr.at[3], "shard", right)
        got(tokp.at[(x + 1) % 4], ts.at[2], tr.at[2])
        ref = tokp.at[(x + 1) % 4, pl.ds(h, h)]
        go(ref, ref, ts.at[4], tr.at[4], "shard", left)

    def tokens_end():
        h = tok_rows // 2
        got(tokp.at[(x + 2) % 4, pl.ds(0, h)], ts.at[3], tr.at[3])
        got(tokp.at[(x + 2) % 4, pl.ds(h, h)], ts.at[4], tr.at[4])

    def near_z(w):
        wait(w, 3)
        start(w, 4, 5, 6)

    def near(w):
        wait(w, 1)
        start(w, 7, 9)
        wait(w, 2)
        start(w, 8, 10)

    def diagonal(w):
        wait(w, 4)
        start(w, 11)
        wait(w, 5)
        start(w, 12)

    def round_z(w):
        wait(w, 4)
        start(w, 13, 11)
        wait(w, 5)
        start(w, 14, 12)

    def far(w):
        wait(w, 7, 8)
        start(w, 15)

    def last(w):
        wait(w, 13, 14)
        start(w, 16)

    near_z(0)
    near(0)
    start(2, 1, 2)
    loads[1].wait()
    turn(tgt, tgt_t)
    tokens_start()
    near_z(1)
    round_z(0)
    near(1)
    use(0, 0)
    far(0)
    use(0, -1)
    use(0, 1)
    tokens_relay()
    round_z(1)
    near_z(2)
    last(0)
    near(2)
    use(1, 0)
    use(2, 0)
    use(1, -1)
    far(1)
    tokens_end()
    use_for_partner(0, 0)
    use_for_partner(0, -1)
    use_for_partner(0, 1)
    use_for_partner(0, 2)
    last(1)
    use_for_partner(1, 0)
    use_for_partner(1, -1)
    use_for_partner(1, 1)
    use_for_partner(1, 2)
    use_for_partner(2, 0)
    round_z(2)
    start(3, 1, 2, 17, 18)
    use(0, 2)
    use(1, 1)
    use(1, 2)
    far(2)
    use_for_partner(2, -1)
    use_for_partner(2, 1)
    last(2)
    use(2, -1)
    use(2, 1)
    use_for_partner(2, 2)
    use(2, 2)
    wait(3, 3)
    start(3, 6)
    wait(3, 1)
    start(3, 7)
    wait(3, 2)
    start(3, 8)
    start(3, 4, 5)

    loads[2].wait()
    got(seg_prev, ms.at[0], mr.at[0])
    lane = lax.broadcasted_iota(jnp.int32, (8, tok_rows), 1)
    here = jnp.broadcast_to(seg[...], (8, tok_rows))
    previous = jnp.where(
        lane == 0,
        pltpu.roll(jnp.broadcast_to(seg_prev[...], (8, tok_rows)), 1, 1),
        pltpu.roll(here, 1, 1),
    )
    first = (lane + d) == 0
    keep[...] = jnp.where(first, 0.0, jnp.where(here == previous, 1.0, 0.0))

    def pointwise(c, parts_of):
        def body(i, _):
            r = pl.ds(pl.multiple_of(i * 16, 16), 16)
            r2 = pl.ds(pl.multiple_of(tok_rows + i * 16, 16), 16)
            pre_gate, up_act, tangent_raw = parts_of(r)
            value, slope, curve = gelu_parts(pre_gate)
            tangent = tangent_raw * inv_root
            stacked[r, c] = (value * up_act).astype(bf)
            stacked[r2, c] = (slope * tangent * up_act).astype(bf)
            fac[0, r, c] = up_act * slope
            fac[1, r, c] = up_act * curve * tangent
            return 0

        lax.fori_loop(0, tok_rows // 16, body, 0)

    pointwise(
        pl.ds(pl.multiple_of(zl * rem, 128), wide), lambda r: [acc[w, r] for w in range(3)]
    )
    wait(3, 17)
    start(3, 9)
    wait(3, 18)
    start(3, 10)
    for w in range(3):
        got(resr.at[w], ts.at[5 + w], tr.at[5 + w])
    pointwise(
        pl.ds(pl.multiple_of((1 - zl) * wide, 128), rem),
        lambda r: [resr[w, r].astype(jnp.float32) for w in range(3)],
    )

    ready = set()

    def out_piece(q):
        row0, size = PIECES[q][0] * 48, PIECES[q][1] * 48
        group = row0 // piece
        if group not in ready:
            ready.add(group)
            if group == 0:
                own_copies[3].wait()
            wait(3, *{0: (0, 6), 1: (9, 10), 2: (11, 12), 3: (15, 16)}[group])
        if size < piece:
            r = pl.ds(row0, size)
            p[r] = dot_nt(full[r], stacked[...]).astype(bf)
            return

        def chunk(n, _):
            r = pl.ds(pl.multiple_of(row0 + n * 2 * depth, 16), 2 * depth)
            p[r] = dot_nt(full[r], stacked[...]).astype(bf)
            return 0

        lax.fori_loop(0, 2, chunk, 0)

    def x_src(row0):
        def src(chunk, lo, size):
            return p.at[pl.ds(row0 + lo, size), pl.ds(pl.multiple_of(((x + chunk) % 4) * 128, 128), 128)]

        return src

    def z_src(row0, size):
        def src(chunk):
            return xc.at[pl.ds(pl.multiple_of(row0 + ((zh + chunk) % 4) * size, 16), size)]

        return src

    def block_owner(group, j):
        hi, lo = j // 2, j % 2
        if group == 0:
            return at(0, hi, lo)
        if group == 3:
            return at(2, hi, lo)
        return at(2 * hi - 1, group - 1, lo)

    def g_block(lo, size, chunk):
        return gt.at[pl.ds(pl.multiple_of(lo, 16), size), pl.ds(pl.multiple_of(((x + chunk) % 4) * 128, 128), 128)]

    def z_peer(k):
        return (zh + k) % 4

    def step(i, q):
        row0, size = PIECES[q][0] * 48, PIECES[q][1] * 48
        group, mid, sub = row0 // piece, size // 2, size // 4
        src, zsrc = x_src(row0), z_src(row0, sub)
        lower, upper = (0, mid), (mid, mid)

        def inbox(dst, part):
            return xin.at[dst, pl.ds(row0 + part[0], part[1])]

        def send(k, frm, dst, target):
            go(frm, dst, sx.at[0], rx.at[q, k], "shard", target, False)

        def came(k, ref):
            got(ref, sx.at[0], rx.at[q, k])

        def zbox(k):
            return zin.at[k - 1, pl.ds(row0 // 4, sub)]

        two = xin.at[pl.ds(1, 2), pl.ds(row0, size)]
        one = xin.at[0, pl.ds(row0, size)]
        three = zin.at[:, pl.ds(row0 // 4, sub)]

        if i == 0:
            send(0, src(2, *upper), inbox(0, upper), right)
            send(0, src(2, *lower), inbox(0, lower), left)
            send(1, src(1, *lower), inbox(1, lower), right)
            send(1, src(3, *upper), inbox(2, upper), left)
        if i == 1:
            came(0, one)
            for part, frm, dst, target in ((upper, 1, 1, right), (lower, 3, 2, left)):
                out = xtx.at[pl.ds(row0 + part[0], part[1])]
                out[...] = plus(src(frm, *part)[...], inbox(0, part)[...]).astype(bf)
                send(1, out, inbox(dst, part), target)
        if i == 2:
            came(1, two)
            both = (0, size)
            xc[row0 : row0 + size] = plus(src(0, *both)[...], inbox(1, both)[...], inbox(2, both)[...]).astype(bf)
            for k in (2, 1, 3):
                send(2, zsrc(k), zbox(k), z_peer(k) * 4 + x)
        if i == 3:
            came(2, three)
            total = plus(zsrc(0)[...], zbox(1)[...], zbox(2)[...], zbox(3)[...])
            lanes = pl.ds(pl.multiple_of((x % 2) * 128, 128), 128)
            row = row0 - group * piece + zh * sub
            block = row // depth
            r = pl.ds(pl.multiple_of(block_owner(group, block) * depth + row - block * depth, 16), sub)
            is_out = (1 - x // 2).astype(jnp.float32)
            wanted = tgt_t[r, lanes].astype(jnp.float32) * is_out
            mine = g_block(row0 + zh * sub, sub, 0)
            mine[...] = (keep[0:1, lanes] * (total - wanted)).astype(bf)
            for k in (2, 1, 3):
                send(3, mine, mine, z_peer(k) * 4 + x)
        if i == 4:
            came(3, three)
            ref = g_block(row0, size, 0)
            send(4, ref, ref, right)
            send(4, ref, ref, left)
        if i == 5:
            came(4, two)
            ref = g_block(row0, mid, 3)
            send(5, ref, ref, right)
            ref = g_block(row0 + mid, mid, 1)
            send(5, ref, ref, left)
        if i == 6:
            came(5, one)

    def back_chunk(group, c):
        r = slice(group * piece, (group + 1) * piece)
        term = dot_tn(gt[r], full[r, c])
        if group == 0:
            back[:, c] = term
        else:
            back[:, c] += term

    def back_piece(group):
        def chunk(n, _):
            back_chunk(group, pl.ds(pl.multiple_of(n * third, 128), third))
            return 0

        lax.fori_loop(0, 3, chunk, 0)

    out_piece(5)
    step(0, 5)
    wait(3, 7)
    start(3, 13)
    wait(3, 8)
    start(3, 14, 15)
    out_piece(0)
    step(0, 0)
    out_piece(1)
    out_piece(3)
    step(0, 3)
    step(0, 1)
    out_piece(2)
    step(1, 5)
    step(1, 0)
    step(0, 2)
    out_piece(4)
    diagonal(3)
    step(1, 3)
    step(1, 1)
    step(2, 5)
    step(0, 4)
    step(2, 0)
    out_piece(8)
    step(0, 8)
    out_piece(6)
    step(0, 6)
    step(2, 3)
    last(3)
    out_piece(7)
    step(1, 2)
    step(0, 7)
    step(2, 1)
    step(1, 4)
    step(3, 5)
    step(3, 0)
    step(1, 8)
    out_piece(9)
    step(0, 9)
    step(3, 3)
    out_piece(11)
    step(1, 6)
    step(2, 2)
    step(0, 11)
    step(3, 1)
    out_piece(10)
    step(2, 4)
    step(1, 7)
    step(0, 10)
    step(4, 5)
    step(2, 6)
    step(2, 8)
    step(1, 9)
    step(4, 0)
    step(2, 7)
    step(3, 2)
    step(1, 10)
    step(1, 11)
    step(5, 5)
    step(3, 4)
    step(4, 1)
    step(3, 6)
    step(2, 10)
    step(3, 8)
    step(2, 11)
    step(4, 3)
    step(5, 0)
    step(3, 7)
    step(6, 5)
    step(4, 2)
    step(4, 4)
    step(2, 9)
    step(5, 1)
    step(4, 6)
    step(5, 3)
    step(6, 0)
    step(3, 10)
    step(4, 8)
    step(5, 2)
    step(3, 11)
    step(4, 7)
    step(6, 1)
    step(5, 4)
    step(3, 9)
    step(5, 6)
    step(4, 10)
    step(6, 3)
    step(5, 8)
    step(6, 2)
    step(4, 11)
    back_piece(0)
    step(4, 9)
    step(5, 7)
    step(6, 4)
    back_piece(1)
    step(6, 8)
    step(6, 6)
    step(5, 10)
    step(5, 11)
    step(5, 9)
    step(6, 7)
    back_piece(2)
    step(6, 11)
    step(6, 10)
    step(6, 9)

    loads[3].wait()
    loads[4].wait()
    got(tok_t2, ms.at[1], mr.at[1])

    def pc(q):
        return pl.ds(*PARTS[q])

    def chip(dy, dz):
        return at(dy, dz, 0) // 2

    def c_block(dy, dz, q, lo=0, size=depth):
        return cp.at[pl.ds(pl.multiple_of(chip(dy, dz) * depth + lo, 16), size), pc(q)]

    def make(q, *which):
        for dy, dz in which:
            r = pl.ds(pl.multiple_of(at(dy, dz, 0) * depth, 16), depth)
            total = dot_nn(tok_t[r], tgg[:, pc(q)]) + dot_nn(tok_t2[r], tgg2[:, pc(q)])
            c_block(dy, dz, q)[...] = (total * inv_root).astype(bf)

    def box(slot, q, lo=0, size=depth):
        return cin.at[slot, pl.ds(lo, size), pc(q)]

    def send_c(src, dst, k, q, target):
        go(src, dst, cs.at[0], cr.at[q, k], "dp", target, False)

    def got_c(ref, k, q):
        got(ref, cs.at[0], cr.at[q, k])

    rest, via_z = depth - cut, 16
    keep_y = depth - via_z

    def reduce_step(i, q):
        if i == 0:
            got(tgg2.at[:, pc(q)], ms.at[2 + q], mr.at[2 + q])
            make(q, (2, 1), (1, 1), (-1, 1))
            send_c(c_block(2, 1, q), box(0, q), 0, q, zed)
            send_c(c_block(1, 1, q, 0, keep_y), box(1, q, 0, keep_y), 1, q, up)
            send_c(c_block(-1, 1, q, 0, keep_y), box(2, q, 0, keep_y), 2, q, down)
            send_c(c_block(1, 1, q, keep_y, via_z), box(1, q, keep_y, via_z), 8, q, zed)
            send_c(c_block(-1, 1, q, keep_y, via_z), box(2, q, keep_y, via_z), 9, q, zed)
            make(q, (2, 0), (0, 1), (1, 0), (-1, 0), (0, 0))
        if i == 1:
            got_c(box(0, q), 0, q)
            cout[0, :, pc(q)] = plus(c_block(2, 0, q)[...], box(0, q)[...]).astype(bf)
            send_c(cout.at[0, pl.ds(0, cut), pc(q)], box(3, q, 0, cut), 3, q, up)
            send_c(cout.at[0, pl.ds(cut, rest), pc(q)], box(3, q, cut, rest), 4, q, down)
            got_c(box(1, q, 0, keep_y), 1, q)
            got_c(box(2, q, 0, keep_y), 2, q)
            cout[1, :keep_y, pc(q)] = plus(
                c_block(0, 1, q, 0, keep_y)[...], box(1, q, 0, keep_y)[...], box(2, q, 0, keep_y)[...]
            ).astype(bf)
            cout[1, keep_y:, pc(q)] = c_block(0, 1, q, keep_y, via_z)[...]
            send_c(cout.at[1, :, pc(q)], box(4, q), 5, q, zed)
        if i == 2:
            got_c(box(3, q, 0, cut), 3, q)
            cout[2, :cut, pc(q)] = plus(c_block(1, 0, q, 0, cut)[...], box(3, q, 0, cut)[...]).astype(bf)
            got_c(box(1, q, keep_y, via_z), 8, q)
            got_c(box(2, q, keep_y, via_z), 9, q)
            cout[2, cut:keep_y, pc(q)] = c_block(1, 0, q, cut, keep_y - cut)[...]
            cout[2, keep_y:, pc(q)] = plus(
                c_block(1, 0, q, keep_y, via_z)[...], box(1, q, keep_y, via_z)[...]
            ).astype(bf)
            send_c(cout.at[2, :, pc(q)], box(5, q), 6, q, up)
            got_c(box(3, q, cut, rest), 4, q)
            cout[3, cut:keep_y, pc(q)] = plus(
                c_block(-1, 0, q, cut, keep_y - cut)[...], box(3, q, cut, keep_y - cut)[...]
            ).astype(bf)
            cout[3, keep_y:, pc(q)] = plus(
                c_block(-1, 0, q, keep_y, via_z)[...],
                box(3, q, keep_y, via_z)[...],
                box(2, q, keep_y, via_z)[...],
            ).astype(bf)
            cout[3, :cut, pc(q)] = c_block(-1, 0, q, 0, cut)[...]
            send_c(cout.at[3, :, pc(q)], box(6, q), 7, q, down)
        if i == 3:
            got_c(box(4, q), 5, q)
            got_c(box(5, q), 6, q)
            got_c(box(6, q), 7, q)
            total = plus(c_block(0, 0, q)[...], box(4, q)[...], box(5, q)[...], box(6, q)[...])
            own = vec[:, pc(q)]
            o_ref[:, pc(q)] = (
                grad[:, pc(q)].astype(jnp.float32)
                + (1.0 - damping) * own.astype(jnp.float32)
                - step_size * total
            ).astype(bf)

    for q in range(len(PARTS)):

        def combine(i, _):
            r = pl.ds(pl.multiple_of(i * 32, 16), 32)
            r2 = pl.ds(pl.multiple_of(tok_rows + i * 32, 16), 32)
            tgg[r, pc(q)] = (fac[0, r, pc(q)] * back[r2, pc(q)] + fac[1, r, pc(q)] * back[r, pc(q)]).astype(bf)
            return 0

        back_chunk(3, pc(q))
        lax.fori_loop(0, tok_rows // 32, combine, 0)
        go(tgg.at[:, pc(q)], tgg2.at[:, pc(q)], ms.at[2 + q], mr.at[2 + q], "dp", sib)
    for q in range(len(PARTS)):
        reduce_step(0, q)
    for q in range(len(PARTS)):
        reduce_step(1, q)
    for q in range(len(PARTS)):
        reduce_step(2, q)
    for q in range(len(PARTS)):
        reduce_step(3, q)
    for w in range(4):
        ref = full if w == 3 else half.at[w]
        ref = ref.at[pl.ds(0, 15 * depth)]
        pltpu.make_async_copy(ref, ref, gs.at[w]).wait()
    ref = full.at[pl.ds(0, width * 15 * 128 // (2 * cols))]
    pltpu.make_async_copy(ref, ref, sx.at[0]).wait()
    ref = full.at[pl.ds(0, 7 * depth)]
    pltpu.make_async_copy(ref, ref, cs.at[0]).wait()
    for copy in sent:
        copy.wait_send()


def per_device(tokens, target, segments, gate_weight, up_weight, down_weight, vector, gradient):
    tok_rows, width = tokens.shape
    depth, cols = gate_weight.shape
    bf, f32 = jnp.bfloat16, jnp.float32
    piece = 4 * depth
    cut = (depth // 32 + 1) * 16
    wide = -(-cols // 256) * 128
    vm, dma = pltpu.VMEM, pltpu.SemaphoreType.DMA
    anywhere = pl.BlockSpec(memory_space=pltpu.HBM)
    scratch = [
        vm((3, width, wide), bf),
        vm((width, cols), bf),
        vm((tok_rows, width), bf),
        vm((tok_rows, width), bf),
        vm((4, tok_rows, piece), bf),
        vm((4, tok_rows, piece), bf),
        vm((width, tok_rows), bf),
        vm((width, tok_rows), bf),
        vm((width, tok_rows), bf),
        vm((1, tok_rows), jnp.int32),
        vm((1, tok_rows), jnp.int32),
        vm((8, tok_rows), f32),
        vm((3, tok_rows, wide), f32),
        vm((3, tok_rows, cols - wide), f32),
        vm((3, tok_rows, cols - wide), bf),
        vm((3, tok_rows, cols - wide), bf),
        vm((2, tok_rows, cols), f32),
        vm((2 * tok_rows, cols), bf),
        vm((width, 2 * tok_rows), bf),
        vm((2 * tok_rows, cols), f32),
        vm((width, 2 * tok_rows), bf),
        vm((3, width, 128), bf),
        vm((width, 128), bf),
        vm((width, 128), bf),
        vm((3, width // 4, 128), bf),
        vm((tok_rows, cols), bf),
        vm((tok_rows, cols), bf),
        vm((8 * depth, cols), bf),
        vm((7, depth, cols), bf),
        vm((4, depth, cols), bf),
        vm((depth, cols), bf),
        vm((depth, cols), bf),
        dma((4,)),
        dma((4, GATHER_COPIES)),
        dma((1,)),
        dma((len(PIECES), 6)),
        dma((1,)),
        dma((len(PARTS), 10)),
        dma((2 + len(PARTS),)),
        dma((2 + len(PARTS),)),
        dma((8,)),
        dma((8,)),
        dma((9,)),
    ]
    return pl.pallas_call(
        functools.partial(step_kernel, (tok_rows, width, depth, cols)),
        out_shape=jax.ShapeDtypeStruct((depth, cols), bf),
        in_specs=[anywhere] * 8,
        out_specs=pl.BlockSpec(memory_space=pltpu.VMEM),
        scratch_shapes=scratch,
        compiler_params=pltpu.CompilerParams(
            collective_id=1, has_side_effects=True, vmem_limit_bytes=107 * 2**19
        ),
    )(tokens, target, segments[None], gate_weight, up_weight, vector, down_weight, gradient)


def solution(mesh):
    return jax.shard_map(
        per_device,
        mesh=mesh,
        in_specs=(
            P("dp", None),
            P("dp", None),
            P("dp"),
            P("dp", "shard"),
            P("dp", "shard"),
            P("dp", "shard"),
            P("dp", "shard"),
            P("dp", "shard"),
        ),
        out_specs=P("dp", "shard"),
        check_vma=False,
    )
```
